32 devices in a mesh: shard: 8 (over y, x, core), replica: 4 (over z).
Axes of the slice: x: 2, y: 2, z: 4, core: 2. Of those that a mesh axis runs over, the one named last changes fastest.
Arguments:
- tokens: bfloat16 [4096, 768], P(('shard', 'replica')), may hold values from -6 to 6
- positions: int32 [4096], P(('shard', 'replica')), may hold values from 0 to 2047, as said below
- qkv_weight: bfloat16 [768, 2304], P('shard'), may hold values from -0.21875 to 0.21875
- attn_weight: bfloat16 [768, 768], P('shard'), may hold values from -0.875 to 0.875
- glu_weight: bfloat16 [768, 2304], P('shard'), may hold values from -0.21875 to 0.21875
- down_weight: bfloat16 [1152, 768], P('shard'), may hold values from -0.1875 to 0.1875
- attn_gain: bfloat16 [768], P('shard'), may hold values from 0.25 to 1.75
- ffn_gain: bfloat16 [768], P('shard'), may hold values from 0.25 to 1.75
- cotangent: bfloat16 [4096, 768], P(('shard', 'replica')), may hold values from -6 to 6
Outputs:
- mixed: bfloat16 [4096, 768], P(('shard', 'replica'))
- grad_tokens: bfloat16 [4096, 768], P(('shard', 'replica'))
- grad_qkv: float32 [768, 2304], P('shard')
- grad_attn: float32 [768, 768], P('shard')
- grad_glu: float32 [768, 2304], P('shard')
- grad_down: float32 [1152, 768], P('shard')
- grad_attn_gain: float32 [768], P('shard')
- grad_ffn_gain: float32 [768], P('shard')
The draws below stay inside these ranges and needn't reach their ends.
Inputs may be any that keep to these rules, and one draw needn't show every extreme that they name: `positions`: sequences lie one after another in the stream, each counting 0, 1, 2, ... from its first token; the stream begins with place 0; every sequence holds 1024 to 2048 tokens, except the last, which the stream's end may cut short.
All inputs are finite; a program needn't handle non-finite values.
Results may differ from the reference program's by a relative error of at most 0.02.
Values may be sent and summed in bfloat16 or wider, within the bound.
No kernel may reach another device: no remote copies, remote signals or barrier semaphores. Data moves between devices by JAX's collectives and lax.ppermute only.
A program may use at most 128 MiB of HBM per device.

```python
import math
import jax
import jax.numpy as jnp
from jax import lax

D = 768
HEADS = 12
HEAD = 64
FF = 1152
WINDOW = 128
SEQ = 2048
TOKENS = 4096


def draw_positions(key, part):
    key = jax.random.fold_in(key, 7)
    slots = TOKENS // (SEQ // 2) + 2
    lengths = jax.random.randint(key, (slots,), SEQ // 2, SEQ + 1, dtype=jnp.int32)
    lengths = lengths.at[1].set(SEQ).astype(jnp.int32)
    starts = (jnp.cumsum(lengths) - lengths).astype(jnp.int32)
    token_index = jnp.arange(TOKENS, dtype=jnp.int32)
    which = (jnp.searchsorted(starts, token_index, side='right') - 1).astype(jnp.int32)
    return (token_index - starts[which]).astype(jnp.int32)


def with_spikes(drawn, rng, source, target, blocks, factor):
    def block_of(axis_at):
        return (jnp.arange(drawn.shape[axis_at]) // (drawn.shape[axis_at] // blocks)).reshape((-1,) + (1,) * (drawn.ndim - 1 - axis_at))

    first = jax.random.permutation(rng, blocks)[block_of(target)]
    far = (block_of(target) + blocks // 2) % blocks
    return jnp.where((block_of(source) == first) | (block_of(source) == far), factor * drawn, drawn)


def block_levels(key, shape, shards, low, top_value):
    gain = 1.0
    for dim, blocks in shards:
        draws = jax.random.uniform(jax.random.fold_in(jax.random.fold_in(key, 6), dim), (blocks,), jnp.float32, low / len(shards), top_value / len(shards))
        gain = gain * jnp.repeat(jnp.exp(draws), shape[dim] // blocks).reshape((-1,) + (1,) * (len(shape) - 1 - dim))
    return gain


def noise(stream_key, extent, scale, bound, cuts=(), kind=jnp.bfloat16):
    array = jax.random.normal(stream_key, extent, jnp.float32) * scale
    if len(cuts) > 0:
        array = block_levels(stream_key, extent, cuts, -0.22, 0.18) * array
    return jnp.clip(array, min=-bound, max=bound).astype(kind)


def bell_draw_with(key, shape, deviation, reach, split, heavy, held_as=jnp.bfloat16):
    values = deviation * jax.random.normal(key, shape, jnp.float32)
    if split:
        values = values * block_levels(key, shape, split, -0.22, 0.18)
    return jnp.clip(with_spikes(values, jax.random.fold_in(key, 3), *heavy), -reach, reach).astype(held_as)


def setup_inputs(seed: int = 0) -> dict:
    key_of = jax.random.split(jax.random.key(seed), 10)
    tokens = bell_draw_with(key_of[0], (TOKENS, D), 1.0, 6.0, ((0, 32),), (0, 1, 32, 2.75))
    positions = draw_positions(jax.random.fold_in(key_of[9], 71), 0)
    qkv_weight = noise(key_of[2], (D, 3 * D), D ** -0.5, 0.21875, ((0, 8),))
    attn_weight = noise(key_of[3], (D, D), (D // 16) ** -0.5, 0.875, ((0, 8),))
    glu_weight = noise(key_of[4], (D, 2 * FF), D ** -0.5, 0.21875, ((0, 8),))
    down_weight = noise(key_of[5], (FF, D), FF ** -0.5, 0.1875, ((0, 8),))
    attn_gain = jnp.clip(1.0 + 0.15 * jax.random.normal(key_of[6], (D,), jnp.float32), 0.25, 1.75).astype(jnp.bfloat16)
    ffn_gain = jnp.clip(1.0 + 0.15 * jax.random.normal(key_of[7], (D,), jnp.float32), 0.25, 1.75).astype(jnp.bfloat16)
    cotangent = noise(key_of[8], (TOKENS, D), 1.0, 6.0, ((0, 32),))
    return dict(tokens=tokens, positions=positions, qkv_weight=qkv_weight, attn_weight=attn_weight, glu_weight=glu_weight, down_weight=down_weight, attn_gain=attn_gain, ffn_gain=ffn_gain, cotangent=cotangent)


HIGHEST = lax.Precision.HIGHEST
EPSILON = 1e-05
THETA_BASE = 10000.0
NEGATIVE = -1e+30

@jax.custom_vjp
def low(v):
    return lax.optimization_barrier(v.astype(jnp.bfloat16)).astype(jnp.float32)

@jax.custom_vjp
def low_back(v):
    return v

def low_keep(v):
    return (low(v), None)

def low_pass(kept, grad):
    return (grad,)

def back_keep(v):
    return (v, None)

def back_low(kept, grad):
    return (low(grad),)
low.defvjp(low_keep, low_pass)
low_back.defvjp(back_keep, back_low)

def layer_norm(vector, scaling):
    average = lax.optimization_barrier(jnp.mean(vector, axis=-1, keepdims=True))
    centred = vector - average
    spread = lax.optimization_barrier(jnp.mean(centred * centred, axis=-1, keepdims=True))
    return centred * lax.rsqrt(spread + EPSILON) * scaling

def rotate(vector, cosine, sine):
    middle = vector.shape[-1] // 2
    turned = jnp.concatenate([-vector[..., middle:], vector[..., :middle]], axis=-1)
    return vector * cosine + turned * sine

def angles(positions, head_size):
    middle = head_size // 2
    inverse = THETA_BASE ** (-(jnp.arange(middle, dtype=jnp.float32) * 2.0 / head_size))
    phases = positions.astype(jnp.float32)[:, None] * inverse[None, :]
    phases = jnp.concatenate([phases, phases], axis=-1)[:, None, :]
    return (jnp.cos(phases), jnp.sin(phases))

def window_mask(near_query, near_key, radius):
    query_at = jnp.arange(near_query.shape[0], dtype=jnp.int32)[:, None]
    key_at = jnp.arange(near_key.shape[0], dtype=jnp.int32)[None, :]
    offset = key_at - radius - query_at
    distance = offset.astype(jnp.float32)
    later_key = near_key[None, :].astype(jnp.float32) >= distance
    later_query = near_query[:, None].astype(jnp.float32) >= -distance
    return (jnp.abs(offset) <= radius) & jnp.where(offset >= 0, later_key, later_query)

def geglu(gate_half, up_half):
    return jax.nn.gelu(gate_half, approximate=False) * up_half

def attention(queries, key_rows, value_rows, positions):
    token_count = queries.shape[0]
    radius = WINDOW // 2
    block_rows = math.gcd(token_count, 512)
    scale = 1.0 / math.sqrt(HEAD)
    padding = ((radius, radius), (0, 0), (0, 0))
    keys_ext = jnp.pad(key_rows, padding)
    values_ext = jnp.pad(value_rows, padding)
    near = jnp.minimum(positions, radius).astype(jnp.int32)
    near_ext = jnp.pad(near, (radius, radius))

    def one_block(first_row):
        queries_blk = lax.dynamic_slice_in_dim(queries, first_row, block_rows, 0)
        keys_blk = lax.dynamic_slice_in_dim(keys_ext, first_row, block_rows + 2 * radius, 0)
        values_blk = lax.dynamic_slice_in_dim(values_ext, first_row, block_rows + 2 * radius, 0)
        allowed = window_mask(lax.dynamic_slice_in_dim(near, first_row, block_rows, 0), lax.dynamic_slice_in_dim(near_ext, first_row, block_rows + 2 * radius, 0), radius)
        logits = jnp.einsum('qhd,khd->hqk', queries_blk, keys_blk, precision=HIGHEST) * scale
        scores = jnp.where(allowed[None], low_back(logits), NEGATIVE)
        peak = lax.optimization_barrier(jnp.max(scores, axis=-1, keepdims=True))
        exponent = jnp.exp(scores - peak)
        shares = exponent / lax.optimization_barrier(jnp.sum(exponent, axis=-1, keepdims=True))
        return jnp.einsum('hqk,khd->qhd', low(shares), values_blk, precision=HIGHEST)
    block_starts = jnp.arange(token_count // block_rows, dtype=jnp.int32) * block_rows
    outputs = lax.map(jax.checkpoint(one_block), block_starts)
    return outputs.reshape(token_count, -1)

def forward(inputs, qkv_w, attn_w, glu_w, down_w, attn_g, ffn_g, positions):
    token_count, model_width = inputs.shape
    normed = low(layer_norm(inputs, attn_g))
    joined = low_back(jnp.dot(normed, qkv_w, precision=HIGHEST))
    cosine, sine = angles(positions, HEAD)
    split_dims = (token_count, HEADS, HEAD)
    queries = low(rotate(joined[:, :model_width].reshape(split_dims), cosine, sine))
    key_rows = low(rotate(joined[:, model_width:2 * model_width].reshape(split_dims), cosine, sine))
    value_rows = low(joined[:, 2 * model_width:].reshape(split_dims))
    context = low(low_back(attention(queries, key_rows, value_rows, positions)))
    hidden = inputs + low_back(jnp.dot(context, attn_w, precision=HIGHEST))
    normed_mlp = low(layer_norm(hidden, ffn_g))
    gate_up = low_back(jnp.dot(normed_mlp, glu_w, precision=HIGHEST))
    activated = low(geglu(gate_up[:, :FF], gate_up[:, FF:]))
    return hidden + jnp.dot(activated, down_w, precision=HIGHEST)

def reference(tokens, positions, qkv_weight, attn_weight, glu_weight, down_weight, attn_gain, ffn_gain, cotangent):
    floats = (tokens.astype(jnp.float32), qkv_weight.astype(jnp.float32), attn_weight.astype(jnp.float32), glu_weight.astype(jnp.float32), down_weight.astype(jnp.float32), attn_gain.astype(jnp.float32), ffn_gain.astype(jnp.float32))

    def layer(inputs, qkv_w, attn_w, glu_w, down_w, attn_g, ffn_g):
        return forward(inputs, qkv_w, attn_w, glu_w, down_w, attn_g, ffn_g, positions)
    mixed, pullback = jax.vjp(layer, *floats)
    grads = pullback(cotangent.astype(jnp.float32))
    return (mixed.astype(jnp.bfloat16), grads[0].astype(jnp.bfloat16), grads[1], grads[2], grads[3], grads[4], grads[5], grads[6])
```

```python
import math

import jax
import jax.numpy as jnp
from jax import lax
from jax.experimental import pallas as pl
from jax.experimental.pallas import tpu as pltpu
from jax.sharding import PartitionSpec as P

HEAD = 64
RADIUS = 64
BLOCK = 128
HALF = 384
EPSILON = 1e-05
THETA_BASE = 10000.0
NEGATIVE = -1e30
VMEM_BYTES = 56 * 1024 * 1024
BF = jnp.bfloat16
F32 = jnp.float32


def xor_send(array, axis, bit):
    count = lax.axis_size(axis)
    return lax.ppermute(array, axis, [(i, i ^ bit) for i in range(count)])


def bits_of(count):
    return [1 << i for i in range(count.bit_length() - 1)]


def gather_pieces(first, second, chip_bits):
    streams = ([(0, 0, first)], [(0, 1, second)])
    for stage in range(len(chip_bits)):
        grown = []
        for which, bit in ((0, chip_bits[stage]), (1, chip_bits[-1 - stage])):
            grown.append(
                [(j ^ bit, s, xor_send(a, "shard", bit)) for j, s, a in streams[which]]
            )
        for held, new in zip(streams, grown):
            held.extend(new)
    pieces = streams[0] + streams[1]
    return pieces + [(j ^ 1, s, xor_send(a, "shard", 1)) for j, s, a in pieces]


def add_low(left, right):
    return (left.astype(F32) + right.astype(F32)).astype(BF)


def scatter_sum(send, keep, order):
    for step, bit in enumerate(order):
        total = add_low(keep, xor_send(send, "shard", bit))
        if step + 1 < len(order):
            middle = total.shape[0] // 2
            keep, send = total[:middle], total[middle:]
    return total[0]


def replica_sum(first, second):
    count = lax.axis_size("replica")
    at = lax.axis_index("replica")
    if count == 1:
        return first, second
    bits = bits_of(count)
    odd = (at & 1) != 0
    held = add_low(
        jnp.where(odd, second, first), xor_send(jnp.where(odd, first, second), "replica", 1)
    )
    for bit in bits[1:]:
        high = (at & bit) != 0
        middle = held.shape[0] // 2
        top, bottom = held[:middle], held[middle:]
        held = add_low(
            jnp.where(high, bottom, top), xor_send(jnp.where(high, top, bottom), "replica", bit)
        )
    for bit in reversed(bits[1:]):
        high = (at & bit) != 0
        other = xor_send(held, "replica", bit)
        held = jnp.concatenate([jnp.where(high, other, held), jnp.where(high, held, other)], axis=0)
    other = xor_send(held, "replica", 1)
    return jnp.where(odd, other, held), jnp.where(odd, held, other)


def dot(left, right):
    return jnp.dot(left, right, preferred_element_type=F32)


def dot_cols(left, right):
    return lax.dot_general(left, right, (((1,), (1,)), ((), ())), preferred_element_type=F32)


def dot_rows(left, right):
    return lax.dot_general(left, right, (((0,), (0,)), ((), ())), preferred_element_type=F32)


def standardize(vector):
    average = jnp.mean(vector, axis=-1, keepdims=True)
    centred = vector - average
    spread = jnp.mean(centred * centred, axis=-1, keepdims=True)
    inverse = lax.rsqrt(spread + EPSILON)
    return centred * inverse, inverse


def norm_back(grad, gain, hat, inverse):
    dhat = grad * gain
    mean = jnp.mean(dhat, axis=-1, keepdims=True)
    along = jnp.mean(dhat * hat, axis=-1, keepdims=True)
    return (dhat - mean - hat * along) * inverse


def turned(vector):
    width = vector.shape[-1]
    lane = lax.broadcasted_iota(jnp.int32, vector.shape, 1)
    return jnp.where(
        (lane & 63) < 32, pltpu.roll(vector, width - 32, 1), pltpu.roll(vector, 32, 1)
    )


def place(me, pieces, refs, layout, sems):
    copies = []
    for (j, stream), ref in zip(pieces, refs):
        owner = me ^ j
        for row, rows, col, cols, dst, dst_col in layout[stream]:
            start = owner * rows
            if rows % 16 == 0:
                start = pl.multiple_of(start, 16)
            copy = pltpu.make_async_copy(
                ref.at[pl.ds(row, rows), pl.ds(col, cols)],
                dst.at[pl.ds(start, rows), pl.ds(dst_col, cols)],
                sems.at[len(copies)],
            )
            copy.start()
            copies.append(copy)
    return copies


def call(kernel, out_shape, inputs, in_any, scratch, flops, traffic):
    any_spec = pl.BlockSpec(memory_space=pl.ANY)
    vmem = pl.BlockSpec(memory_space=pltpu.VMEM)
    smem = pl.BlockSpec(memory_space=pltpu.SMEM)
    specs = [smem] + [vmem] * (len(inputs) - 1) + [any_spec] * len(in_any)
    return pl.pallas_call(
        kernel,
        out_shape=out_shape,
        in_specs=specs,
        out_specs=jax.tree.map(lambda _: vmem, out_shape),
        scratch_shapes=scratch,
        compiler_params=pltpu.CompilerParams(vmem_limit_bytes=VMEM_BYTES),
        cost_estimate=pl.CostEstimate(flops=flops, bytes_accessed=traffic, transcendentals=0),
    )(*inputs, *in_any)


def shaped(shape, dtype):
    return jax.ShapeDtypeStruct(shape, dtype)


def qkv_layout(rows, weight, gains):
    wide = 3 * HALF
    return (
        ((0, rows, 0, wide, weight, 0), (0, rows, wide, 128, gains, 0)),
        ((0, rows, 0, wide, weight, wide),),
    )


def project_kernel(pieces, rows, width):
    heads = width // HEAD

    def body(me_ref, before, own, after, cosine, sine, bias, *rest):
        refs, rest = rest[: len(pieces)], rest[len(pieces) :]
        q_out, k_out, v_out, p_out, ctx_out, normed_out, gains_out = rest[:7]
        weight, gain_cols, normed, sems = rest[7:]
        copies = place(me_ref[0], pieces, refs, qkv_layout(rows, weight, gain_cols), sems)
        hats = [standardize(ref[...].astype(F32))[0] for ref in (before, own, after)]
        for copy in copies:
            copy.wait()
        pick = jnp.where(
            lax.broadcasted_iota(jnp.int32, (8, 128), 0)
            == lax.broadcasted_iota(jnp.int32, (8, 128), 1),
            1.0,
            0.0,
        ).astype(BF)
        gains = dot_cols(pick, gain_cols[...])
        gains_out[...] = gains
        for i, hat in enumerate(hats):
            normed[i * BLOCK : (i + 1) * BLOCK, :] = (hat * gains[0:1]).astype(BF)
        normed_out[...] = normed[BLOCK : 2 * BLOCK, :]
        cos2 = jnp.concatenate([cosine[...]] * 2, axis=1)
        sin2 = jnp.concatenate([sine[...]] * 2, axis=1)
        mid = slice(RADIUS, RADIUS + 2 * BLOCK)
        for c in range(0, width, 256):
            joined = dot(normed[mid, :], weight[:, c : c + 256])
            joined = joined * cos2[mid] + turned(joined) * sin2[mid]
            q_out[:, c : c + 256] = joined.astype(BF)
            joined = dot(normed[...], weight[:, width + c : width + c + 256])
            joined = joined * cos2 + turned(joined) * sin2
            k_out[:, c : c + 256] = joined.astype(BF)
            joined = dot(normed[...], weight[:, 2 * width + c : 2 * width + c + 256])
            v_out[:, c : c + 256] = joined.astype(BF)
        lane = lax.broadcasted_iota(jnp.int32, (BLOCK, 128), 1)
        scale = 1.0 / math.sqrt(HEAD)
        for pair in range(heads // 2):
            cols = slice(pair * 128, pair * 128 + 128)
            for b in range(2):
                rows_q = slice(b * BLOCK, (b + 1) * BLOCK)
                rows_k = slice(b * BLOCK, (b + 2) * BLOCK)
                queries, keys, values = q_out[rows_q, cols], k_out[rows_k, cols], v_out[rows_k, cols]
                parts = []
                for h in range(2):
                    mine = (lane < HEAD) if h == 0 else (lane >= HEAD)
                    masked = jnp.where(mine, queries.astype(F32) * scale, 0.0).astype(BF)
                    scores = dot_cols(masked, keys) + bias[rows_q, :]
                    exponent = jnp.exp(scores - jnp.max(scores, axis=1, keepdims=True))
                    total = jnp.sum(exponent, axis=1, keepdims=True)
                    shares = (exponent * (1.0 / total)).astype(BF)
                    p_out[(pair * 2 + h) * 2 + b] = shares
                    parts.append(dot(shares, values))
                ctx_out[rows_q, cols] = jnp.where(lane < HEAD, parts[0], parts[1]).astype(BF)

    return body


def mlp_layout(rows, down_rows, attn, glu, down):
    width, hidden = 2 * HALF, 3 * HALF
    streams = []
    for s in range(2):
        parts = [(0, rows, 0, HALF, attn, s * HALF)]
        for c in range(3):
            parts.append(((1 + c) * rows, rows, 0, HALF, glu, s * hidden + c * HALF))
        if down is not None:
            parts.append((4 * rows, down_rows, 0, HALF, down, s * HALF))
        streams.append(tuple(parts))
    return tuple(streams)


def mlp_kernel(pieces, rows, down_rows, width, hidden, down_given):
    def body(me_ref, before, own, after, ctx, dy_before, dy_own, dy_after, gains, *rest):
        down_ref = None
        if down_given:
            down_ref, rest = rest[0], rest[1:]
        refs, rest = rest[: len(pieces)], rest[len(pieces) :]
        mixed_out, shared_out, ghid_out, gctx_out, fgain_out = rest[:5]
        if down_given:
            attn, glu, x_mid, dy, ggu, sems = rest[5:]
            layout = mlp_layout(rows, down_rows, attn, glu, None)
            down = down_ref
        else:
            attn, glu, x_mid, dy, ggu, down, sems = rest[5:]
            layout = mlp_layout(rows, down_rows, attn, glu, down)
        copies = place(me_ref[0], pieces, refs, layout, sems)
        mine = slice(RADIUS, RADIUS + BLOCK)
        x_mid[0:RADIUS, :] = before[BLOCK - RADIUS :, :].astype(F32)
        x_mid[mine, :] = own[...].astype(F32)
        x_mid[RADIUS + BLOCK :, :] = after[0:RADIUS, :].astype(F32)
        dy[0:RADIUS, :] = dy_before[...]
        dy[mine, :] = dy_own[...]
        dy[RADIUS + BLOCK :, :] = dy_after[...]
        for copy in copies:
            copy.wait()
        x_mid[...] = x_mid[...] + dot(ctx[...], attn[...])
        hat, inverse = standardize(x_mid[...])
        gain = gains[1:2, :]
        normed = (hat * gain).astype(BF)
        low = 0
        shared_out[:, 0:width] = normed[mine]
        mixed = x_mid[mine, :]
        act_at, ggu_at = width, width + hidden
        for c in range(0, hidden, HALF):
            cols = slice(c, c + HALF)
            gate = dot(normed, glu[:, c : c + HALF])
            up = dot(normed, glu[:, hidden + c : hidden + c + HALF])
            grad_act = dot_cols(dy[...], down[c : c + HALF, :])
            share = 0.5 * (1.0 + lax.erf(gate * (1.0 / math.sqrt(2.0))))
            density = jnp.exp(-0.5 * gate * gate) * (1.0 / math.sqrt(2.0 * math.pi))
            gelu = gate * share
            act = (gelu[mine] * up[mine]).astype(BF)
            shared_out[:, act_at + c : act_at + c + HALF] = act
            mixed = mixed + dot(act, down[c : c + HALF, :])
            ggu[:, cols] = (grad_act * up * (share + gate * density)).astype(BF)
            ggu[:, hidden + c : hidden + c + HALF] = (grad_act * gelu).astype(BF)
        mixed_out[...] = mixed.astype(BF)
        shared_out[:, ggu_at : ggu_at + 2 * hidden] = ggu[mine, :]
        grad = dot_cols(ggu[...], glu[...])
        fgain = jnp.sum(grad[mine] * hat[mine], axis=0, keepdims=True)
        fgain_out[...] = jnp.broadcast_to(fgain, fgain_out.shape)
        grad_hidden = dy[...].astype(F32) + norm_back(grad, gain, hat, inverse)
        ghid_out[...] = grad_hidden[mine]
        grad_low = grad_hidden.astype(BF)
        ctx_at = ggu_at + 2 * hidden
        shared_out[:, ctx_at : ctx_at + width] = ctx[mine, :]
        shared_out[:, ctx_at + width : ctx_at + 2 * width] = grad_low[mine]
        gctx_out[...] = dot_cols(grad_low, attn[...]).astype(BF)

    return body


def back_kernel(pieces, rows, width):
    heads = width // HEAD

    def body(me_ref, gctx, q, k, v, p, cosine, sine, own, ghid, gains, fgain, *rest):
        refs, rest = rest[: len(pieces)], rest[len(pieces) :]
        gj_out, gtok_out, weight, gain_cols, sems = rest
        copies = place(me_ref[0], pieces, refs, qkv_layout(rows, weight, gain_cols), sems)
        lane = lax.broadcasted_iota(jnp.int32, (BLOCK, 128), 1)
        scale = 1.0 / math.sqrt(HEAD)
        cos, sin = cosine[BLOCK : 2 * BLOCK, :], sine[BLOCK : 2 * BLOCK, :]
        for pair in range(heads // 2):
            cols = slice(pair * 128, pair * 128 + 128)
            grad_q = jnp.zeros((BLOCK, 128), F32)
            grad_k = jnp.zeros((BLOCK, 128), F32)
            grad_v = jnp.zeros((BLOCK, 128), F32)
            for h in range(2):
                mine = (lane < HEAD) if h == 0 else (lane >= HEAD)
                scores, shares, queries, grads, pieces_q = [], [], [], [], []
                for b in range(2):
                    rows_q = slice(b * BLOCK, (b + 1) * BLOCK)
                    rows_k = slice(b * BLOCK, (b + 2) * BLOCK)
                    keys, values = k[rows_k, cols], v[rows_k, cols]
                    lowered = jnp.where(mine, gctx[rows_q, cols].astype(F32), 0.0).astype(BF)
                    query = jnp.where(mine, q[rows_q, cols].astype(F32) * scale, 0.0).astype(BF)
                    share = p[(pair * 2 + h) * 2 + b]
                    wide = share.astype(F32)
                    grad_share = dot_cols(lowered, values)
                    row = jnp.sum(wide * grad_share, axis=1, keepdims=True)
                    grad_score = (wide * (grad_share - row)).astype(BF)
                    ours = slice(BLOCK, 2 * BLOCK) if b == 0 else slice(0, BLOCK)
                    scores.append(grad_score[:, ours])
                    shares.append(share[:, ours])
                    queries.append(query)
                    grads.append(lowered)
                    mid = slice(RADIUS, BLOCK) if b == 0 else slice(0, RADIUS)
                    pieces_q.append(dot(grad_score[mid], keys))
                part = jnp.concatenate(pieces_q, axis=0) * scale
                grad_q = grad_q + jnp.where(mine, part, 0.0)
                grad_k = grad_k + dot_rows(
                    jnp.concatenate(scores, axis=0), jnp.concatenate(queries, axis=0)
                )
                grad_v = grad_v + dot_rows(
                    jnp.concatenate(shares, axis=0), jnp.concatenate(grads, axis=0)
                )
            at = pair * 128
            gj_out[0:BLOCK, at : at + 128] = (grad_q * cos - turned(grad_q) * sin).astype(BF)
            at += width
            gj_out[0:BLOCK, at : at + 128] = (grad_k * cos - turned(grad_k) * sin).astype(BF)
            at += width
            gj_out[0:BLOCK, at : at + 128] = grad_v.astype(BF)
        for copy in copies:
            copy.wait()
        hat, inverse = standardize(own[...].astype(F32))
        grad = dot_cols(gj_out[0:BLOCK, :], weight[...])
        gain = gains[0:1, :]
        again = jnp.sum(grad * hat, axis=0, keepdims=True)
        gtok_out[...] = (ghid[...] + norm_back(grad, gain, hat, inverse)).astype(BF)
        tail = gj_out.shape[0] - BLOCK
        line = lax.broadcasted_iota(jnp.int32, (tail, width), 0)
        both = jnp.where(line == 0, again, jnp.where(line == 1, fgain[0:1, :], 0.0))
        gj_out[BLOCK:, 0:width] = both.astype(BF)
        gj_out[BLOCK:, width:] = jnp.zeros((tail, 2 * width), BF)

    return body


def slots_of(count, chip_bits):
    streams = []
    for order in (chip_bits, chip_bits[::-1]):
        kept = [0]
        for bit in order[1:][::-1]:
            kept = kept + [j | bit for j in kept]
        table = {j: (1, i) for i, j in enumerate(kept)}
        table.update({j | order[0]: (0, i) for i, j in enumerate(kept)})
        streams.append(table)
    return streams


def weight_grad(me, js, lhs_t, rhs, rows, cols, emit):
    left = jnp.concatenate(
        [
            lhs_t[pl.ds(pl.multiple_of((me ^ j) * rows, 16 if rows % 16 == 0 else 8), rows), :]
            for j in js
        ],
        axis=0,
    ).astype(BF)
    grad = dot(left, rhs[:, cols]).astype(BF)
    for i, j in enumerate(js):
        emit(j, grad[i * rows : (i + 1) * rows])


def mlp_grad_kernel(js, slots, rows, down_rows, width, hidden):
    def body(me_ref, own, other, dy_own, dy_other, *rest):
        outs, (normed_t, act_t, ctx_t, ggu, low, dy) = rest[:4], rest[4:]
        me = me_ref[0]
        act_at, ggu_at = width, width + hidden
        ctx_at = ggu_at + 2 * hidden
        for i, (ref, dref) in enumerate(((own, dy_own), (other, dy_other))):
            tok = slice(i * BLOCK, (i + 1) * BLOCK)
            normed_t[:, tok] = ref[:, 0:width].T.astype(normed_t.dtype)
            act_t[:, tok] = ref[:, act_at : act_at + hidden].T.astype(act_t.dtype)
            ctx_t[:, tok] = ref[:, ctx_at : ctx_at + width].T.astype(ctx_t.dtype)
            ggu[tok, :] = ref[:, ggu_at : ggu_at + 2 * hidden]
            low[tok, :] = ref[:, ctx_at + width : ctx_at + 2 * width]
            dy[tok, :] = dref[...]

        def emit_at(stream, row):
            def emit(j, grad):
                kept, i = slots[stream][j]
                outs[2 * stream + kept][i, row : row + grad.shape[0], :] = grad

            return emit

        for s in range(2):
            half = slice(s * HALF, (s + 1) * HALF)
            weight_grad(me, js, ctx_t, low, rows, half, emit_at(s, 0))
            for c in range(3):
                at = s * hidden + c * HALF
                weight_grad(
                    me, js, normed_t, ggu, rows, slice(at, at + HALF), emit_at(s, (1 + c) * rows)
                )
            weight_grad(me, js, act_t, dy, down_rows, half, emit_at(s, 4 * rows))

    return body


def qkv_grad_kernel(js, slots, rows, width):
    def body(me_ref, normed_own, normed_other, own, other, *rest):
        outs, (normed_t, gj) = rest[:4], rest[4:]
        me = me_ref[0]
        for i, (nref, ref) in enumerate(((normed_own, own), (normed_other, other))):
            tok = slice(i * BLOCK, (i + 1) * BLOCK)
            normed_t[:, tok] = nref[...].T.astype(normed_t.dtype)
            gj[tok, :] = ref[0:BLOCK, :]
        gains = own[BLOCK : BLOCK + 16, 0:width].astype(F32) + other[
            BLOCK : BLOCK + 16, 0:width
        ].astype(F32)
        for s in range(2):

            def emit_at(row):
                def emit(j, grad):
                    kept, i = slots[s][j]
                    outs[2 * s + kept][i, row : row + rows, :] = grad

                return emit

            for c in range(3):
                at = s * 3 * HALF + c * HALF
                weight_grad(me, js, normed_t, gj, rows, slice(at, at + HALF), emit_at(c * rows))
            for j in js:
                kept, i = slots[s][j]
                moved = pltpu.roll(gains, lax.rem(width - (me ^ j) * rows, width), 1)
                outs[2 * s + kept][i, 3 * rows : 3 * rows + 16, :] = moved[:, 0:HALF].astype(BF)

    return body


def on_device(
    tokens,
    positions,
    qkv_weight,
    attn_weight,
    glu_weight,
    down_weight,
    attn_gain,
    ffn_gain,
    cotangent,
):
    block, width = tokens.shape
    rows, down_rows = qkv_weight.shape[0], down_weight.shape[0]
    hidden = glu_weight.shape[1] // 2
    heads = width // HEAD
    count = lax.axis_size("shard")
    everyone = count * lax.axis_size("replica")
    me = lax.axis_index("shard").astype(jnp.int32)
    me_arr = me[None]
    chip_bits = bits_of(count)[1:]

    gain_cols = jnp.pad(jnp.stack([attn_gain, ffn_gain], axis=1), ((0, 0), (0, 126)))
    first = jnp.concatenate([qkv_weight[:, : 3 * HALF], gain_cols], axis=1)
    qkv_parts = gather_pieces(first, qkv_weight[:, 3 * HALF :], chip_bits)

    up = [(i, i + 1) for i in range(everyone - 1)]
    down = [(i + 1, i) for i in range(everyone - 1)]
    both = ("shard", "replica")
    places = jnp.stack([positions >> 8, positions & 255]).astype(BF)
    places = jnp.pad(places, ((0, 14), (0, width - block)))
    before = lax.ppermute(
        jnp.concatenate([tokens, cotangent[block - RADIUS :], places], axis=0), both, up
    )
    after = lax.ppermute(jnp.concatenate([tokens, cotangent[:RADIUS], places], axis=0), both, down)
    dy_other = xor_send(cotangent, "shard", 1)

    def places_of(packed):
        near = packed[block + RADIUS : block + RADIUS + 2, :block].astype(F32)
        return near[0] * 256.0 + near[1]

    where = jnp.concatenate([places_of(before), positions.astype(F32), places_of(after)])
    middle = HEAD // 2
    inverse = THETA_BASE ** (-(jnp.arange(middle, dtype=F32) * 2.0 / HEAD))
    phases = where[:, None] * inverse[None, :]
    cosine, sine = jnp.cos(phases), jnp.sin(phases)
    cosine = jnp.concatenate([cosine] * 4, axis=1)
    sine = jnp.concatenate([-sine, sine, -sine, sine], axis=1)
    offset = (
        jnp.arange(2 * BLOCK, dtype=jnp.int32)[None, :]
        - RADIUS
        - jnp.arange(BLOCK, dtype=jnp.int32)[:, None]
    )
    bias = []
    for b in range(2):
        later_key = where[None, b * BLOCK : (b + 2) * BLOCK] >= offset.astype(F32)
        start = RADIUS + b * BLOCK
        later_query = where[start : start + BLOCK, None] >= -offset.astype(F32)
        allowed = (jnp.abs(offset) <= RADIUS) & jnp.where(offset >= 0, later_key, later_query)
        bias.append(jnp.where(allowed, 0.0, NEGATIVE))
    bias = jnp.concatenate(bias, axis=0).astype(F32)

    packs = []
    for s in range(2):
        half = slice(s * HALF, (s + 1) * HALF)
        parts = [attn_weight[:, half]]
        parts += [
            glu_weight[:, s * hidden + c * HALF : s * hidden + (c + 1) * HALF] for c in range(3)
        ]
        packs.append(jnp.concatenate(parts + [down_weight[:, half]], axis=0))
    mlp_parts = gather_pieces(packs[0], packs[1], chip_bits)

    qkv_names = [(j, s) for j, s, _ in qkv_parts]
    qkv_arrays = [a for _, _, a in qkv_parts]
    mlp_names = [(j, s) for j, s, _ in mlp_parts]
    mlp_arrays = [a for _, _, a in mlp_parts]
    weight_bytes = width * 3 * width * 2

    tok_before, tok_after = before[:block], after[:block]
    q, k, v, p, ctx, normed, gains = call(
        project_kernel(qkv_names, rows, width),
        (
            shaped((2 * BLOCK, width), BF),
            shaped((3 * BLOCK, width), BF),
            shaped((3 * BLOCK, width), BF),
            shaped((2 * heads, BLOCK, 2 * BLOCK), BF),
            shaped((2 * BLOCK, width), BF),
            shaped((BLOCK, width), BF),
            shaped((8, width), F32),
        ),
        (me_arr, tok_before, tokens, tok_after, cosine, sine, bias),
        qkv_arrays,
        [
            pltpu.VMEM((width, 3 * width), BF),
            pltpu.VMEM((width, 128), BF),
            pltpu.VMEM((3 * BLOCK, width), BF),
            pltpu.SemaphoreType.DMA((3 * len(qkv_arrays),)),
        ],
        8_000_000_000,
        2 * weight_bytes,
    )
    normed_other = xor_send(normed, "shard", 1)

    down_full = ()
    extra = [pltpu.VMEM((count * down_rows, width), BF)]
    if down_rows % 16:
        halves = []
        order = me ^ jnp.arange(count, dtype=jnp.int32)
        for s in range(2):
            held = {j: a[4 * rows :] for j, t, a in mlp_parts if t == s}
            halves.append(jnp.stack([held[j] for j in range(count)])[order])
        down_full = (jnp.concatenate(halves, axis=2).reshape(count * down_rows, width),)
        extra = []
    shared_width = 3 * width + 3 * hidden
    mixed, shared, ghid, gctx, fgain = call(
        mlp_kernel(mlp_names, rows, down_rows, width, hidden, bool(down_full)),
        (
            shaped((BLOCK, width), BF),
            shaped((BLOCK, shared_width), BF),
            shaped((BLOCK, width), F32),
            shaped((2 * BLOCK, width), BF),
            shaped((8, width), F32),
        ),
        (
            me_arr,
            tok_before,
            tokens,
            tok_after,
            ctx,
            before[block : block + RADIUS],
            cotangent,
            after[block : block + RADIUS],
            gains,
        )
        + down_full,
        mlp_arrays,
        [
            pltpu.VMEM((width, width), BF),
            pltpu.VMEM((width, 2 * hidden), BF),
            pltpu.VMEM((2 * BLOCK, width), F32),
            pltpu.VMEM((2 * BLOCK, width), BF),
            pltpu.VMEM((2 * BLOCK, 2 * hidden), BF),
        ]
        + extra
        + [pltpu.SemaphoreType.DMA((5 * len(mlp_arrays),))],
        8_000_000_000,
        3 * weight_bytes,
    )
    shared_other = xor_send(shared, "shard", 1)

    gj, grad_tokens = call(
        back_kernel(qkv_names, rows, width),
        (shaped((BLOCK + 16, 3 * width), BF), shaped((BLOCK, width), BF)),
        (me_arr, gctx, q, k, v, p, cosine, sine, tokens, ghid, gains, fgain),
        qkv_arrays,
        [
            pltpu.VMEM((width, 3 * width), BF),
            pltpu.VMEM((width, 128), BF),
            pltpu.SemaphoreType.DMA((3 * len(qkv_arrays),)),
        ],
        8_000_000_000,
        2 * weight_bytes,
    )
    gj_other = xor_send(gj, "shard", 1)

    js = [2 * i for i in range(count // 2)]
    slots = slots_of(count, chip_bits)
    portion = count // 4

    def stack(height):
        return (shaped((portion, height, HALF), BF),) * 4

    act_type = BF if down_rows % 16 == 0 else F32
    height = 4 * rows + down_rows
    sums = call(
        mlp_grad_kernel(js, slots, rows, down_rows, width, hidden),
        stack(height),
        (me_arr, shared, shared_other, cotangent, dy_other),
        [],
        [
            pltpu.VMEM((width, 2 * BLOCK), BF),
            pltpu.VMEM((hidden, 2 * BLOCK), act_type),
            pltpu.VMEM((width, 2 * BLOCK), BF),
            pltpu.VMEM((2 * BLOCK, 2 * hidden), BF),
            pltpu.VMEM((2 * BLOCK, width), BF),
            pltpu.VMEM((2 * BLOCK, width), BF),
        ],
        3_000_000_000,
        2 * weight_bytes,
    )
    mlp_sums = [
        scatter_sum(sums[0], sums[1], chip_bits),
        scatter_sum(sums[2], sums[3], chip_bits[::-1]),
    ]
    mlp_sums = replica_sum(*mlp_sums)

    sums = call(
        qkv_grad_kernel(js, slots, rows, width),
        stack(3 * rows + 16),
        (me_arr, normed, normed_other, gj, gj_other),
        [],
        [pltpu.VMEM((width, 2 * BLOCK), BF), pltpu.VMEM((2 * BLOCK, 3 * width), BF)],
        2_000_000_000,
        weight_bytes,
    )
    qkv_sums = [
        scatter_sum(sums[0], sums[1], chip_bits),
        scatter_sum(sums[2], sums[3], chip_bits[::-1]),
    ]
    qkv_sums = replica_sum(*qkv_sums)

    def columns(sums, first_row):
        return [
            part[first_row + c * rows : first_row + (c + 1) * rows] for part in sums for c in range(3)
        ]

    grad_attn = jnp.concatenate([part[:rows] for part in mlp_sums], axis=1).astype(F32)
    grad_glu = jnp.concatenate(columns(mlp_sums, rows), axis=1).astype(F32)
    grad_down = jnp.concatenate([part[4 * rows :] for part in mlp_sums], axis=1).astype(F32)
    grad_qkv = jnp.concatenate(columns(qkv_sums, 0), axis=1).astype(F32)
    grad_gains = qkv_sums[0][3 * rows :, :rows].astype(F32)
    return (
        mixed,
        grad_tokens,
        grad_qkv,
        grad_attn,
        grad_glu,
        grad_down,
        grad_gains[0],
        grad_gains[1],
    )


def solution(mesh):
    in_specs = (
        P(("shard", "replica"), None),
        P(("shard", "replica")),
        P("shard", None),
        P("shard", None),
        P("shard", None),
        P("shard", None),
        P("shard"),
        P("shard"),
        P(("shard", "replica"), None),
    )
    out_specs = (
        P(("shard", "replica"), None),
        P(("shard", "replica"), None),
        P("shard", None),
        P("shard", None),
        P("shard", None),
        P("shard", None),
        P("shard"),
        P("shard"),
    )
    return jax.shard_map(
        on_device, mesh=mesh, in_specs=in_specs, out_specs=out_specs, check_vma=False
    )
```

```python
import math

import jax
import jax.numpy as jnp
from jax import lax
from jax.experimental import pallas as pl
from jax.experimental.pallas import tpu as pltpu
from jax.sharding import PartitionSpec as P

HEAD = 64
RADIUS = 64
BLOCK = 128
EPSILON = 1e-05
THETA_BASE = 10000.0
NEGATIVE = -1e30
VMEM_BYTES = 56 * 1024 * 1024
BF = jnp.bfloat16
F32 = jnp.float32


def xor_send(array, axis, bit):
    count = lax.axis_size(axis)
    return lax.ppermute(array, axis, [(i, i ^ bit) for i in range(count)])


def bits_of(count):
    return [1 << i for i in range(count.bit_length() - 1)]


def gather_pieces(own, split, chip_bits):
    if len(chip_bits) == 2:
        x, y = chip_bits
        from_x, from_y = xor_send(own, "shard", x), xor_send(own, "shard", y)
        pieces = [(0, 2, own), (x, 2, from_x), (y, 2, from_y)]
        pieces.append((x | y, 0, xor_send(from_x[:, :split], "shard", y)))
        pieces.append((x | y, 1, xor_send(from_y[:, split:], "shard", x)))
    else:
        streams = ([(0, 0, own[:, :split])], [(0, 1, own[:, split:])])
        for stage in range(len(chip_bits)):
            grown = []
            for which, bit in ((0, chip_bits[stage]), (1, chip_bits[-1 - stage])):
                grown.append(
                    [(j ^ bit, s, xor_send(a, "shard", bit)) for j, s, a in streams[which]]
                )
            for held, more in zip(streams, grown):
                held.extend(more)
        pieces = streams[0] + streams[1]
    return pieces


def with_core(pieces, after=None):
    others = []
    for i, (j, s, a) in enumerate(pieces):
        if after is not None and i >= len(pieces) - 2:
            a, _ = lax.optimization_barrier((a, after))
        others.append((j ^ 1, s, xor_send(a, "shard", 1)))
    return pieces + others


def add_low(left, right):
    return (left.astype(F32) + right.astype(F32)).astype(BF)


def scatter_sum(send, keep, order, after=None):
    for bit in order[:-1]:
        other = xor_send(send, "shard", bit)
        if after is not None:
            other, _ = lax.optimization_barrier((other, after))
        middle = keep.shape[0] // 2
        send = add_low(keep[middle:], other[middle:])
        keep = add_low(keep[:middle], other[:middle])
    return keep, xor_send(send, "shard", order[-1])


def both_sums(sums_0, sums_1):
    return jnp.concatenate([add_low(k[0], o[0]) for k, o in (sums_0, sums_1)], axis=0)


def replica_sum(total):
    for bit in bits_of(lax.axis_size("replica"))[1:]:
        total = add_low(total, xor_send(total, "replica", bit))
    return total, xor_send(total, "replica", 1)


def dot(left, right):
    return jnp.dot(left, right, preferred_element_type=F32)


def dot_cols(left, right):
    return lax.dot_general(left, right, (((1,), (1,)), ((), ())), preferred_element_type=F32)


def dot_rows(left, right):
    return lax.dot_general(left, right, (((0,), (0,)), ((), ())), preferred_element_type=F32)


def standardize(vector):
    average = jnp.mean(vector, axis=-1, keepdims=True)
    centred = vector - average
    spread = jnp.mean(centred * centred, axis=-1, keepdims=True)
    inverse = lax.rsqrt(spread + EPSILON)
    return centred * inverse, inverse


def norm_back(grad, gain, hat, inverse):
    dhat = grad * gain
    mean = jnp.mean(dhat, axis=-1, keepdims=True)
    along = jnp.mean(dhat * hat, axis=-1, keepdims=True)
    return (dhat - mean - hat * along) * inverse


def turned(vector):
    width = vector.shape[-1]
    lane = lax.broadcasted_iota(jnp.int32, vector.shape, 1)
    return jnp.where(
        (lane & 63) < 32, pltpu.roll(vector, width - 32, 1), pltpu.roll(vector, 32, 1)
    )


def place(me, pieces, refs, layout, sems):
    copies = []
    for (j, stream), ref in zip(pieces, refs):
        owner = me ^ j
        for row, rows, col, cols, dst, dst_col in layout[stream]:
            start = owner * rows
            if rows % 16 == 0:
                start = pl.multiple_of(start, 16)
            copy = pltpu.make_async_copy(
                ref.at[pl.ds(row, rows), pl.ds(col, cols)],
                dst.at[pl.ds(start, rows), pl.ds(dst_col, cols)],
                sems.at[len(copies)],
            )
            copy.start()
            copies.append(copy)
    return copies


def call(kernel, out_shape, inputs, in_any, scratch, flops, traffic):
    any_spec = pl.BlockSpec(memory_space=pl.ANY)
    vmem = pl.BlockSpec(memory_space=pltpu.VMEM)
    smem = pl.BlockSpec(memory_space=pltpu.SMEM)
    specs = [smem] + [vmem] * (len(inputs) - 1) + [any_spec] * len(in_any)
    return pl.pallas_call(
        kernel,
        out_shape=out_shape,
        in_specs=specs,
        out_specs=jax.tree.map(lambda _: vmem, out_shape),
        scratch_shapes=scratch,
        compiler_params=pltpu.CompilerParams(vmem_limit_bytes=VMEM_BYTES),
        cost_estimate=pl.CostEstimate(flops=flops, bytes_accessed=traffic, transcendentals=0),
    )(*inputs, *in_any)


def shaped(shape, dtype):
    return jax.ShapeDtypeStruct(shape, dtype)


def pack_qkv_kernel(half):
    def body(info, weight, gains, out):
        width = 2 * half

        def pick(first):
            for i in range(3):
                out[:, i * half : (i + 1) * half] = weight[
                    :, i * width + first : i * width + first + half
                ]

        @pl.when(info[1] == 0)
        def _():
            pick(0)

        @pl.when(info[1] != 0)
        def _():
            pick(half)

        out[:, 3 * half :] = gains[...]

    return body


def pack_mlp_kernel(count, down_rows, take):
    def body(info, attn, glu, down, out):
        rows, width = attn.shape
        units = count * take
        hidden = count * down_rows
        out[:, 0:width] = attn[...]
        last = width + 2 * units

        def pick(first):
            for part in range(2):
                for s in range(count):
                    at = part * hidden + s * down_rows + first
                    to = width + part * units + s * take
                    out[:, to : to + take] = glu[:, at : at + take]
            out[0:take, last:] = down[first : first + take, :]

        @pl.when(info[1] == 0)
        def _():
            pick(0)

        @pl.when(info[1] != 0)
        def _():
            pick(down_rows - take)

        if rows > take:
            out[take:, last:] = jnp.zeros((rows - take, width), BF)

    return body


def around_kernel(info, own, dy_own, partner, near, far, tok, dy):
    mine = slice(0, BLOCK)

    def arrange(first, first_dy, second, second_dy, before, after):
        tok[0:BLOCK, :] = before[mine, :]
        tok[BLOCK : 2 * BLOCK, :] = first
        tok[2 * BLOCK : 3 * BLOCK, :] = second
        tok[3 * BLOCK :, :] = after[mine, :]
        halo = slice(BLOCK, BLOCK + RADIUS)
        dy[0:RADIUS, :] = before[halo, :]
        dy[RADIUS : RADIUS + BLOCK, :] = first_dy
        dy[RADIUS + BLOCK : RADIUS + 2 * BLOCK, :] = second_dy
        dy[RADIUS + 2 * BLOCK :, :] = after[halo, :]

    other = partner[mine, :]
    other_dy = partner[BLOCK : 2 * BLOCK, :]

    @pl.when(info[1] == 0)
    def _():
        arrange(own[...], dy_own[...], other, other_dy, near, far)

    @pl.when(info[1] != 0)
    def _():
        arrange(other, other_dy, own[...], dy_own[...], far, near)


def qkv_layout(rows, half, split, weight, gains):
    wide = 3 * half
    first = (0, rows, 0, split, weight, 0)
    second = ((0, rows, 0, wide - split, weight, split), (0, rows, wide - split, 128, gains, 0))
    whole = ((0, rows, 0, wide, weight, 0), (0, rows, wide, 128, gains, 0))
    return ((first,), second, whole)


def project_kernel(pieces, rows, width, split):
    half = width // 2
    span = 4 * BLOCK

    def body(info, tok, cosine, sine, bias, *rest):
        refs, rest = rest[: len(pieces)], rest[len(pieces) :]
        q_out, k_out, v_out, p_out, ctx_out, normed_out, gains_out = rest[:7]
        weight, gain_cols, normed, sems = rest[7:]
        layout = qkv_layout(rows, half, split, weight, gain_cols)
        copies = place(info[0], pieces, refs, layout, sems)
        hats = [
            standardize(tok[i * BLOCK : (i + 1) * BLOCK, :].astype(F32))[0] for i in range(4)
        ]
        for copy in copies:
            copy.wait()
        pick = jnp.where(
            lax.broadcasted_iota(jnp.int32, (8, 128), 0)
            == lax.broadcasted_iota(jnp.int32, (8, 128), 1),
            1.0,
            0.0,
        ).astype(BF)
        gains = dot_cols(pick, gain_cols[...])
        gains_out[...] = gains
        for i, hat in enumerate(hats):
            normed[i * BLOCK : (i + 1) * BLOCK, :] = (hat * gains[0:1]).astype(BF)
        normed_out[...] = normed[BLOCK : 3 * BLOCK, :]
        cos3 = jnp.concatenate([cosine[...]] * 3, axis=1)
        sin3 = jnp.concatenate([sine[...]] * 3, axis=1)
        mid = slice(RADIUS, span - RADIUS)
        joined = dot(normed[mid, :], weight[:, 0:half])
        q_out[...] = (joined * cos3[mid] + turned(joined) * sin3[mid]).astype(BF)
        joined = dot(normed[...], weight[:, half : 2 * half])
        k_out[...] = (joined * cos3 + turned(joined) * sin3).astype(BF)
        v_out[...] = dot(normed[...], weight[:, 2 * half : 3 * half]).astype(BF)
        lane = lax.broadcasted_iota(jnp.int32, (BLOCK, 128), 1)
        scale = 1.0 / math.sqrt(HEAD)
        for pair in range(half // 128):
            cols = slice(pair * 128, pair * 128 + 128)
            for b in range(3):
                rows_q = slice(b * BLOCK, (b + 1) * BLOCK)
                rows_k = slice(b * BLOCK, (b + 2) * BLOCK)
                queries, keys, values = q_out[rows_q, cols], k_out[rows_k, cols], v_out[rows_k, cols]
                parts = []
                for h in range(2):
                    mine = (lane < HEAD) if h == 0 else (lane >= HEAD)
                    masked = jnp.where(mine, queries.astype(F32) * scale, 0.0).astype(BF)
                    scores = dot_cols(masked, keys) + bias[rows_q, :]
                    exponent = jnp.exp(scores - jnp.max(scores, axis=1, keepdims=True))
                    total = jnp.sum(exponent, axis=1, keepdims=True)
                    shares = (exponent * (1.0 / total)).astype(BF)
                    p_out[(pair * 2 + h) * 3 + b] = shares
                    parts.append(dot(shares, values))
                ctx_out[rows_q, cols] = jnp.where(lane < HEAD, parts[0], parts[1]).astype(BF)

    return body


def mlp_layout(rows, take, width, units, attn, glu, down):
    one = (0, rows, 0, width, attn, 0)
    gate = (0, rows, width, units, glu, 0)
    up = (0, rows, 0, units, glu, units)
    low = (0, take, units, width, down, 0)
    whole = (one, (0, rows, width, 2 * units, glu, 0), (0, take, width + 2 * units, width, down, 0))
    return ((one, gate), (up, low), whole)


def mlp_kernel(pieces, rows, take, width, units):
    half = width // 2
    pair = slice(RADIUS, RADIUS + 2 * BLOCK)

    def body(info, tok, ctx_own, ctx_other, dy, gains, mask, *rest):
        refs, rest = rest[: len(pieces)], rest[len(pieces) :]
        mix_keep, mix_send, shared, ctx_pair, hidden, gn_out, fgain_out = rest[:7]
        attn, glu, down, ggu, mix, sems = rest[7:]
        layout = mlp_layout(rows, take, width, units, attn, glu, down)
        copies = place(info[0], pieces, refs, layout, sems)
        at = info[1]
        inputs = tok[RADIUS : RADIUS + 3 * BLOCK, :].astype(F32)
        own_rows = pl.ds(pl.multiple_of(at * half, 128), half)
        other_rows = pl.ds(pl.multiple_of((1 - at) * half, 128), half)

        @pl.when(at == 0)
        def _():
            ctx_pair[:, 0:half] = ctx_own[pair, :]
            ctx_pair[:, half:] = ctx_other[pair, :]

        @pl.when(at != 0)
        def _():
            ctx_pair[:, 0:half] = ctx_other[pair, :]
            ctx_pair[:, half:] = ctx_own[pair, :]

        for copy in copies:
            copy.wait()
        lifted = dot(ctx_own[...], attn[own_rows, :]) + dot(ctx_other[...], attn[other_rows, :])
        hidden[...] = inputs + lifted
        hat, _ = standardize(hidden[...])
        normed = (hat * gains[1:2, :]).astype(BF)
        shared[:, 0:width] = normed[pair]
        partial = jnp.zeros((2 * BLOCK, width), F32)
        for c in range(0, units, 256):
            wide = min(256, units - c)
            cols = slice(c, c + wide)
            gate = dot(normed, glu[:, cols])
            up = dot(normed, glu[:, units + c : units + c + wide])
            grad_act = dot_cols(dy[...], down[cols, :]) * mask[0:1, cols]
            share = 0.5 * (1.0 + lax.erf(gate * (1.0 / math.sqrt(2.0))))
            density = jnp.exp(-0.5 * gate * gate) * (1.0 / math.sqrt(2.0 * math.pi))
            gelu = gate * share
            act = (gelu[pair] * up[pair] * mask[0:1, cols]).astype(BF)
            shared[:, width + c : width + c + wide] = act
            partial = partial + dot(act, down[cols, :])
            ggu[:, cols] = (grad_act * up * (share + gate * density)).astype(BF)
            ggu[:, units + c : units + c + wide] = (grad_act * gelu).astype(BF)
        mix[...] = partial
        mine = pl.ds(pl.multiple_of(at * BLOCK, BLOCK), BLOCK)
        theirs = pl.ds(pl.multiple_of((1 - at) * BLOCK, BLOCK), BLOCK)
        mix_keep[...] = mix[mine, :] + hidden[pl.ds(pl.multiple_of(RADIUS + at * BLOCK, 8), BLOCK), :]
        mix_send[...] = mix[theirs, :].astype(BF)
        shared[:, width + units :] = ggu[pair, :]
        grad = dot_cols(ggu[...], glu[...])
        gn_out[...] = grad.astype(BF)
        fgain = jnp.sum(grad[pair] * hat[pair], axis=0, keepdims=True)
        fgain_out[...] = jnp.broadcast_to(fgain, fgain_out.shape)

    return body


def pair_back(pair, gctx, q, k, v, p, cos, sin):
    lane = lax.broadcasted_iota(jnp.int32, (BLOCK, 128), 1)
    lane2 = lax.broadcasted_iota(jnp.int32, (2 * BLOCK, 128), 1)
    scale = 1.0 / math.sqrt(HEAD)
    cols = slice(pair * 128, pair * 128 + 128)
    first, second = slice(0, BLOCK), slice(BLOCK, 2 * BLOCK)
    low, high = slice(0, RADIUS), slice(RADIUS, BLOCK)
    grad_q = jnp.zeros((2 * BLOCK, 128), F32)
    grad_k, grad_v = [0.0, 0.0], [0.0, 0.0]
    for h in range(2):
        mine = (lane < HEAD) if h == 0 else (lane >= HEAD)
        mine2 = (lane2 < HEAD) if h == 0 else (lane2 >= HEAD)
        scores, shares, queries, grads, parts = [], [], [], [], []
        for b in range(3):
            rows_q = slice(b * BLOCK, (b + 1) * BLOCK)
            rows_k = slice(b * BLOCK, (b + 2) * BLOCK)
            keys, values = k[rows_k, cols], v[rows_k, cols]
            lowered = jnp.where(mine, gctx[rows_q, cols].astype(F32), 0.0).astype(BF)
            query = jnp.where(mine, q[rows_q, cols].astype(F32) * scale, 0.0).astype(BF)
            share = p[(pair * 2 + h) * 3 + b]
            wide = share.astype(F32)
            grad_share = dot_cols(lowered, values)
            row = jnp.sum(wide * grad_share, axis=1, keepdims=True)
            grad_score = (wide * (grad_share - row)).astype(BF)
            scores.append(grad_score)
            shares.append(share)
            queries.append(query)
            grads.append(lowered)
            part = (high, first, low)[b]
            parts.append(dot(grad_score[part], keys))
        grad_q = grad_q + jnp.where(mine2, jnp.concatenate(parts, axis=0) * scale, 0.0)
        for i in range(2):
            two = slice(i, i + 2)
            for total, left, right in ((grad_k, scores, queries), (grad_v, shares, grads)):
                upper, lower = left[i][:, second], left[i + 1][:, first]
                total[i] = total[i] + dot_rows(
                    jnp.concatenate([upper, lower], axis=0), jnp.concatenate(right[two], axis=0)
                )
    grad_k, grad_v = jnp.concatenate(grad_k, axis=0), jnp.concatenate(grad_v, axis=0)
    return (
        (grad_q * cos - turned(grad_q) * sin).astype(BF),
        (grad_k * cos - turned(grad_k) * sin).astype(BF),
        grad_v.astype(BF),
    )


def back_kernel(qkv_pieces, mlp_pieces, rows, width, split):
    half = width // 2
    pair = slice(RADIUS, RADIUS + 2 * BLOCK)

    def body(info, tok, gn_own, gn_other, hidden, dy, gains, fgain, q, k, v, p, cosine, sine, *rest):
        refs = rest[1:]
        n_qkv, n_mlp = len(qkv_pieces), len(mlp_pieces)
        qkv_refs, mlp_refs, rest = refs[:n_qkv], refs[n_qkv : n_qkv + n_mlp], refs[n_qkv + n_mlp :]
        gj_out, keep_out, send_out, ghid_out = rest[:4]
        weight, gain_cols, attn, gctx, held, sems, attn_sems = rest[4:]
        one = (0, rows, 0, width, attn, 0)
        attn_copies = place(info[0], mlp_pieces, mlp_refs, ((one,), (), (one,)), attn_sems)
        layout = qkv_layout(rows, half, split, weight, gain_cols)
        copies = place(info[0], qkv_pieces, qkv_refs, layout, sems)
        at = info[1]
        mine = pl.ds(pl.multiple_of(at * BLOCK, BLOCK), BLOCK)
        theirs = pl.ds(pl.multiple_of((1 - at) * BLOCK, BLOCK), BLOCK)
        hat, inverse = standardize(hidden[...])
        grad = gn_own[...].astype(F32) + gn_other[...].astype(F32)
        grad_hidden = dy[...].astype(F32) + norm_back(grad, gains[1:2, :], hat, inverse)
        held[...] = grad_hidden[pair]
        ghid_out[...] = held[mine, :]
        halves = jnp.where(at == 0, grad_hidden[pair, 0:half], grad_hidden[pair, half:])
        tokens_in = 2 * BLOCK
        gj_out[0:tokens_in, 3 * half :] = halves.astype(BF)
        grad_low = grad_hidden.astype(BF)
        for copy in attn_copies:
            copy.wait()
        own_rows = pl.ds(pl.multiple_of(at * half, 128), half)
        gctx[...] = dot_cols(grad_low, attn[own_rows, :]).astype(BF)
        cos, sin = cosine[BLOCK : 3 * BLOCK, :], sine[BLOCK : 3 * BLOCK, :]
        for i in range(half // 128):
            for part, grad in enumerate(pair_back(i, gctx, q, k, v, p, cos, sin)):
                col = part * half + i * 128
                gj_out[0:tokens_in, col : col + 128] = grad
        for copy in copies:
            copy.wait()
        grad = dot_cols(gj_out[0:tokens_in, 0 : 3 * half], weight[...])
        hat, _ = standardize(tok[BLOCK : 3 * BLOCK, :].astype(F32))
        again = jnp.sum(grad * hat, axis=0, keepdims=True)
        held[...] = grad
        keep_out[...] = held[mine, :]
        send_out[...] = held[theirs, :].astype(BF)
        tail = gj_out.shape[0] - tokens_in
        line = lax.broadcasted_iota(jnp.int32, (tail, width), 0)
        gain_rows = jnp.where(line == 0, again, jnp.where(line == 1, fgain[0:1, :], 0.0))
        gj_out[tokens_in:, 0:width] = gain_rows.astype(BF)
        gj_out[tokens_in:, width:] = jnp.zeros((tail, width), BF)

    return body


def final_kernel(info, tok, keep, other, ghid, gains, out):
    hat, inverse = standardize(tok[...].astype(F32))
    grad = keep[...] + other[...].astype(F32)
    out[...] = (ghid[...] + norm_back(grad, gains[0:1, :], hat, inverse)).astype(BF)


def slots_of(count, chip_bits):
    streams = []
    for order in (chip_bits, chip_bits[::-1]):
        kept = [0]
        for bit in order[1:][::-1]:
            kept = kept + [j | bit for j in kept]
        table = {j: (1, i) for i, j in enumerate(kept)}
        table.update({j | order[0]: (0, i) for i, j in enumerate(kept)})
        streams.append(table)
    return streams


def owner_rows(me, js, lhs_t, rows):
    return jnp.concatenate(
        [lhs_t[pl.ds(pl.multiple_of((me ^ j) * rows, 16), rows), :] for j in js], axis=0
    )


def emit(outs, slots, stream, js, rows, grad, start):
    grad = grad.astype(BF)
    for i, j in enumerate(js):
        kept, at = slots[stream][j]
        for c in range(grad.shape[1] // 128):
            row = start + c * rows
            outs[2 * stream + kept][at, row : row + rows, :] = grad[
                i * rows : (i + 1) * rows, c * 128 : (c + 1) * 128
            ]


def mlp_grad_kernel(js, slots, rows, take, width, units):
    half = width // 2

    def body(info, own, other, dy_own, dy_other, *rest):
        outs, (normed_t, act_t, ggu, dy) = rest[:4], rest[4:]
        me = info[0]
        pair = slice(RADIUS, RADIUS + 2 * BLOCK)
        for i, (ref, dref) in enumerate(((own, dy_own), (other, dy_other))):
            tok = slice(i * 2 * BLOCK, (i + 1) * 2 * BLOCK)
            normed_t[:, tok] = ref[:, 0:width].T
            act_t[:, tok] = ref[:, width : width + units].T
            ggu[tok, :] = ref[:, width + units :]
            dy[tok, :] = dref[pair, :]
        left = owner_rows(me, js, normed_t, rows)
        act = owner_rows(me, js, act_t, take)
        for s in range(2):
            grad = dot(left, ggu[:, s * units : (s + 1) * units])
            emit(outs, slots, s, js, rows, grad, 0)
            grad = dot(act, dy[:, s * half : (s + 1) * half])
            emit(outs, slots, s, js, take, grad, rows * (units // 128))

    return body


def qkv_grad_kernel(js, slots, rows, width):
    half = width // 2

    def body(info, normed_own, normed_other, ctx_own, ctx_other, own, other, *rest):
        outs, (normed_t, ctx_t, gj) = rest[:4], rest[4:]
        me = info[0]
        count = 2 * BLOCK
        each = ((normed_own, ctx_own, own), (normed_other, ctx_other, other))
        for i, (nref, cref, ref) in enumerate(each):
            tok = slice(i * count, (i + 1) * count)
            normed_t[:, tok] = nref[...].T
            ctx_t[:, tok] = cref[...].T
            gj[tok, :] = ref[0:count, :]
        left = owner_rows(me, js, normed_t, rows)
        ctx = owner_rows(me, js, ctx_t, rows)
        emit(outs, slots, 0, js, rows, dot(left, gj[:, 0 : 2 * half]), 0)
        emit(outs, slots, 1, js, rows, dot(left, gj[:, 2 * half : 3 * half]), 0)
        emit(outs, slots, 1, js, rows, dot(ctx, gj[:, 3 * half :]), 3 * rows)
        gains = own[count:, 0:width].astype(F32) + other[count:, 0:width].astype(F32)
        for s in range(2):
            for j in js:
                kept, i = slots[s][j]
                moved = pltpu.roll(gains, lax.rem(width - (me ^ j) * rows, width), 1)
                outs[2 * s + kept][i, 6 * rows : 6 * rows + 16, :] = moved[:, 0:128].astype(BF)

    return body


def mlp_unpack_kernel(rows, down_rows, take, width, units, count):
    hidden = count * down_rows
    spare = 2 * take - down_rows

    def body(info, mine, other, glu, down, held, wide):
        at = info[1]
        held[at] = mine[...].astype(F32)
        held[1 - at] = other[...].astype(F32)
        height = mine.shape[0] // 2
        tiles = units // 128
        for s in range(2):
            for t in range(2):
                for c in range(tiles):
                    row = s * height + c * rows
                    wide[:, c * 128 : (c + 1) * 128] = held[t, row : row + rows, :]
                skip = 0 if t == 0 else spare
                for i in range(count):
                    col = s * hidden + i * down_rows + t * take
                    glu[:, col : col + take - skip] = wide[:, i * take + skip : (i + 1) * take]
                for c in range(width // 256):
                    row = s * height + tiles * rows + c * take
                    col = s * (width // 2) + c * 128
                    down[t * take : (t + 1) * take - skip, col : col + 128] = held[
                        t, row + skip : row + take, :
                    ]

    return body


def qkv_unpack_kernel(rows, width):
    half = width // 2

    def body(info, mine, other, qkv, attn, gains, held):
        at = info[1]
        held[at] = mine[...].astype(F32)
        held[1 - at] = other[...].astype(F32)
        height = mine.shape[0] // 2
        for t in range(2):
            for i in range(3):
                for c in range(half // 128):
                    row = i // 2 * height + (i % 2 * (half // 128) + c) * rows
                    col = i * width + t * half + c * 128
                    qkv[:, col : col + 128] = held[t, row : row + rows, :]
            for c in range(half // 128):
                row = height + (half // 128 + c) * rows
                attn[:, t * half + c * 128 : t * half + (c + 1) * 128] = held[t, row : row + rows, :]
        gains[...] = held[0, 6 * rows : 6 * rows + 8, :] + held[1, 6 * rows : 6 * rows + 8, :]

    return body


def on_device(
    tokens,
    positions,
    qkv_weight,
    attn_weight,
    glu_weight,
    down_weight,
    attn_gain,
    ffn_gain,
    cotangent,
):
    block, width = tokens.shape
    half = width // 2
    rows, down_rows = qkv_weight.shape[0], down_weight.shape[0]
    count, replicas = lax.axis_size("shard"), lax.axis_size("replica")
    everyone = count * replicas
    take = -(-down_rows // 32) * 16
    units = count * take
    me = lax.axis_index("shard").astype(jnp.int32)
    side = lax.axis_index("replica").astype(jnp.int32) & 1
    info = jnp.stack([me, side])
    chip_bits = bits_of(count)[1:]

    gain_cols = jnp.pad(jnp.stack([attn_gain, ffn_gain], axis=1), ((0, 0), (0, 126)))
    own = call(
        pack_qkv_kernel(half),
        shaped((rows, 3 * half + 128), BF),
        (info, qkv_weight, gain_cols),
        [],
        [],
        1_000_000,
        1_000_000,
    )
    qkv_split = (3 * half + 128) // 2
    qkv_parts = gather_pieces(own, qkv_split, chip_bits)

    places = jnp.stack([positions >> 8, positions & 255]).astype(BF)
    places = jnp.pad(places, ((0, 14), (0, width - block)))
    rim = jnp.where(side == 0, cotangent[:RADIUS], cotangent[block - RADIUS :])
    rim = jnp.concatenate([tokens, rim, places], axis=0)
    step = [1 if i & 1 else -1 for i in range(everyone)]
    both = ("shard", "replica")

    def outward(array, length):
        moves = [(i, i + length * step[i]) for i in range(everyone)]
        return lax.ppermute(array, both, [(a, b) for a, b in moves if 0 <= b < everyone])

    near, far = outward(rim, 1), outward(rim, 2)
    partner = xor_send(jnp.concatenate([tokens, cotangent, places], axis=0), "replica", 1)

    own = call(
        pack_mlp_kernel(count, down_rows, take),
        shaped((rows, 2 * width + 2 * units), BF),
        (info, attn_weight, glu_weight, down_weight),
        [],
        [],
        1_000_000,
        2_000_000,
    )
    mlp_parts = gather_pieces(own, width + units, chip_bits)

    tok, dy = call(
        around_kernel,
        (shaped((4 * BLOCK, width), BF), shaped((3 * BLOCK, width), BF)),
        (info, tokens, cotangent, partner, near, far),
        [],
        [],
        1_000_000,
        2_000_000,
    )

    def places_of(packed, row):
        return packed[row, :block].astype(F32) * 256.0 + packed[row + 1, :block].astype(F32)

    mine, theirs = positions.astype(F32), places_of(partner, 2 * block)
    inner, outer = places_of(near, block + RADIUS), places_of(far, block + RADIUS)
    where = jnp.where(
        side == 0,
        jnp.concatenate([inner, mine, theirs, outer]),
        jnp.concatenate([outer, theirs, mine, inner]),
    )
    middle = HEAD // 2
    inverse = THETA_BASE ** (-(jnp.arange(middle, dtype=F32) * 2.0 / HEAD))
    phases = where[:, None] * inverse[None, :]
    cosine, sine = jnp.cos(phases), jnp.sin(phases)
    cosine = jnp.concatenate([cosine] * 4, axis=1)
    sine = jnp.concatenate([-sine, sine, -sine, sine], axis=1)
    offset = (
        jnp.arange(2 * BLOCK, dtype=jnp.int32)[None, :]
        - RADIUS
        - jnp.arange(BLOCK, dtype=jnp.int32)[:, None]
    )
    bias = []
    for b in range(3):
        later_key = where[None, b * BLOCK : (b + 2) * BLOCK] >= offset.astype(F32)
        start = RADIUS + b * BLOCK
        later_query = where[start : start + BLOCK, None] >= -offset.astype(F32)
        allowed = (jnp.abs(offset) <= RADIUS) & jnp.where(offset >= 0, later_key, later_query)
        bias.append(jnp.where(allowed, 0.0, NEGATIVE))
    bias = jnp.concatenate(bias, axis=0).astype(F32)
    unit = jnp.arange(units, dtype=jnp.int32) % take
    mask = jnp.where(unit >= side * (2 * take - down_rows), 1.0, 0.0).astype(F32)
    mask = jnp.broadcast_to(mask, (8, units))

    qkv_parts = with_core(qkv_parts)
    qkv_names = [(j, s) for j, s, _ in qkv_parts]
    qkv_arrays = [a for _, _, a in qkv_parts]
    weight_bytes = width * 3 * width * 2

    q, k, v, p, ctx, normed, gains = call(
        project_kernel(qkv_names, rows, width, qkv_split),
        (
            shaped((3 * BLOCK, half), BF),
            shaped((4 * BLOCK, half), BF),
            shaped((4 * BLOCK, half), BF),
            shaped((3 * half // HEAD, BLOCK, 2 * BLOCK), BF),
            shaped((3 * BLOCK, half), BF),
            shaped((2 * BLOCK, width), BF),
            shaped((8, width), F32),
        ),
        (info, tok, cosine, sine, bias),
        qkv_arrays,
        [
            pltpu.VMEM((width, 3 * half), BF),
            pltpu.VMEM((width, 128), BF),
            pltpu.VMEM((4 * BLOCK, width), BF),
            pltpu.SemaphoreType.DMA((2 * len(qkv_arrays),)),
        ],
        7_000_000_000,
        weight_bytes,
    )
    ctx_other = xor_send(ctx, "replica", 1)
    normed_other = xor_send(normed, "shard", 1)
    dy_other = xor_send(dy, "shard", 1)

    mlp_parts = with_core(mlp_parts, ctx)
    mlp_names = [(j, s) for j, s, _ in mlp_parts]
    mlp_arrays = [a for _, _, a in mlp_parts]
    mix_keep, mix_send, shared, ctx_pair, hidden, gn, fgain = call(
        mlp_kernel(mlp_names, rows, take, width, units),
        (
            shaped((BLOCK, width), F32),
            shaped((BLOCK, width), BF),
            shaped((2 * BLOCK, width + 3 * units), BF),
            shaped((2 * BLOCK, width), BF),
            shaped((3 * BLOCK, width), F32),
            shaped((3 * BLOCK, width), BF),
            shaped((8, width), F32),
        ),
        (info, tok, ctx, ctx_other, dy, gains, mask),
        mlp_arrays,
        [
            pltpu.VMEM((width, width), BF),
            pltpu.VMEM((width, 2 * units), BF),
            pltpu.VMEM((units, width), BF),
            pltpu.VMEM((3 * BLOCK, 2 * units), BF),
            pltpu.VMEM((2 * BLOCK, width), F32),
            pltpu.SemaphoreType.DMA((3 * len(mlp_arrays),)),
        ],
        8_000_000_000,
        2 * weight_bytes,
    )
    gn_other = xor_send(gn, "replica", 1)
    shared_other = xor_send(shared, "shard", 1)
    ctx_pair_other = xor_send(ctx_pair, "shard", 1)

    js = [2 * i for i in range(count // 2)]
    slots = slots_of(count, chip_bits)
    portion = count // 4

    def stack(height):
        return (shaped((portion, height, 128), BF),) * 4

    height = rows * (units // 128) + take * (half // 128)
    sums = call(
        mlp_grad_kernel(js, slots, rows, take, width, units),
        stack(height),
        (info, shared, shared_other, dy, dy_other),
        [],
        [
            pltpu.VMEM((width, 4 * BLOCK), BF),
            pltpu.VMEM((units, 4 * BLOCK), BF),
            pltpu.VMEM((4 * BLOCK, 2 * units), BF),
            pltpu.VMEM((4 * BLOCK, width), BF),
        ],
        4_000_000_000,
        weight_bytes,
    )

    gj, norm_keep, norm_send, ghid = call(
        back_kernel(qkv_names, mlp_names, rows, width, qkv_split),
        (
            shaped((2 * BLOCK + 16, 4 * half), BF),
            shaped((BLOCK, width), F32),
            shaped((BLOCK, width), BF),
            shaped((BLOCK, width), F32),
        ),
        (info, tok, gn, gn_other, hidden, dy, gains, fgain, q, k, v, p, cosine, sine),
        [sums[1]] + qkv_arrays + mlp_arrays,
        [
            pltpu.VMEM((width, 3 * half), BF),
            pltpu.VMEM((width, 128), BF),
            pltpu.VMEM((width, width), BF),
            pltpu.VMEM((3 * BLOCK, half), BF),
            pltpu.VMEM((2 * BLOCK, width), F32),
            pltpu.SemaphoreType.DMA((2 * len(qkv_arrays),)),
            pltpu.SemaphoreType.DMA((len(mlp_arrays),)),
        ],
        9_000_000_000,
        weight_bytes,
    )
    mlp_sums = (
        scatter_sum(sums[0], sums[1], chip_bits, gj),
        scatter_sum(sums[2], sums[3], chip_bits[::-1], gj),
    )
    gj_other = xor_send(gj, "shard", 1)
    sums = call(
        qkv_grad_kernel(js, slots, rows, width),
        stack(6 * rows + 16),
        (info, normed, normed_other, ctx_pair, ctx_pair_other, gj, gj_other),
        [],
        [
            pltpu.VMEM((width, 4 * BLOCK), BF),
            pltpu.VMEM((width, 4 * BLOCK), BF),
            pltpu.VMEM((4 * BLOCK, 4 * half), BF),
        ],
        3_000_000_000,
        weight_bytes,
    )
    qkv_sums = (
        scatter_sum(sums[0], sums[1], chip_bits),
        scatter_sum(sums[2], sums[3], chip_bits[::-1]),
    )
    mlp_total = replica_sum(both_sums(*mlp_sums))
    qkv_total = replica_sum(both_sums(*qkv_sums))

    mix_send, norm_send, _ = lax.optimization_barrier((mix_send, norm_send, gj))
    mix_other = xor_send(mix_send, "replica", 1)
    norm_other = xor_send(norm_send, "replica", 1)
    mixed = (mix_keep + mix_other.astype(F32)).astype(BF)
    grad_tokens = call(
        final_kernel,
        shaped((block, width), BF),
        (info, tokens, norm_keep, norm_other, ghid, gains),
        [],
        [],
        1_000_000,
        1_000_000,
    )
    grad_glu, grad_down = call(
        mlp_unpack_kernel(rows, down_rows, take, width, units, count),
        (shaped((rows, 2 * count * down_rows), F32), shaped((down_rows, width), F32)),
        (info,) + mlp_total,
        [],
        [pltpu.VMEM((2, 2 * height, 128), F32), pltpu.VMEM((rows, units), F32)],
        1_000_000,
        4_000_000,
    )
    grad_qkv, grad_attn, grad_gains = call(
        qkv_unpack_kernel(rows, width),
        (shaped((rows, 3 * width), F32), shaped((rows, width), F32), shaped((8, 128), F32)),
        (info,) + qkv_total,
        [],
        [pltpu.VMEM((2, 2 * (6 * rows + 16), 128), F32)],
        1_000_000,
        4_000_000,
    )
    return (
        mixed,
        grad_tokens,
        grad_qkv,
        grad_attn,
        grad_glu,
        grad_down,
        grad_gains[0, :rows],
        grad_gains[1, :rows],
    )


def solution(mesh):
    in_specs = (
        P(("shard", "replica"), None),
        P(("shard", "replica")),
        P("shard", None),
        P("shard", None),
        P("shard", None),
        P("shard", None),
        P("shard"),
        P("shard"),
        P(("shard", "replica"), None),
    )
    out_specs = (
        P(("shard", "replica"), None),
        P(("shard", "replica"), None),
        P("shard", None),
        P("shard", None),
        P("shard", None),
        P("shard", None),
        P("shard"),
        P("shard"),
    )
    return jax.shard_map(
        on_device, mesh=mesh, in_specs=in_specs, out_specs=out_specs, check_vma=False
    )
```

```python
import math

import jax
import jax.numpy as jnp
from jax import lax
from jax.experimental import pallas as pl
from jax.experimental.pallas import tpu as pltpu
from jax.sharding import PartitionSpec as P

HEAD = 64
RADIUS = 64
BLOCK = 128
EPSILON = 1e-05
THETA_BASE = 10000.0
NEGATIVE = -1e30
VMEM_BYTES = 56 * 1024 * 1024
BF = jnp.bfloat16
F32 = jnp.float32


def xor_send(array, axis, bit):
    count = lax.axis_size(axis)
    return lax.ppermute(array, axis, [(i, i ^ bit) for i in range(count)])


def bits_of(count):
    return [1 << i for i in range(count.bit_length() - 1)]


def gather_pieces(own, split, chip_bits, before):
    if len(chip_bits) == 2:
        x, y = chip_bits
        from_x, from_y = xor_send(own, "shard", x), xor_send(own, "shard", y)
        (from_x, from_y), before = lax.optimization_barrier(((from_x, from_y), before))
        pieces = [(0, 2, own), (x, 2, from_x), (y, 2, from_y)]
        pieces.append((x | y, 0, xor_send(from_x[:, :split], "shard", y)))
        pieces.append((x | y, 1, xor_send(from_y[:, split:], "shard", x)))
    else:
        streams = ([(0, 0, own[:, :split])], [(0, 1, own[:, split:])])
        for stage in range(len(chip_bits)):
            grown = []
            for which, bit in ((0, chip_bits[stage]), (1, chip_bits[-1 - stage])):
                grown.append(
                    [(j ^ bit, s, xor_send(a, "shard", bit)) for j, s, a in streams[which]]
                )
            for held, more in zip(streams, grown):
                held.extend(more)
        pieces = streams[0] + streams[1]
    return pieces, before


def with_core(pieces, after=None):
    rows = pieces[0][2].shape[0]
    arrays = [a for _, _, a in pieces]
    names = [(j, s, i, 0) for i, (j, s, _) in enumerate(pieces)]
    whole = [p for p in pieces if p[1] == 2]
    if whole:
        arrays.append(xor_send(jnp.concatenate([a for _, _, a in whole], axis=0), "shard", 1))
        names += [(p[0] ^ 1, 2, len(arrays) - 1, i * rows) for i, p in enumerate(whole)]
    for j, s, a in pieces[len(whole) :]:
        if after is not None:
            a, _ = lax.optimization_barrier((a, after))
        arrays.append(xor_send(a, "shard", 1))
        names.append((j ^ 1, s, len(arrays) - 1, 0))
    return names, arrays


def add_low(left, right):
    return (left.astype(F32) + right.astype(F32)).astype(BF)


def halve(keep, other):
    middle = keep.shape[0] // 2
    return add_low(keep[middle:], other[middle:]), add_low(keep[:middle], other[:middle])


def scatter_sums(sums, chip_bits, before_add=None, before_last=None):
    send, keep = [sums[0], sums[2]], [sums[1], sums[3]]
    orders = (chip_bits, chip_bits[::-1])
    for step in range(len(chip_bits) - 1):
        others = [xor_send(send[s], "shard", orders[s][step]) for s in range(2)]
        if before_add is not None:
            others, _ = lax.optimization_barrier((others, before_add))
        for s in range(2):
            send[s], keep[s] = halve(keep[s], others[s])
        if before_last is not None:
            send, _ = lax.optimization_barrier((send, before_last))
    return [
        (keep[s], xor_send(send[s], "shard", orders[s][-1]), send[s]) for s in range(2)
    ]


def last_sum(stream):
    keep, other, _ = stream
    return add_low(keep[0], other[0])


def side_sum(total, after=None):
    for bit in bits_of(lax.axis_size("replica"))[1:]:
        other = xor_send(total, "replica", bit)
        if after is not None:
            other, _ = lax.optimization_barrier((other, after))
        total = add_low(total, other)
    return total


def dot(left, right):
    return jnp.dot(left, right, preferred_element_type=F32)


def dot_cols(left, right):
    return lax.dot_general(left, right, (((1,), (1,)), ((), ())), preferred_element_type=F32)


def dot_rows(left, right):
    return lax.dot_general(left, right, (((0,), (0,)), ((), ())), preferred_element_type=F32)


def standardize(vector):
    average = jnp.mean(vector, axis=-1, keepdims=True)
    centred = vector - average
    spread = jnp.mean(centred * centred, axis=-1, keepdims=True)
    inverse = lax.rsqrt(spread + EPSILON)
    return centred * inverse, inverse


def norm_back(grad, gain, hat, inverse):
    dhat = grad * gain
    mean = jnp.mean(dhat, axis=-1, keepdims=True)
    along = jnp.mean(dhat * hat, axis=-1, keepdims=True)
    return (dhat - mean - hat * along) * inverse


def turned(vector):
    width = vector.shape[-1]
    lane = lax.broadcasted_iota(jnp.int32, vector.shape, 1)
    return jnp.where(
        (lane & 63) < 32, pltpu.roll(vector, width - 32, 1), pltpu.roll(vector, 32, 1)
    )


def place(me, pieces, refs, layout, sems):
    copies = []
    for j, stream, which, base in pieces:
        owner = me ^ j
        ref = refs[which]
        for row, rows, col, cols, dst, dst_col in layout[stream]:
            start = owner * rows
            if rows % 16 == 0:
                start = pl.multiple_of(start, 16)
            copy = pltpu.make_async_copy(
                ref.at[pl.ds(base + row, rows), pl.ds(col, cols)],
                dst.at[pl.ds(start, rows), pl.ds(dst_col, cols)],
                sems.at[len(copies)],
            )
            copy.start()
            copies.append(copy)
    return copies


def call(kernel, out_shape, inputs, in_any, scratch, flops, traffic):
    any_spec = pl.BlockSpec(memory_space=pl.ANY)
    vmem = pl.BlockSpec(memory_space=pltpu.VMEM)
    specs = [vmem] * len(inputs) + [any_spec] * len(in_any)
    return pl.pallas_call(
        kernel,
        out_shape=out_shape,
        in_specs=specs,
        out_specs=jax.tree.map(lambda _: vmem, out_shape),
        scratch_shapes=scratch,
        compiler_params=pltpu.CompilerParams(vmem_limit_bytes=VMEM_BYTES),
        cost_estimate=pl.CostEstimate(flops=flops, bytes_accessed=traffic, transcendentals=0),
    )(*inputs, *in_any)


def shard_at():
    return lax.axis_index("shard").astype(jnp.int32)


def side_at():
    return lax.axis_index("replica").astype(jnp.int32) & 1


def shaped(shape, dtype):
    return jax.ShapeDtypeStruct(shape, dtype)


def pack_kernel(count, down_rows, take):
    def body(qkv, attn, glu, down, attn_gain, ffn_gain, out):
        rows, width = attn.shape
        half = width // 2
        units = count * take
        hidden = count * down_rows
        first = 3 * half + 128
        middle = first + width
        last = middle + 2 * units

        def pick(side):
            for i in range(3):
                at = i * width + side * half
                out[:, i * half : (i + 1) * half] = qkv[:, at : at + half]
            skip = side * (down_rows - take)
            for part in range(2):
                for s in range(count):
                    at = part * hidden + s * down_rows + skip
                    to = middle + part * units + s * take
                    out[:, to : to + take] = glu[:, at : at + take]
            out[0:take, last:] = down[skip : skip + take, :]

        @pl.when(side_at() == 0)
        def _():
            pick(0)

        @pl.when(side_at() != 0)
        def _():
            pick(1)

        out[:, first:middle] = attn[...]
        if rows > take:
            out[take:, last:] = jnp.zeros((rows - take, width), BF)
        gains = [ref[...].astype(F32) for ref in (attn_gain, ffn_gain)]
        gains = jnp.concatenate(gains + [jnp.zeros((6, rows), F32)], axis=0)
        gains = jnp.concatenate([gains, jnp.zeros((8, 128 - rows), F32)], axis=1)
        square = jnp.concatenate([gains, jnp.zeros((120, 128), F32)], axis=0)
        out[:, 3 * half : first] = square.T[0:rows, :].astype(BF)

    return body


def around_kernel(own, dy_own, partner, near, far, tok, dy):
    mine = slice(0, BLOCK)

    def arrange(first, first_dy, second, second_dy, before, after):
        tok[0:BLOCK, :] = before[mine, :]
        tok[BLOCK : 2 * BLOCK, :] = first
        tok[2 * BLOCK : 3 * BLOCK, :] = second
        tok[3 * BLOCK :, :] = after[mine, :]
        halo = slice(BLOCK, BLOCK + RADIUS)
        dy[0:RADIUS, :] = before[halo, :]
        dy[RADIUS : RADIUS + BLOCK, :] = first_dy
        dy[RADIUS + BLOCK : RADIUS + 2 * BLOCK, :] = second_dy
        dy[RADIUS + 2 * BLOCK :, :] = after[halo, :]

    other = partner[mine, :]
    other_dy = partner[BLOCK : 2 * BLOCK, :]

    @pl.when(side_at() == 0)
    def _():
        arrange(own[...], dy_own[...], other, other_dy, near, far)

    @pl.when(side_at() != 0)
    def _():
        arrange(other, other_dy, own[...], dy_own[...], far, near)


def qkv_layout(rows, half, weight, gains=None):
    parts = [(0, rows, 0, 3 * half, weight, 0)]
    if gains is not None:
        parts.append((0, rows, 3 * half, 128, gains, 0))
    return (parts, (), parts)


def project_kernel(pieces, n_refs, rows, width):
    half = width // 2
    span = 4 * BLOCK

    def body(tok, cosine, sine, bias, *rest):
        refs, rest = rest[:n_refs], rest[n_refs:]
        q_out, k_out, v_out, p_out, ctx_out, normed_out, gains_out = rest[:7]
        weight, gain_cols, normed, sems = rest[7:]
        layout = qkv_layout(rows, half, weight, gain_cols)
        copies = place(shard_at(), pieces, refs, layout, sems)
        hats = [
            standardize(tok[i * BLOCK : (i + 1) * BLOCK, :].astype(F32))[0] for i in range(4)
        ]
        for copy in copies:
            copy.wait()
        pick = jnp.where(
            lax.broadcasted_iota(jnp.int32, (8, 128), 0)
            == lax.broadcasted_iota(jnp.int32, (8, 128), 1),
            1.0,
            0.0,
        ).astype(BF)
        gains = dot_cols(pick, gain_cols[...])
        gains_out[...] = gains
        for i, hat in enumerate(hats):
            normed[i * BLOCK : (i + 1) * BLOCK, :] = (hat * gains[0:1]).astype(BF)
        normed_out[...] = normed[BLOCK : 3 * BLOCK, :]
        cos3 = jnp.concatenate([cosine[...]] * 3, axis=1)
        sin3 = jnp.concatenate([sine[...]] * 3, axis=1)
        mid = slice(RADIUS, span - RADIUS)
        joined = dot(normed[mid, :], weight[:, 0:half])
        q_out[...] = (joined * cos3[mid] + turned(joined) * sin3[mid]).astype(BF)
        joined = dot(normed[...], weight[:, half : 2 * half])
        k_out[...] = (joined * cos3 + turned(joined) * sin3).astype(BF)
        v_out[...] = dot(normed[...], weight[:, 2 * half : 3 * half]).astype(BF)
        lane = lax.broadcasted_iota(jnp.int32, (BLOCK, 128), 1)
        scale = 1.0 / math.sqrt(HEAD)
        for pair in range(half // 128):
            cols = slice(pair * 128, pair * 128 + 128)
            for b in range(3):
                rows_q = slice(b * BLOCK, (b + 1) * BLOCK)
                rows_k = slice(b * BLOCK, (b + 2) * BLOCK)
                queries, keys, values = q_out[rows_q, cols], k_out[rows_k, cols], v_out[rows_k, cols]
                parts = []
                for h in range(2):
                    mine = (lane < HEAD) if h == 0 else (lane >= HEAD)
                    masked = jnp.where(mine, queries.astype(F32) * scale, 0.0).astype(BF)
                    scores = dot_cols(masked, keys) + bias[rows_q, :]
                    exponent = jnp.exp(scores - jnp.max(scores, axis=1, keepdims=True))
                    total = jnp.sum(exponent, axis=1, keepdims=True)
                    shares = (exponent * (1.0 / total)).astype(BF)
                    p_out[(pair * 2 + h) * 3 + b] = shares
                    parts.append(dot(shares, values))
                ctx_out[rows_q, cols] = jnp.where(lane < HEAD, parts[0], parts[1]).astype(BF)

    return body


def attn_layout(rows, width, attn):
    parts = [(0, rows, 3 * width // 2 + 128, width, attn, 0)]
    return (parts, (), parts)


def mlp_layout(rows, take, width, units, attn, glu, down):
    split = 3 * width // 2 + 128 + width
    first = attn_layout(rows, width, attn)[0]
    streams = [first]
    for start in (0, split):
        parts = [(0, rows, start, 2 * units, glu, 0)]
        parts.append((0, take, start + 2 * units, width, down, 0))
        streams.append(parts if start == 0 else first + parts)
    return streams


def mlp_kernel(pieces, n_refs, rows, down_rows, take, width, units):
    half = width // 2
    pair = slice(RADIUS, RADIUS + 2 * BLOCK)

    def body(tok, ctx_own, ctx_other, dy, gains, *rest):
        refs, rest = rest[2 : n_refs + 2], rest[n_refs + 2 :]
        mix_keep, mix_send, shared, ctx_pair, hidden, gn_out = rest[:6]
        attn, glu, down, ggu, mix, sems = rest[6:]
        layout = mlp_layout(rows, take, width, units, attn, glu, down)
        copies = place(shard_at(), pieces, refs, layout, sems)
        at = side_at()
        inputs = tok[RADIUS : RADIUS + 3 * BLOCK, :].astype(F32)
        own_rows = pl.ds(pl.multiple_of(at * half, 128), half)
        other_rows = pl.ds(pl.multiple_of((1 - at) * half, 128), half)

        @pl.when(at == 0)
        def _():
            ctx_pair[:, 0:half] = ctx_own[pair, :]
            ctx_pair[:, half:] = ctx_other[pair, :]

        @pl.when(at != 0)
        def _():
            ctx_pair[:, 0:half] = ctx_other[pair, :]
            ctx_pair[:, half:] = ctx_own[pair, :]

        for copy in copies:
            copy.wait()
        lifted = dot(ctx_own[...], attn[own_rows, :]) + dot(ctx_other[...], attn[other_rows, :])
        hidden[...] = inputs + lifted
        hat, _ = standardize(hidden[...])
        normed = (hat * gains[1:2, :]).astype(BF)
        shared[:, 0:width] = normed[pair]
        partial = jnp.zeros((2 * BLOCK, width), F32)
        unit = lax.rem(lax.broadcasted_iota(jnp.int32, (1, units), 1), take)
        mask = jnp.where(unit >= at * (2 * take - down_rows), 1.0, 0.0)
        for c in range(0, units, 256):
            wide = min(256, units - c)
            cols = slice(c, c + wide)
            gate = dot(normed, glu[:, cols])
            up = dot(normed, glu[:, units + c : units + c + wide])
            grad_act = dot_cols(dy[...], down[cols, :]) * mask[:, cols]
            share = 0.5 * (1.0 + lax.erf(gate * (1.0 / math.sqrt(2.0))))
            density = jnp.exp(-0.5 * gate * gate) * (1.0 / math.sqrt(2.0 * math.pi))
            gelu = gate * share
            act = (gelu[pair] * up[pair] * mask[:, cols]).astype(BF)
            shared[:, width + c : width + c + wide] = act
            partial = partial + dot(act, down[cols, :])
            ggu[:, cols] = (grad_act * up * (share + gate * density)).astype(BF)
            ggu[:, units + c : units + c + wide] = (grad_act * gelu).astype(BF)
        mix[...] = partial
        mine = pl.ds(pl.multiple_of(at * BLOCK, BLOCK), BLOCK)
        theirs = pl.ds(pl.multiple_of((1 - at) * BLOCK, BLOCK), BLOCK)
        mix_keep[...] = mix[mine, :] + hidden[pl.ds(pl.multiple_of(RADIUS + at * BLOCK, 8), BLOCK), :]
        mix_send[...] = mix[theirs, :].astype(BF)
        shared[:, width + units :] = ggu[pair, :]
        grad = dot_cols(ggu[...], glu[...])
        gn_out[...] = grad.astype(BF)

    return body


def pair_back(pair, gctx, q, k, v, p, cos, sin):
    lane = lax.broadcasted_iota(jnp.int32, (BLOCK, 128), 1)
    lane2 = lax.broadcasted_iota(jnp.int32, (2 * BLOCK, 128), 1)
    scale = 1.0 / math.sqrt(HEAD)
    cols = slice(pair * 128, pair * 128 + 128)
    first, second = slice(0, BLOCK), slice(BLOCK, 2 * BLOCK)
    low, high = slice(0, RADIUS), slice(RADIUS, BLOCK)
    grad_q = jnp.zeros((2 * BLOCK, 128), F32)
    grad_k, grad_v = [0.0, 0.0], [0.0, 0.0]
    for h in range(2):
        mine = (lane < HEAD) if h == 0 else (lane >= HEAD)
        mine2 = (lane2 < HEAD) if h == 0 else (lane2 >= HEAD)
        scores, shares, queries, grads, parts = [], [], [], [], []
        for b in range(3):
            rows_q = slice(b * BLOCK, (b + 1) * BLOCK)
            rows_k = slice(b * BLOCK, (b + 2) * BLOCK)
            keys, values = k[rows_k, cols], v[rows_k, cols]
            lowered = jnp.where(mine, gctx[rows_q, cols].astype(F32), 0.0).astype(BF)
            query = jnp.where(mine, q[rows_q, cols].astype(F32) * scale, 0.0).astype(BF)
            share = p[(pair * 2 + h) * 3 + b]
            wide = share.astype(F32)
            grad_share = dot_cols(lowered, values)
            row = jnp.sum(wide * grad_share, axis=1, keepdims=True)
            grad_score = (wide * (grad_share - row)).astype(BF)
            scores.append(grad_score)
            shares.append(share)
            queries.append(query)
            grads.append(lowered)
            part = (high, first, low)[b]
            parts.append(dot(grad_score[part], keys))
        grad_q = grad_q + jnp.where(mine2, jnp.concatenate(parts, axis=0) * scale, 0.0)
        for i in range(2):
            two = slice(i, i + 2)
            for total, left, right in ((grad_k, scores, queries), (grad_v, shares, grads)):
                upper, lower = left[i][:, second], left[i + 1][:, first]
                total[i] = total[i] + dot_rows(
                    jnp.concatenate([upper, lower], axis=0), jnp.concatenate(right[two], axis=0)
                )
    grad_k, grad_v = jnp.concatenate(grad_k, axis=0), jnp.concatenate(grad_v, axis=0)
    return (
        (grad_q * cos - turned(grad_q) * sin).astype(BF),
        (grad_k * cos - turned(grad_k) * sin).astype(BF),
        grad_v.astype(BF),
    )


def hidden_back_kernel(mlp_pieces, n_mlp, rows, width):
    half = width // 2
    pair = slice(RADIUS, RADIUS + 2 * BLOCK)

    def body(gn_own, gn_other, hidden, dy, gains, q, k, v, p, cosine, sine, *rest):
        mlp_refs, rest = rest[1 : n_mlp + 1], rest[n_mlp + 1 :]
        ghid_out, halves_out, gctx, first_out, attn, held, attn_sems = rest
        copies = place(shard_at(), mlp_pieces, mlp_refs, attn_layout(rows, width, attn), attn_sems)
        at = side_at()
        hat, inverse = standardize(hidden[...])
        grad = gn_own[...].astype(F32) + gn_other[...].astype(F32)
        grad_hidden = dy[...].astype(F32) + norm_back(grad, gains[1:2, :], hat, inverse)
        held[...] = grad_hidden[pair]
        ghid_out[...] = held[pl.ds(pl.multiple_of(at * BLOCK, BLOCK), BLOCK), :]
        halves = jnp.where(at == 0, grad_hidden[pair, 0:half], grad_hidden[pair, half:])
        halves_out[...] = halves.astype(BF)
        grad_low = grad_hidden.astype(BF)
        for copy in copies:
            copy.wait()
        own_rows = pl.ds(pl.multiple_of(at * half, 128), half)
        gctx[...] = dot_cols(grad_low, attn[own_rows, :]).astype(BF)
        cos, sin = cosine[BLOCK : 3 * BLOCK, :], sine[BLOCK : 3 * BLOCK, :]
        for part, grad in enumerate(pair_back(0, gctx, q, k, v, p, cos, sin)):
            first_out[:, part * 128 : (part + 1) * 128] = grad

    return body


def back_kernel(width):
    half = width // 2

    def body(first, halves, gctx, q, k, v, p, cosine, sine, sent_0, sent_1, mixed, gj_out):
        gj_out[:, 3 * half :] = halves[...]
        cos, sin = cosine[BLOCK : 3 * BLOCK, :], sine[BLOCK : 3 * BLOCK, :]
        for part in range(3):
            gj_out[:, part * half : part * half + 128] = first[:, part * 128 : (part + 1) * 128]
        for i in range(1, half // 128):
            for part, grad in enumerate(pair_back(i, gctx, q, k, v, p, cos, sin)):
                col = part * half + i * 128
                gj_out[:, col : col + 128] = grad

    return body


def norm_back_kernel(pieces, n_refs, rows, width):
    half = width // 2

    def body(gj, *rest):
        refs, rest = rest[:n_refs], rest[n_refs:]
        keep_out, send_out, weight, held, sems = rest
        copies = place(shard_at(), pieces, refs, qkv_layout(rows, half, weight), sems)
        at = side_at()
        for copy in copies:
            copy.wait()
        held[...] = dot_cols(gj[:, 0 : 3 * half], weight[...])
        keep_out[...] = held[pl.ds(pl.multiple_of(at * BLOCK, BLOCK), BLOCK), :]
        theirs = pl.ds(pl.multiple_of((1 - at) * BLOCK, BLOCK), BLOCK)
        send_out[...] = held[theirs, :].astype(BF)

    return body


def final_kernel(tok, keep, other, ghid, gains, out):
    hat, inverse = standardize(tok[...].astype(F32))
    grad = keep[...] + other[...].astype(F32)
    out[...] = (ghid[...] + norm_back(grad, gains[0:1, :], hat, inverse)).astype(BF)


def slots_of(count, chip_bits):
    streams = []
    for order in (chip_bits, chip_bits[::-1]):
        kept = [0]
        for bit in order[1:][::-1]:
            kept = kept + [j | bit for j in kept]
        table = {j: (1, i) for i, j in enumerate(kept)}
        table.update({j | order[0]: (0, i) for i, j in enumerate(kept)})
        streams.append(table)
    return streams


def owner_rows(me, js, lhs_t, rows):
    return jnp.concatenate(
        [lhs_t[pl.ds(pl.multiple_of((me ^ j) * rows, 16), rows), :] for j in js], axis=0
    )


def emit(outs, slots, stream, js, rows, grad, start):
    grad = grad.astype(BF)
    for i, j in enumerate(js):
        kept, at = slots[stream][j]
        for c in range(grad.shape[1] // 128):
            row = start + c * rows
            outs[2 * stream + kept][at, row : row + rows, :] = grad[
                i * rows : (i + 1) * rows, c * 128 : (c + 1) * 128
            ]


def mlp_grad_kernel(js, slots, rows, take, width, units):
    half = width // 2

    def body(own, other, dy_own, dy_other, *rest):
        outs, (normed_t, act_t, ggu, dy) = rest[1:5], rest[5:]
        me = shard_at()
        pair = slice(RADIUS, RADIUS + 2 * BLOCK)
        for i, (ref, dref) in enumerate(((own, dy_own), (other, dy_other))):
            tok = slice(i * 2 * BLOCK, (i + 1) * 2 * BLOCK)
            normed_t[:, tok] = ref[:, 0:width].T
            act_t[:, tok] = ref[:, width : width + units].T
            ggu[tok, :] = ref[:, width + units :]
            dy[tok, :] = dref[pair, :]
        left = owner_rows(me, js, normed_t, rows)
        act = owner_rows(me, js, act_t, take)
        for s in range(2):
            grad = dot(left, ggu[:, s * units : (s + 1) * units])
            emit(outs, slots, s, js, rows, grad, 0)
            grad = dot(act, dy[:, s * half : (s + 1) * half])
            emit(outs, slots, s, js, take, grad, rows * (units // 128))

    return body


def qkv_grad_kernel(js, slots, rows, width):
    half = width // 2

    def body(normed_own, normed_other, ctx_own, ctx_other, own, other, *rest):
        outs, (normed_t, ctx_t, gj) = rest[1:5], rest[5:]
        me = shard_at()
        count = 2 * BLOCK
        each = ((normed_own, ctx_own, own), (normed_other, ctx_other, other))
        for i, (nref, cref, ref) in enumerate(each):
            tok = slice(i * count, (i + 1) * count)
            normed_t[:, tok] = nref[...].T
            ctx_t[:, tok] = cref[...].T
            gj[tok, :] = ref[...]
        left = owner_rows(me, js, normed_t, rows)
        ctx = owner_rows(me, js, ctx_t, rows)
        emit(outs, slots, 0, js, rows, dot(left, gj[:, 0 : 2 * half]), 0)
        emit(outs, slots, 1, js, rows, dot(left, gj[:, 2 * half : 3 * half]), 0)
        emit(outs, slots, 1, js, rows, dot(ctx, gj[:, 3 * half :]), 3 * rows)

    return body


def gain_grad(weight, grad, gain):
    total = jnp.sum(weight[...].astype(F32) * grad[...], axis=1, keepdims=True)
    rows = total.shape[0]
    total = jnp.concatenate([total, jnp.zeros((128 - rows, 1), F32)], axis=0)
    return jnp.broadcast_to(total, (128, 128)).T[0:1, 0:rows] / gain[...].astype(F32)


def mlp_unpack_kernel(rows, down_rows, take, width, units, count):
    hidden = count * down_rows
    spare = 2 * take - down_rows

    def body(mine_0, mine_1, other_0, other_1, weight, gain, glu, down, gain_out, held, wide):
        at = side_at()
        tiles = units // 128
        for s, (mine, other) in enumerate(((mine_0, other_0), (mine_1, other_1))):
            held[at, s] = mine[...].astype(F32)
            held[1 - at, s] = other[...].astype(F32)
        for s in range(2):
            for t in range(2):
                for c in range(tiles):
                    row = c * rows
                    wide[:, c * 128 : (c + 1) * 128] = held[t, s, row : row + rows, :]
                skip = 0 if t == 0 else spare
                for i in range(count):
                    col = s * hidden + i * down_rows + t * take
                    glu[:, col : col + take - skip] = wide[:, i * take + skip : (i + 1) * take]
                for c in range(width // 256):
                    row = tiles * rows + c * take
                    col = s * (width // 2) + c * 128
                    down[t * take : (t + 1) * take - skip, col : col + 128] = held[
                        t, s, row + skip : row + take, :
                    ]
        gain_out[...] = gain_grad(weight, glu, gain)

    return body


def qkv_unpack_kernel(rows, width):
    half = width // 2
    tiles = half // 128

    def body(mine_0, mine_1, other_0, other_1, weight, gain, qkv, attn, gain_out, held):
        at = side_at()
        for s, (mine, other) in enumerate(((mine_0, other_0), (mine_1, other_1))):
            held[at, s] = mine[...].astype(F32)
            held[1 - at, s] = other[...].astype(F32)
        for t in range(2):
            for i in range(3):
                for c in range(tiles):
                    row = (i % 2 * tiles + c) * rows
                    col = i * width + t * half + c * 128
                    qkv[:, col : col + 128] = held[t, i // 2, row : row + rows, :]
            for c in range(tiles):
                row = (tiles + c) * rows
                attn[:, t * half + c * 128 : t * half + (c + 1) * 128] = held[t, 1, row : row + rows, :]
        gain_out[...] = gain_grad(weight, qkv, gain)

    return body


def on_device(
    tokens,
    positions,
    qkv_weight,
    attn_weight,
    glu_weight,
    down_weight,
    attn_gain,
    ffn_gain,
    cotangent,
):
    block, width = tokens.shape
    half = width // 2
    rows, down_rows = qkv_weight.shape[0], down_weight.shape[0]
    count, replicas = lax.axis_size("shard"), lax.axis_size("replica")
    everyone = count * replicas
    take = -(-down_rows // 32) * 16
    units = count * take
    me = lax.axis_index("shard").astype(jnp.int32)
    side = lax.axis_index("replica").astype(jnp.int32) & 1
    chip_bits = bits_of(count)[1:]

    own = call(
        pack_kernel(count, down_rows, take),
        shaped((rows, 3 * half + 128 + 2 * width + 2 * units), BF),
        (qkv_weight, attn_weight, glu_weight, down_weight, attn_gain[None], ffn_gain[None]),
        [],
        [],
        1_000_000,
        2_000_000,
    )

    places = jnp.stack([positions >> 8, positions & 255]).astype(BF)
    places = jnp.pad(places, ((0, 14), (0, width - block)))
    rim = jnp.where(side == 0, cotangent[:RADIUS], cotangent[block - RADIUS :])
    rim = jnp.concatenate([tokens, rim, places], axis=0)
    packed = jnp.concatenate([tokens, cotangent, places], axis=0)
    rim, packed, _ = lax.optimization_barrier((rim, packed, own))
    step = [1 if i & 1 else -1 for i in range(everyone)]
    both = ("shard", "replica")

    def outward(array):
        moves = [(i, i + step[i]) for i in range(everyone)]
        return lax.ppermute(array, both, [(a, b) for a, b in moves if 0 <= b < everyone])

    near, partner = outward(rim), xor_send(packed, "replica", 1)
    parts, (near, partner) = gather_pieces(
        own, 3 * half + 128 + width, chip_bits, (near, partner)
    )
    far = xor_send(near, "replica", 1)

    tok, dy = call(
        around_kernel,
        (shaped((4 * BLOCK, width), BF), shaped((3 * BLOCK, width), BF)),
        (tokens, cotangent, partner, near, far),
        [],
        [],
        1_000_000,
        2_000_000,
    )

    def places_of(packed, row):
        return packed[row, :block].astype(F32) * 256.0 + packed[row + 1, :block].astype(F32)

    mine, theirs = positions.astype(F32), places_of(partner, 2 * block)
    inner, outer = places_of(near, block + RADIUS), places_of(far, block + RADIUS)
    where = jnp.where(
        side == 0,
        jnp.concatenate([inner, mine, theirs, outer]),
        jnp.concatenate([outer, theirs, mine, inner]),
    )
    middle = HEAD // 2
    inverse = THETA_BASE ** (-(jnp.arange(middle, dtype=F32) * 2.0 / HEAD))
    phases = where[:, None] * inverse[None, :]
    cosine, sine = jnp.cos(phases), jnp.sin(phases)
    cosine = jnp.concatenate([cosine] * 4, axis=1)
    sine = jnp.concatenate([-sine, sine, -sine, sine], axis=1)
    offset = (
        jnp.arange(2 * BLOCK, dtype=jnp.int32)[None, :]
        - RADIUS
        - jnp.arange(BLOCK, dtype=jnp.int32)[:, None]
    )
    bias = []
    for b in range(3):
        later_key = where[None, b * BLOCK : (b + 2) * BLOCK] >= offset.astype(F32)
        start = RADIUS + b * BLOCK
        later_query = where[start : start + BLOCK, None] >= -offset.astype(F32)
        allowed = (jnp.abs(offset) <= RADIUS) & jnp.where(offset >= 0, later_key, later_query)
        bias.append(jnp.where(allowed, 0.0, NEGATIVE))
    bias = jnp.concatenate(bias, axis=0).astype(F32)
    names, arrays = with_core(parts)
    weight_bytes = width * 3 * width * 2

    q, k, v, p, ctx, normed, gains = call(
        project_kernel(names, len(arrays), rows, width),
        (
            shaped((3 * BLOCK, half), BF),
            shaped((4 * BLOCK, half), BF),
            shaped((4 * BLOCK, half), BF),
            shaped((3 * half // HEAD, BLOCK, 2 * BLOCK), BF),
            shaped((3 * BLOCK, half), BF),
            shaped((2 * BLOCK, width), BF),
            shaped((8, width), F32),
        ),
        (tok, cosine, sine, bias),
        arrays,
        [
            pltpu.VMEM((width, 3 * half), BF),
            pltpu.VMEM((width, 128), BF),
            pltpu.VMEM((4 * BLOCK, width), BF),
            pltpu.SemaphoreType.DMA((2 * len(names),)),
        ],
        7_000_000_000,
        weight_bytes,
    )
    ctx_other = xor_send(ctx, "replica", 1)
    normed_other = xor_send(normed, "shard", 1)
    dy_other = xor_send(dy, "shard", 1)

    mix_keep, mix_send, shared, ctx_pair, hidden, gn = call(
        mlp_kernel(names, len(arrays), rows, down_rows, take, width, units),
        (
            shaped((BLOCK, width), F32),
            shaped((BLOCK, width), BF),
            shaped((2 * BLOCK, width + 3 * units), BF),
            shaped((2 * BLOCK, width), BF),
            shaped((3 * BLOCK, width), F32),
            shaped((3 * BLOCK, width), BF),
        ),
        (tok, ctx, ctx_other, dy, gains),
        [normed_other, dy_other] + arrays,
        [
            pltpu.VMEM((width, width), BF),
            pltpu.VMEM((width, 2 * units), BF),
            pltpu.VMEM((units, width), BF),
            pltpu.VMEM((3 * BLOCK, 2 * units), BF),
            pltpu.VMEM((2 * BLOCK, width), F32),
            pltpu.SemaphoreType.DMA((3 * len(names),)),
        ],
        8_000_000_000,
        2 * weight_bytes,
    )
    gn_other = xor_send(gn, "replica", 1)
    shared_other = xor_send(shared, "shard", 1)
    ctx_pair_other = xor_send(ctx_pair, "shard", 1)

    js = [2 * i for i in range(count // 2)]
    slots = slots_of(count, chip_bits)
    portion = count // 4

    def stack(height):
        return (shaped((portion, height, 128), BF),) * 4

    height = rows * (units // 128) + take * (half // 128)
    sums = call(
        mlp_grad_kernel(js, slots, rows, take, width, units),
        stack(height),
        (shared, shared_other, dy, dy_other),
        [ctx_pair_other],
        [
            pltpu.VMEM((width, 4 * BLOCK), BF),
            pltpu.VMEM((units, 4 * BLOCK), BF),
            pltpu.VMEM((4 * BLOCK, 2 * units), BF),
            pltpu.VMEM((4 * BLOCK, width), BF),
        ],
        4_000_000_000,
        weight_bytes,
    )

    ghid, halves, gctx, gj_first = call(
        hidden_back_kernel(names, len(arrays), rows, width),
        (
            shaped((BLOCK, width), F32),
            shaped((2 * BLOCK, half), BF),
            shaped((3 * BLOCK, half), BF),
            shaped((2 * BLOCK, 3 * 128), BF),
        ),
        (gn, gn_other, hidden, dy, gains, q, k, v, p, cosine, sine),
        [sums[1]] + arrays,
        [
            pltpu.VMEM((width, width), BF),
            pltpu.VMEM((2 * BLOCK, width), F32),
            pltpu.SemaphoreType.DMA((len(names),)),
        ],
        5_000_000_000,
        weight_bytes,
    )
    mlp_sums = scatter_sums(sums, chip_bits, gctx)
    mix_other = xor_send(mix_send, "replica", 1)
    gj = call(
        back_kernel(width),
        shaped((2 * BLOCK, 4 * half), BF),
        (gj_first, halves, gctx, q, k, v, p, cosine, sine),
        [mlp_sums[0][2], mlp_sums[1][2], mix_other],
        [],
        6_000_000_000,
        weight_bytes,
    )
    gj, _ = lax.optimization_barrier((gj, (mlp_sums[0][1], mlp_sums[1][1])))
    mlp_sums = [last_sum(stream) for stream in mlp_sums]
    gj, mlp_sums = lax.optimization_barrier((gj, mlp_sums))
    gj_other = xor_send(gj, "shard", 1)
    norm_keep, norm_send = call(
        norm_back_kernel(names, len(arrays), rows, width),
        (shaped((BLOCK, width), F32), shaped((BLOCK, width), BF)),
        (gj,),
        arrays,
        [
            pltpu.VMEM((width, 3 * half), BF),
            pltpu.VMEM((2 * BLOCK, width), F32),
            pltpu.SemaphoreType.DMA((len(names),)),
        ],
        3_000_000_000,
        weight_bytes,
    )
    sums = call(
        qkv_grad_kernel(js, slots, rows, width),
        stack(6 * rows),
        (normed, normed_other, ctx_pair, ctx_pair_other, gj, gj_other),
        [norm_keep],
        [
            pltpu.VMEM((width, 4 * BLOCK), BF),
            pltpu.VMEM((width, 4 * BLOCK), BF),
            pltpu.VMEM((4 * BLOCK, 4 * half), BF),
        ],
        3_000_000_000,
        weight_bytes,
    )
    mlp_mine = [side_sum(mlp_sums[0], sums[1])]
    qkv_sums = scatter_sums(sums, chip_bits, None, mlp_mine[0])
    mlp_mine.append(side_sum(mlp_sums[1], (qkv_sums[0][2], qkv_sums[1][2])))
    mlp_other = [xor_send(part, "replica", 1) for part in mlp_mine]
    sent = (qkv_sums[0][1], qkv_sums[1][1])
    norm_send, _ = lax.optimization_barrier((norm_send, sums[1]))
    norm_other = xor_send(norm_send, "replica", 1)
    norm_other, mix_other, _ = lax.optimization_barrier((norm_other, mix_other, sent))
    mixed = (mix_keep + mix_other.astype(F32)).astype(BF)
    grad_tokens = call(
        final_kernel,
        shaped((block, width), BF),
        (tokens, norm_keep, norm_other, ghid, gains),
        [],
        [],
        1_000_000,
        1_000_000,
    )
    grad_glu, grad_down, grad_ffn_gain = call(
        mlp_unpack_kernel(rows, down_rows, take, width, units, count),
        (
            shaped((rows, 2 * count * down_rows), F32),
            shaped((down_rows, width), F32),
            shaped((1, rows), F32),
        ),
        (*mlp_mine, *mlp_other, glu_weight, ffn_gain[None]),
        [],
        [pltpu.VMEM((2, 2, height, 128), F32), pltpu.VMEM((rows, units), F32)],
        1_000_000,
        4_000_000,
    )
    done = (mixed, grad_tokens, grad_glu)
    qkv_mine = [side_sum(last_sum(stream), done) for stream in qkv_sums]
    qkv_other = [xor_send(part, "replica", 1) for part in qkv_mine]
    grad_qkv, grad_attn, grad_attn_gain = call(
        qkv_unpack_kernel(rows, width),
        (
            shaped((rows, 3 * width), F32),
            shaped((rows, width), F32),
            shaped((1, rows), F32),
        ),
        (*qkv_mine, *qkv_other, qkv_weight, attn_gain[None]),
        [],
        [pltpu.VMEM((2, 2, 6 * rows, 128), F32)],
        1_000_000,
        4_000_000,
    )
    return (
        mixed,
        grad_tokens,
        grad_qkv,
        grad_attn,
        grad_glu,
        grad_down,
        grad_attn_gain.reshape(rows),
        grad_ffn_gain.reshape(rows),
    )


def solution(mesh):
    in_specs = (
        P(("shard", "replica"), None),
        P(("shard", "replica")),
        P("shard", None),
        P("shard", None),
        P("shard", None),
        P("shard", None),
        P("shard"),
        P("shard"),
        P(("shard", "replica"), None),
    )
    out_specs = (
        P(("shard", "replica"), None),
        P(("shard", "replica"), None),
        P("shard", None),
        P("shard", None),
        P("shard", None),
        P("shard", None),
        P("shard"),
        P("shard"),
    )
    return jax.shard_map(
        on_device, mesh=mesh, in_specs=in_specs, out_specs=out_specs, check_vma=False
    )
```

```python
import math

import jax
import jax.numpy as jnp
from jax import lax
from jax.experimental import pallas as pl
from jax.experimental.pallas import tpu as pltpu
from jax.sharding import PartitionSpec as P

HEAD = 64
RADIUS = 64
BLOCK = 128
EPSILON = 1e-05
THETA_BASE = 10000.0
NEGATIVE = -1e30
VMEM_BYTES = 24 * 1024 * 1024
BF = jnp.bfloat16
F32 = jnp.float32


def xor_send(array, axis, bit):
    count = lax.axis_size(axis)
    return lax.ppermute(array, axis, [(i, i ^ bit) for i in range(count)])


def bits_of(count):
    return [1 << i for i in range(count.bit_length() - 1)]


def gather_pieces(own, split, chip_bits, before=None):
    if len(chip_bits) == 2:
        x, y = chip_bits
        from_x, from_y = xor_send(own, "shard", x), xor_send(own, "shard", y)
        if before is not None:
            (from_x, from_y), _ = lax.optimization_barrier(((from_x, from_y), before))
        pieces = [(0, 2, own), (x, 2, from_x), (y, 2, from_y)]
        forward = [from_x[:, :split], from_y[:, split:]]
        pieces.append((x | y, 0, xor_send(forward[0], "shard", y)))
        pieces.append((x | y, 1, xor_send(forward[1], "shard", x)))
    else:
        streams = ([(0, 0, own[:, :split])], [(0, 1, own[:, split:])])
        for stage in range(len(chip_bits)):
            grown = []
            for which, bit in ((0, chip_bits[stage]), (1, chip_bits[-1 - stage])):
                grown.append(
                    [(j ^ bit, s, xor_send(a, "shard", bit)) for j, s, a in streams[which]]
                )
            for held, more in zip(streams, grown):
                held.extend(more)
        pieces = streams[0] + streams[1]
        forward = []
    return pieces, forward


def with_core(pieces, joined):
    rows = pieces[0][2].shape[0]
    arrays = [a for _, _, a in pieces]
    names = [(j, s, i, 0) for i, (j, s, _) in enumerate(pieces)]
    whole = [p for p in pieces if p[1] == 2]
    others = pieces[len(whole) :]
    if joined and whole:
        whole.append((others[0][0], 2, jnp.concatenate([a for _, _, a in others], axis=1)))
        others = []
    groups = ([whole] if whole else []) + [[p] for p in others]
    for group in groups:
        sent = [a for _, _, a in group]
        sent = jnp.concatenate(sent, axis=0) if len(sent) > 1 else sent[0]
        arrays.append(xor_send(sent, "shard", 1))
        names += [(p[0] ^ 1, p[1], len(arrays) - 1, i * rows) for i, p in enumerate(group)]
    return names, arrays


def add_low(left, right):
    return (left.astype(F32) + right.astype(F32)).astype(BF)


def halve(keep, other):
    middle = keep.shape[0] // 2
    return add_low(keep[middle:], other[middle:]), add_low(keep[:middle], other[:middle])


def scatter_sums(sums, chip_bits, before_add=None, before_last=None):
    send, keep = [sums[0], sums[2]], [sums[1], sums[3]]
    orders = (chip_bits, chip_bits[::-1])
    for step in range(len(chip_bits) - 1):
        others = [xor_send(send[s], "shard", orders[s][step]) for s in range(2)]
        if before_add is not None:
            others, _ = lax.optimization_barrier((others, before_add))
        for s in range(2):
            send[s], keep[s] = halve(keep[s], others[s])
        if before_last is not None:
            send, _ = lax.optimization_barrier((send, before_last))
    return [
        (keep[s], xor_send(send[s], "shard", orders[s][-1]), send[s]) for s in range(2)
    ]


def last_sum(stream):
    keep, other, _ = stream
    return add_low(keep[0], other[0])


def side_sum(total, after=None):
    for bit in bits_of(lax.axis_size("replica"))[1:]:
        other = xor_send(total, "replica", bit)
        if after is not None:
            other, _ = lax.optimization_barrier((other, after))
        total = add_low(total, other)
    return total


def dot(left, right):
    return jnp.dot(left, right, preferred_element_type=F32)


def dot_cols(left, right):
    return lax.dot_general(left, right, (((1,), (1,)), ((), ())), preferred_element_type=F32)


def dot_rows(left, right):
    return lax.dot_general(left, right, (((0,), (0,)), ((), ())), preferred_element_type=F32)


def standardize(vector):
    average = jnp.mean(vector, axis=-1, keepdims=True)
    centred = vector - average
    spread = jnp.mean(centred * centred, axis=-1, keepdims=True)
    inverse = lax.rsqrt(spread + EPSILON)
    return centred * inverse, inverse


def norm_back(grad, gain, hat, inverse):
    dhat = grad * gain
    mean = jnp.mean(dhat, axis=-1, keepdims=True)
    along = jnp.mean(dhat * hat, axis=-1, keepdims=True)
    return (dhat - mean - hat * along) * inverse


def turned(vector):
    width = vector.shape[-1]
    lane = lax.broadcasted_iota(jnp.int32, vector.shape, 1)
    return jnp.where(
        (lane & 63) < 32, pltpu.roll(vector, width - 32, 1), pltpu.roll(vector, 32, 1)
    )


def place(me, pieces, refs, layout, sems):
    copies = []
    for j, stream, which, base in pieces:
        owner = me ^ j
        ref = refs[which]
        for row, rows, col, cols, dst, dst_col in layout[stream]:
            start = owner * rows
            if rows % 16 == 0:
                start = pl.multiple_of(start, 16)
            copy = pltpu.make_async_copy(
                ref.at[pl.ds(base + row, rows), pl.ds(col, cols)],
                dst.at[pl.ds(start, rows), pl.ds(dst_col, cols)],
                sems.at[len(copies)],
            )
            copy.start()
            copies.append(copy)
    return copies


def call(kernel, out_shape, inputs, in_any, scratch, flops, traffic):
    any_spec = pl.BlockSpec(memory_space=pl.ANY)
    vmem = pl.BlockSpec(memory_space=pltpu.VMEM)
    specs = [vmem] * len(inputs) + [any_spec] * len(in_any)
    return pl.pallas_call(
        kernel,
        out_shape=out_shape,
        in_specs=specs,
        out_specs=jax.tree.map(lambda _: vmem, out_shape),
        scratch_shapes=scratch,
        compiler_params=pltpu.CompilerParams(vmem_limit_bytes=VMEM_BYTES),
        cost_estimate=pl.CostEstimate(flops=flops, bytes_accessed=traffic, transcendentals=0),
    )(*inputs, *in_any)


def shard_at():
    return lax.axis_index("shard").astype(jnp.int32)


def side_at():
    return lax.axis_index("replica").astype(jnp.int32) & 1


def shaped(shape, dtype):
    return jax.ShapeDtypeStruct(shape, dtype)


def pack_qkv_kernel(half):
    def body(weight, attn_gain, ffn_gain, out):
        width = 2 * half
        rows = weight.shape[0]

        def pick(first):
            for i in range(3):
                out[:, i * half : (i + 1) * half] = weight[
                    :, i * width + first : i * width + first + half
                ]

        @pl.when(side_at() == 0)
        def _():
            pick(0)

        @pl.when(side_at() != 0)
        def _():
            pick(half)

        gains = [ref[...].astype(F32) for ref in (attn_gain, ffn_gain)]
        gains = jnp.concatenate(gains + [jnp.zeros((6, rows), F32)], axis=0)
        gains = jnp.concatenate([gains, jnp.zeros((8, 128 - rows), F32)], axis=1)
        square = jnp.concatenate([gains, jnp.zeros((120, 128), F32)], axis=0)
        out[:, 3 * half :] = square.T[0:rows, :].astype(BF)

    return body


def pack_mlp_kernel(count, down_rows, take):
    def body(attn, glu, down, out):
        rows, width = attn.shape
        units = count * take
        hidden = count * down_rows
        out[:, 0:width] = attn[...]
        last = width + 2 * units

        def pick(first):
            for part in range(2):
                for s in range(count):
                    at = part * hidden + s * down_rows + first
                    to = width + part * units + s * take
                    out[:, to : to + take] = glu[:, at : at + take]
            out[0:take, last:] = down[first : first + take, :]

        @pl.when(side_at() == 0)
        def _():
            pick(0)

        @pl.when(side_at() != 0)
        def _():
            pick(down_rows - take)

        if rows > take:
            out[take:, last:] = jnp.zeros((rows - take, width), BF)

    return body


def around_kernel(own, places, partner, near, far, out, cosine, sine, bias):
    def arrange(*blocks):
        for i, ref in enumerate(blocks):
            out[i * BLOCK : (i + 1) * BLOCK, :] = ref[0:BLOCK, :]

    @pl.when(side_at() == 0)
    def _():
        arrange(near, own, partner, far)

    @pl.when(side_at() != 0)
    def _():
        arrange(far, partner, own, near)

    def places_of(ref):
        first = ref.shape[0] - 16
        return ref[first : first + 1, 0:BLOCK].astype(F32) * 256.0 + ref[
            first + 1 : first + 2, 0:BLOCK
        ].astype(F32)

    mine, theirs = places[...].astype(F32), places_of(partner)
    inner, outer = places_of(near), places_of(far)
    even = side_at() == 0
    lines = [
        jnp.where(even, inner, outer),
        jnp.where(even, mine, theirs),
        jnp.where(even, theirs, mine),
        jnp.where(even, outer, inner),
    ]
    stacked = jnp.concatenate([jnp.broadcast_to(line, (BLOCK, BLOCK)).T for line in lines], axis=0)
    lane = lax.broadcasted_iota(jnp.int32, (1, 128), 1)
    power = lax.rem(lane, HEAD // 2).astype(F32) * (2.0 / HEAD)
    phases = stacked * jnp.exp(power * -math.log(THETA_BASE))
    cosine[...] = jnp.cos(phases)
    sine[...] = jnp.where((lane & 63) < 32, -1.0, 1.0) * jnp.sin(phases)
    offset = (
        lax.broadcasted_iota(jnp.int32, (BLOCK, 2 * BLOCK), 1)
        - RADIUS
        - lax.broadcasted_iota(jnp.int32, (BLOCK, 2 * BLOCK), 0)
    )
    distance = offset.astype(F32)
    for b in range(3):
        start = RADIUS + b * BLOCK
        key = jnp.concatenate([lines[b], lines[b + 1]], axis=1)
        query = jnp.concatenate([stacked[start : start + BLOCK, :]] * 2, axis=1)
        later = jnp.where(offset >= 0, key - distance, query + distance)
        allowed = (jnp.abs(offset) <= RADIUS) & (later >= 0.0)
        bias[b * BLOCK : (b + 1) * BLOCK, :] = jnp.where(allowed, 0.0, NEGATIVE)


def around_back_kernel(own, partner, near, far, out):
    def arrange(before, first, second, after):
        out[0:RADIUS, :] = before[...]
        out[RADIUS : RADIUS + BLOCK, :] = first
        out[RADIUS + BLOCK : RADIUS + 2 * BLOCK, :] = second
        out[RADIUS + 2 * BLOCK :, :] = after[...]

    theirs = partner[...]

    @pl.when(side_at() == 0)
    def _():
        arrange(near, own[...], theirs, far)

    @pl.when(side_at() != 0)
    def _():
        arrange(far, theirs, own[...], near)


def qkv_layout(rows, half, weight, gains=None):
    wide = 3 * half
    split = (wide + 128) // 2
    streams = [[(0, rows, 0, split, weight, 0)], [(0, rows, 0, wide - split, weight, split)]]
    streams.append([(0, rows, 0, wide, weight, 0)])
    if gains is not None:
        streams[1].append((0, rows, wide - split, 128, gains, 0))
        streams[2].append((0, rows, wide, 128, gains, 0))
    return streams


def project_kernel(pieces, n_refs, rows, width, skip):
    half = width // 2
    span = 4 * BLOCK

    def body(tok, cosine, sine, bias, *rest):
        refs, rest = rest[skip : n_refs + skip], rest[n_refs + skip :]
        q_out, k_out, v_out, p_out, ctx_out, normed_out, gains_out = rest[:7]
        weight, gain_cols, normed, sems = rest[7:]
        layout = qkv_layout(rows, half, weight, gain_cols)
        copies = place(shard_at(), pieces, refs, layout, sems)
        hats = [
            standardize(tok[i * BLOCK : (i + 1) * BLOCK, :].astype(F32))[0] for i in range(4)
        ]
        for copy in copies:
            copy.wait()
        pick = jnp.where(
            lax.broadcasted_iota(jnp.int32, (8, 128), 0)
            == lax.broadcasted_iota(jnp.int32, (8, 128), 1),
            1.0,
            0.0,
        ).astype(BF)
        gains = dot_cols(pick, gain_cols[...])
        gains_out[...] = gains
        for i, hat in enumerate(hats):
            normed[i * BLOCK : (i + 1) * BLOCK, :] = (hat * gains[0:1]).astype(BF)
        normed_out[...] = normed[BLOCK : 3 * BLOCK, :]
        cos3 = jnp.concatenate([cosine[...]] * 3, axis=1)
        sin3 = jnp.concatenate([sine[...]] * 3, axis=1)
        mid = slice(RADIUS, span - RADIUS)
        joined = dot(normed[mid, :], weight[:, 0:half])
        q_out[...] = (joined * cos3[mid] + turned(joined) * sin3[mid]).astype(BF)
        joined = dot(normed[...], weight[:, half : 2 * half])
        k_out[...] = (joined * cos3 + turned(joined) * sin3).astype(BF)
        v_out[...] = dot(normed[...], weight[:, 2 * half : 3 * half]).astype(BF)
        lane = lax.broadcasted_iota(jnp.int32, (BLOCK, 128), 1)
        scale = 1.0 / math.sqrt(HEAD)
        for pair in range(half // 128):
            cols = slice(pair * 128, pair * 128 + 128)
            for b in range(3):
                rows_q = slice(b * BLOCK, (b + 1) * BLOCK)
                rows_k = slice(b * BLOCK, (b + 2) * BLOCK)
                queries, keys, values = q_out[rows_q, cols], k_out[rows_k, cols], v_out[rows_k, cols]
                parts = []
                for h in range(2):
                    mine = (lane < HEAD) if h == 0 else (lane >= HEAD)
                    masked = jnp.where(mine, queries.astype(F32) * scale, 0.0).astype(BF)
                    scores = dot_cols(masked, keys) + bias[rows_q, :]
                    exponent = jnp.exp(scores - jnp.max(scores, axis=1, keepdims=True))
                    total = jnp.sum(exponent, axis=1, keepdims=True)
                    shares = (exponent * (1.0 / total)).astype(BF)
                    p_out[(pair * 2 + h) * 3 + b] = shares
                    parts.append(dot(shares, values))
                ctx_out[rows_q, cols] = jnp.where(lane < HEAD, parts[0], parts[1]).astype(BF)

    return body


def attn_layout(rows, width, attn):
    parts = [(0, rows, 0, width, attn, 0)]
    return (parts, (), parts)


def mlp_layout(rows, take, width, units, attn, glu, down):
    one = (0, rows, 0, width, attn, 0)
    gate = (0, rows, width, units, glu, 0)
    up = (0, rows, 0, units, glu, units)
    low = (0, take, units, width, down, 0)
    whole = (one, (0, rows, width, 2 * units, glu, 0), (0, take, width + 2 * units, width, down, 0))
    return ((one, gate), (up, low), whole)


def mlp_kernel(pieces, n_refs, rows, down_rows, take, width, units):
    half = width // 2
    pair = slice(RADIUS, RADIUS + 2 * BLOCK)

    def body(tok, ctx_own, ctx_other, dy, gains, *rest):
        refs, rest = rest[1 : n_refs + 1], rest[n_refs + 1 :]
        mix_keep, mix_send, shared, ctx_pair, hidden, gn_out = rest[:6]
        attn, glu, down, ggu, mix, sems = rest[6:]
        layout = mlp_layout(rows, take, width, units, attn, glu, down)
        copies = place(shard_at(), pieces, refs, layout, sems)
        at = side_at()
        inputs = tok[RADIUS : RADIUS + 3 * BLOCK, :].astype(F32)
        own_rows = pl.ds(pl.multiple_of(at * half, 128), half)
        other_rows = pl.ds(pl.multiple_of((1 - at) * half, 128), half)

        @pl.when(at == 0)
        def _():
            ctx_pair[:, 0:half] = ctx_own[pair, :]
            ctx_pair[:, half:] = ctx_other[pair, :]

        @pl.when(at != 0)
        def _():
            ctx_pair[:, 0:half] = ctx_other[pair, :]
            ctx_pair[:, half:] = ctx_own[pair, :]

        for copy in copies:
            copy.wait()
        lifted = dot(ctx_own[...], attn[own_rows, :]) + dot(ctx_other[...], attn[other_rows, :])
        hidden[...] = inputs + lifted
        hat, _ = standardize(hidden[...])
        normed = (hat * gains[1:2, :]).astype(BF)
        shared[:, 0:width] = normed[pair]
        partial = jnp.zeros((2 * BLOCK, width), F32)
        unit = lax.rem(lax.broadcasted_iota(jnp.int32, (1, units), 1), take)
        mask = jnp.where(unit >= at * (2 * take - down_rows), 1.0, 0.0)
        for c in range(0, units, 256):
            wide = min(256, units - c)
            cols = slice(c, c + wide)
            gate = dot(normed, glu[:, cols])
            up = dot(normed, glu[:, units + c : units + c + wide])
            grad_act = dot_cols(dy[...], down[cols, :]) * mask[:, cols]
            share = 0.5 * (1.0 + lax.erf(gate * (1.0 / math.sqrt(2.0))))
            density = jnp.exp(-0.5 * gate * gate) * (1.0 / math.sqrt(2.0 * math.pi))
            gelu = gate * share
            act = (gelu[pair] * up[pair] * mask[:, cols]).astype(BF)
            shared[:, width + c : width + c + wide] = act
            partial = partial + dot(act, down[cols, :])
            ggu[:, cols] = (grad_act * up * (share + gate * density)).astype(BF)
            ggu[:, units + c : units + c + wide] = (grad_act * gelu).astype(BF)
        mix[...] = partial
        mine = pl.ds(pl.multiple_of(at * BLOCK, BLOCK), BLOCK)
        theirs = pl.ds(pl.multiple_of((1 - at) * BLOCK, BLOCK), BLOCK)
        mix_keep[...] = mix[mine, :] + hidden[pl.ds(pl.multiple_of(RADIUS + at * BLOCK, 8), BLOCK), :]
        mix_send[...] = mix[theirs, :].astype(BF)
        shared[:, width + units :] = ggu[pair, :]
        grad = dot_cols(ggu[...], glu[...])
        gn_out[...] = grad.astype(BF)

    return body


def pair_back(pair, gctx, q, k, v, p, cos, sin):
    lane = lax.broadcasted_iota(jnp.int32, (BLOCK, 128), 1)
    lane2 = lax.broadcasted_iota(jnp.int32, (2 * BLOCK, 128), 1)
    scale = 1.0 / math.sqrt(HEAD)
    cols = slice(pair * 128, pair * 128 + 128)
    first, second = slice(0, BLOCK), slice(BLOCK, 2 * BLOCK)
    low, high = slice(0, RADIUS), slice(RADIUS, BLOCK)
    grad_q = jnp.zeros((2 * BLOCK, 128), F32)
    grad_k, grad_v = [0.0, 0.0], [0.0, 0.0]
    for h in range(2):
        mine = (lane < HEAD) if h == 0 else (lane >= HEAD)
        mine2 = (lane2 < HEAD) if h == 0 else (lane2 >= HEAD)
        scores, shares, queries, grads, parts = [], [], [], [], []
        for b in range(3):
            rows_q = slice(b * BLOCK, (b + 1) * BLOCK)
            rows_k = slice(b * BLOCK, (b + 2) * BLOCK)
            keys, values = k[rows_k, cols], v[rows_k, cols]
            lowered = jnp.where(mine, gctx[rows_q, cols].astype(F32), 0.0).astype(BF)
            query = jnp.where(mine, q[rows_q, cols].astype(F32) * scale, 0.0).astype(BF)
            share = p[(pair * 2 + h) * 3 + b]
            wide = share.astype(F32)
            grad_share = dot_cols(lowered, values)
            row = jnp.sum(wide * grad_share, axis=1, keepdims=True)
            grad_score = (wide * (grad_share - row)).astype(BF)
            scores.append(grad_score)
            shares.append(share)
            queries.append(query)
            grads.append(lowered)
            part = (high, first, low)[b]
            parts.append(dot(grad_score[part], keys))
        grad_q = grad_q + jnp.where(mine2, jnp.concatenate(parts, axis=0) * scale, 0.0)
        for i in range(2):
            two = slice(i, i + 2)
            for total, left, right in ((grad_k, scores, queries), (grad_v, shares, grads)):
                upper, lower = left[i][:, second], left[i + 1][:, first]
                total[i] = total[i] + dot_rows(
                    jnp.concatenate([upper, lower], axis=0), jnp.concatenate(right[two], axis=0)
                )
    grad_k, grad_v = jnp.concatenate(grad_k, axis=0), jnp.concatenate(grad_v, axis=0)
    return (
        (grad_q * cos - turned(grad_q) * sin).astype(BF),
        (grad_k * cos - turned(grad_k) * sin).astype(BF),
        grad_v.astype(BF),
    )


def hidden_back_kernel(mlp_pieces, n_mlp, rows, width):
    half = width // 2
    pair = slice(RADIUS, RADIUS + 2 * BLOCK)

    def body(gn_own, gn_other, hidden, dy, gains, q, k, v, p, cosine, sine, *rest):
        mlp_refs, rest = rest[1 : n_mlp + 1], rest[n_mlp + 1 :]
        ghid_out, halves_out, gctx, first_out, attn, held, attn_sems = rest
        copies = place(shard_at(), mlp_pieces, mlp_refs, attn_layout(rows, width, attn), attn_sems)
        at = side_at()
        hat, inverse = standardize(hidden[...])
        grad = gn_own[...].astype(F32) + gn_other[...].astype(F32)
        grad_hidden = dy[...].astype(F32) + norm_back(grad, gains[1:2, :], hat, inverse)
        held[...] = grad_hidden[pair]
        ghid_out[...] = held[pl.ds(pl.multiple_of(at * BLOCK, BLOCK), BLOCK), :]
        halves = jnp.where(at == 0, grad_hidden[pair, 0:half], grad_hidden[pair, half:])
        halves_out[...] = halves.astype(BF)
        grad_low = grad_hidden.astype(BF)
        for copy in copies:
            copy.wait()
        own_rows = pl.ds(pl.multiple_of(at * half, 128), half)
        gctx[...] = dot_cols(grad_low, attn[own_rows, :]).astype(BF)
        cos, sin = cosine[BLOCK : 3 * BLOCK, :], sine[BLOCK : 3 * BLOCK, :]
        for part, grad in enumerate(pair_back(0, gctx, q, k, v, p, cos, sin)):
            first_out[:, part * 128 : (part + 1) * 128] = grad

    return body


def back_kernel(width):
    half = width // 2

    def body(first, halves, gctx, q, k, v, p, cosine, sine, sent_0, sent_1, mixed, gj_out):
        gj_out[:, 3 * half :] = halves[...]
        cos, sin = cosine[BLOCK : 3 * BLOCK, :], sine[BLOCK : 3 * BLOCK, :]
        for part in range(3):
            gj_out[:, part * half : part * half + 128] = first[:, part * 128 : (part + 1) * 128]
        for i in range(1, half // 128):
            for part, grad in enumerate(pair_back(i, gctx, q, k, v, p, cos, sin)):
                col = part * half + i * 128
                gj_out[:, col : col + 128] = grad

    return body


def norm_back_kernel(pieces, n_refs, rows, width):
    half = width // 2

    def body(gj, *rest):
        refs, rest = rest[:n_refs], rest[n_refs:]
        keep_out, send_out, weight, held, sems = rest
        copies = place(shard_at(), pieces, refs, qkv_layout(rows, half, weight), sems)
        at = side_at()
        for copy in copies:
            copy.wait()
        held[...] = dot_cols(gj[:, 0 : 3 * half], weight[...])
        keep_out[...] = held[pl.ds(pl.multiple_of(at * BLOCK, BLOCK), BLOCK), :]
        theirs = pl.ds(pl.multiple_of((1 - at) * BLOCK, BLOCK), BLOCK)
        send_out[...] = held[theirs, :].astype(BF)

    return body


def final_kernel(tok, keep, other, ghid, gains, out):
    hat, inverse = standardize(tok[...].astype(F32))
    grad = keep[...] + other[...].astype(F32)
    out[...] = (ghid[...] + norm_back(grad, gains[0:1, :], hat, inverse)).astype(BF)


def slots_of(count, chip_bits):
    streams = []
    for order in (chip_bits, chip_bits[::-1]):
        kept = [0]
        for bit in order[1:][::-1]:
            kept = kept + [j | bit for j in kept]
        table = {j: (1, i) for i, j in enumerate(kept)}
        table.update({j | order[0]: (0, i) for i, j in enumerate(kept)})
        streams.append(table)
    return streams


def owner_rows(me, js, lhs_t, rows):
    return jnp.concatenate(
        [lhs_t[pl.ds(pl.multiple_of((me ^ j) * rows, 16), rows), :] for j in js], axis=0
    )


def emit(outs, slots, stream, js, rows, grad, start):
    grad = grad.astype(BF)
    for i, j in enumerate(js):
        kept, at = slots[stream][j]
        for c in range(grad.shape[1] // 128):
            row = start + c * rows
            outs[2 * stream + kept][at, row : row + rows, :] = grad[
                i * rows : (i + 1) * rows, c * 128 : (c + 1) * 128
            ]


def mlp_grad_kernel(js, slots, rows, take, width, units):
    half = width // 2

    def body(own, other, dy_own, dy_other, *rest):
        outs, (normed_t, act_t, ggu, dy) = rest[1:5], rest[5:]
        me = shard_at()
        pair = slice(RADIUS, RADIUS + 2 * BLOCK)
        for i, (ref, dref) in enumerate(((own, dy_own), (other, dy_other))):
            tok = slice(i * 2 * BLOCK, (i + 1) * 2 * BLOCK)
            normed_t[:, tok] = ref[:, 0:width].T
            act_t[:, tok] = ref[:, width : width + units].T
            ggu[tok, :] = ref[:, width + units :]
            dy[tok, :] = dref[pair, :]
        left = owner_rows(me, js, normed_t, rows)
        act = owner_rows(me, js, act_t, take)
        for s in range(2):
            grad = dot(left, ggu[:, s * units : (s + 1) * units])
            emit(outs, slots, s, js, rows, grad, 0)
            grad = dot(act, dy[:, s * half : (s + 1) * half])
            emit(outs, slots, s, js, take, grad, rows * (units // 128))

    return body


def qkv_grad_kernel(js, slots, rows, width):
    half = width // 2

    def body(normed_own, normed_other, ctx_own, ctx_other, own, other, *rest):
        outs, (normed_t, ctx_t, gj) = rest[1:5], rest[5:]
        me = shard_at()
        count = 2 * BLOCK
        each = ((normed_own, ctx_own, own), (normed_other, ctx_other, other))
        for i, (nref, cref, ref) in enumerate(each):
            tok = slice(i * count, (i + 1) * count)
            normed_t[:, tok] = nref[...].T
            ctx_t[:, tok] = cref[...].T
            gj[tok, :] = ref[...]
        left = owner_rows(me, js, normed_t, rows)
        ctx = owner_rows(me, js, ctx_t, rows)
        emit(outs, slots, 0, js, rows, dot(left, gj[:, 0 : 2 * half]), 0)
        emit(outs, slots, 1, js, rows, dot(left, gj[:, 2 * half : 3 * half]), 0)
        emit(outs, slots, 1, js, rows, dot(ctx, gj[:, 3 * half :]), 3 * rows)

    return body


def gain_grad(weight, grad, gain):
    total = jnp.sum(weight[...].astype(F32) * grad[...], axis=1, keepdims=True)
    rows = total.shape[0]
    total = jnp.concatenate([total, jnp.zeros((128 - rows, 1), F32)], axis=0)
    return jnp.broadcast_to(total, (128, 128)).T[0:1, 0:rows] / gain[...].astype(F32)


def mlp_unpack_kernel(rows, down_rows, take, width, units, count):
    hidden = count * down_rows
    spare = 2 * take - down_rows

    def body(mine_0, mine_1, other_0, other_1, weight, gain, glu, down, gain_out, held, wide):
        at = side_at()
        tiles = units // 128
        for s, (mine, other) in enumerate(((mine_0, other_0), (mine_1, other_1))):
            held[at, s] = mine[...].astype(F32)
            held[1 - at, s] = other[...].astype(F32)
        for s in range(2):
            for t in range(2):
                for c in range(tiles):
                    row = c * rows
                    wide[:, c * 128 : (c + 1) * 128] = held[t, s, row : row + rows, :]
                skip = 0 if t == 0 else spare
                for i in range(count):
                    col = s * hidden + i * down_rows + t * take
                    glu[:, col : col + take - skip] = wide[:, i * take + skip : (i + 1) * take]
                for c in range(width // 256):
                    row = tiles * rows + c * take
                    col = s * (width // 2) + c * 128
                    down[t * take : (t + 1) * take - skip, col : col + 128] = held[
                        t, s, row + skip : row + take, :
                    ]
        gain_out[...] = gain_grad(weight, glu, gain)

    return body


def qkv_unpack_kernel(rows, width):
    half = width // 2
    tiles = half // 128

    def body(mine_0, mine_1, other_0, other_1, weight, gain, qkv, attn, gain_out, held):
        at = side_at()
        for s, (mine, other) in enumerate(((mine_0, other_0), (mine_1, other_1))):
            held[at, s] = mine[...].astype(F32)
            held[1 - at, s] = other[...].astype(F32)
        for t in range(2):
            for i in range(3):
                for c in range(tiles):
                    row = (i % 2 * tiles + c) * rows
                    col = i * width + t * half + c * 128
                    qkv[:, col : col + 128] = held[t, i // 2, row : row + rows, :]
            for c in range(tiles):
                row = (tiles + c) * rows
                attn[:, t * half + c * 128 : t * half + (c + 1) * 128] = held[t, 1, row : row + rows, :]
        gain_out[...] = gain_grad(weight, qkv, gain)

    return body


def on_device(
    tokens,
    positions,
    qkv_weight,
    attn_weight,
    glu_weight,
    down_weight,
    attn_gain,
    ffn_gain,
    cotangent,
):
    block, width = tokens.shape
    half = width // 2
    rows, down_rows = qkv_weight.shape[0], down_weight.shape[0]
    count, replicas = lax.axis_size("shard"), lax.axis_size("replica")
    everyone = count * replicas
    take = -(-down_rows // 32) * 16
    units = count * take
    me = lax.axis_index("shard").astype(jnp.int32)
    side = lax.axis_index("replica").astype(jnp.int32) & 1
    chip_bits = bits_of(count)[1:]

    own = call(
        pack_qkv_kernel(half),
        shaped((rows, 3 * half + 128), BF),
        (qkv_weight, attn_gain[None], ffn_gain[None]),
        [],
        [],
        1_000_000,
        1_000_000,
    )

    places = jnp.stack([positions >> 8, positions & 255]).astype(BF)
    places = jnp.pad(places, ((0, 14), (0, width - block)))
    rim = jnp.concatenate([tokens, places], axis=0)
    rim, _ = lax.optimization_barrier((rim, own))
    step = [1 if i & 1 else -1 for i in range(everyone)]
    both = ("shard", "replica")

    def outward(array):
        moves = [(i, i + step[i]) for i in range(everyone)]
        return lax.ppermute(array, both, [(a, b) for a, b in moves if 0 <= b < everyone])

    own_mlp = call(
        pack_mlp_kernel(count, down_rows, take),
        shaped((rows, 2 * width + 2 * units), BF),
        (attn_weight, glu_weight, down_weight),
        [],
        [],
        1_000_000,
        2_000_000,
    )
    qkv_parts, _ = gather_pieces(
        own, (3 * half + 128) // 2, chip_bits, rim
    )
    near, partner = outward(rim), xor_send(rim, "replica", 1)
    arrived = [a for _, _, a in qkv_parts]
    own, near, partner, arrived = lax.optimization_barrier((own_mlp, near, partner, arrived))
    qkv_parts = [(j, s, a) for (j, s, _), a in zip(qkv_parts, arrived)]
    far = xor_send(near, "replica", 1)
    mlp_parts, forward = gather_pieces(own, width + units, chip_bits)

    tok, cosine, sine, bias = call(
        around_kernel,
        (
            shaped((4 * BLOCK, width), BF),
            shaped((4 * BLOCK, 128), F32),
            shaped((4 * BLOCK, 128), F32),
            shaped((3 * BLOCK, 2 * BLOCK), F32),
        ),
        (tokens, positions[None], partner, near, far),
        [],
        [],
        1_000_000,
        2_000_000,
    )
    rim = jnp.where(side == 0, cotangent[:RADIUS], cotangent[block - RADIUS :])
    rim, _ = lax.optimization_barrier((rim, near))
    near_dy = outward(rim)
    sent, near_dy = lax.optimization_barrier((cotangent, near_dy))
    partner_dy = xor_send(sent, "replica", 1)
    far_dy = xor_send(near_dy, "replica", 1)
    qkv_names, qkv_arrays = with_core(qkv_parts, True)
    weight_bytes = width * 3 * width * 2

    q, k, v, p, ctx, normed, gains = call(
        project_kernel(qkv_names, len(qkv_arrays), rows, width, 2 + len(forward)),
        (
            shaped((3 * BLOCK, half), BF),
            shaped((4 * BLOCK, half), BF),
            shaped((4 * BLOCK, half), BF),
            shaped((3 * half // HEAD, BLOCK, 2 * BLOCK), BF),
            shaped((3 * BLOCK, half), BF),
            shaped((2 * BLOCK, width), BF),
            shaped((8, width), F32),
        ),
        (tok, cosine, sine, bias),
        [far_dy, partner_dy] + forward + qkv_arrays,
        [
            pltpu.VMEM((width, 3 * half), BF),
            pltpu.VMEM((width, 128), BF),
            pltpu.VMEM((4 * BLOCK, width), BF),
            pltpu.SemaphoreType.DMA((2 * len(qkv_names),)),
        ],
        7_000_000_000,
        weight_bytes,
    )
    ctx_other = xor_send(ctx, "replica", 1)
    normed_other = xor_send(normed, "shard", 1)
    near_dy, far_dy, partner_dy, _ = lax.optimization_barrier(
        (near_dy, far_dy, partner_dy, ctx)
    )
    dy = call(
        around_back_kernel,
        shaped((3 * BLOCK, width), BF),
        (cotangent, partner_dy, near_dy, far_dy),
        [],
        [],
        1_000_000,
        2_000_000,
    )
    dy_other = xor_send(dy, "shard", 1)
    held, _ = lax.optimization_barrier(([a for _, _, a in mlp_parts], ctx))
    mlp_parts = [(j, s, a) for (j, s, _), a in zip(mlp_parts, held)]
    names, arrays = with_core(mlp_parts, False)

    mix_keep, mix_send, shared, ctx_pair, hidden, gn = call(
        mlp_kernel(names, len(arrays), rows, down_rows, take, width, units),
        (
            shaped((BLOCK, width), F32),
            shaped((BLOCK, width), BF),
            shaped((2 * BLOCK, width + 3 * units), BF),
            shaped((2 * BLOCK, width), BF),
            shaped((3 * BLOCK, width), F32),
            shaped((3 * BLOCK, width), BF),
        ),
        (tok, ctx, ctx_other, dy, gains),
        [normed_other] + arrays,
        [
            pltpu.VMEM((width, width), BF),
            pltpu.VMEM((width, 2 * units), BF),
            pltpu.VMEM((units, width), BF),
            pltpu.VMEM((3 * BLOCK, 2 * units), BF),
            pltpu.VMEM((2 * BLOCK, width), F32),
            pltpu.SemaphoreType.DMA((3 * len(names),)),
        ],
        8_000_000_000,
        2 * weight_bytes,
    )
    gn_other = xor_send(gn, "replica", 1)
    shared_other = xor_send(shared, "shard", 1)
    ctx_pair_other = xor_send(ctx_pair, "shard", 1)

    js = [2 * i for i in range(count // 2)]
    slots = slots_of(count, chip_bits)
    portion = count // 4

    def stack(height):
        return (shaped((portion, height, 128), BF),) * 4

    height = rows * (units // 128) + take * (half // 128)
    sums = call(
        mlp_grad_kernel(js, slots, rows, take, width, units),
        stack(height),
        (shared, shared_other, dy, dy_other),
        [ctx_pair_other],
        [
            pltpu.VMEM((width, 4 * BLOCK), BF),
            pltpu.VMEM((units, 4 * BLOCK), BF),
            pltpu.VMEM((4 * BLOCK, 2 * units), BF),
            pltpu.VMEM((4 * BLOCK, width), BF),
        ],
        4_000_000_000,
        weight_bytes,
    )

    ghid, halves, gctx, gj_first = call(
        hidden_back_kernel(names, len(arrays), rows, width),
        (
            shaped((BLOCK, width), F32),
            shaped((2 * BLOCK, half), BF),
            shaped((3 * BLOCK, half), BF),
            shaped((2 * BLOCK, 3 * 128), BF),
        ),
        (gn, gn_other, hidden, dy, gains, q, k, v, p, cosine, sine),
        [sums[1]] + arrays,
        [
            pltpu.VMEM((width, width), BF),
            pltpu.VMEM((2 * BLOCK, width), F32),
            pltpu.SemaphoreType.DMA((len(names),)),
        ],
        5_000_000_000,
        weight_bytes,
    )
    mlp_sums = scatter_sums(sums, chip_bits, gctx)
    mix_other = xor_send(mix_send, "replica", 1)
    gj = call(
        back_kernel(width),
        shaped((2 * BLOCK, 4 * half), BF),
        (gj_first, halves, gctx, q, k, v, p, cosine, sine),
        [mlp_sums[0][2], mlp_sums[1][2], mix_other],
        [],
        6_000_000_000,
        weight_bytes,
    )
    gj, _ = lax.optimization_barrier((gj, (mlp_sums[0][1], mlp_sums[1][1])))
    mlp_sums = [last_sum(stream) for stream in mlp_sums]
    gj, mlp_sums = lax.optimization_barrier((gj, mlp_sums))
    gj_other = xor_send(gj, "shard", 1)
    norm_keep, norm_send = call(
        norm_back_kernel(qkv_names, len(qkv_arrays), rows, width),
        (shaped((BLOCK, width), F32), shaped((BLOCK, width), BF)),
        (gj,),
        qkv_arrays,
        [
            pltpu.VMEM((width, 3 * half), BF),
            pltpu.VMEM((2 * BLOCK, width), F32),
            pltpu.SemaphoreType.DMA((len(qkv_names),)),
        ],
        3_000_000_000,
        weight_bytes,
    )
    sums = call(
        qkv_grad_kernel(js, slots, rows, width),
        stack(6 * rows),
        (normed, normed_other, ctx_pair, ctx_pair_other, gj, gj_other),
        [norm_keep],
        [
            pltpu.VMEM((width, 4 * BLOCK), BF),
            pltpu.VMEM((width, 4 * BLOCK), BF),
            pltpu.VMEM((4 * BLOCK, 4 * half), BF),
        ],
        3_000_000_000,
        weight_bytes,
    )
    mlp_mine = [side_sum(mlp_sums[0], sums[1])]
    qkv_sums = scatter_sums(sums, chip_bits, None, mlp_mine[0])
    mlp_mine.append(side_sum(mlp_sums[1], (qkv_sums[0][2], qkv_sums[1][2])))
    mlp_other = [xor_send(part, "replica", 1) for part in mlp_mine]
    sent = (qkv_sums[0][1], qkv_sums[1][1])
    norm_send, _ = lax.optimization_barrier((norm_send, sums[1]))
    norm_other = xor_send(norm_send, "replica", 1)
    norm_other, mix_other, _ = lax.optimization_barrier((norm_other, mix_other, sent))
    mixed = (mix_keep + mix_other.astype(F32)).astype(BF)
    grad_tokens = call(
        final_kernel,
        shaped((block, width), BF),
        (tokens, norm_keep, norm_other, ghid, gains),
        [],
        [],
        1_000_000,
        1_000_000,
    )
    grad_glu, grad_down, grad_ffn_gain = call(
        mlp_unpack_kernel(rows, down_rows, take, width, units, count),
        (
            shaped((rows, 2 * count * down_rows), F32),
            shaped((down_rows, width), F32),
            shaped((1, rows), F32),
        ),
        (*mlp_mine, *mlp_other, glu_weight, ffn_gain[None]),
        [],
        [pltpu.VMEM((2, 2, height, 128), F32), pltpu.VMEM((rows, units), F32)],
        1_000_000,
        4_000_000,
    )
    done = (mixed, grad_tokens, grad_glu)
    qkv_mine = [side_sum(last_sum(stream), done) for stream in qkv_sums]
    qkv_other = [xor_send(part, "replica", 1) for part in qkv_mine]
    grad_qkv, grad_attn, grad_attn_gain = call(
        qkv_unpack_kernel(rows, width),
        (
            shaped((rows, 3 * width), F32),
            shaped((rows, width), F32),
            shaped((1, rows), F32),
        ),
        (*qkv_mine, *qkv_other, qkv_weight, attn_gain[None]),
        [],
        [pltpu.VMEM((2, 2, 6 * rows, 128), F32)],
        1_000_000,
        4_000_000,
    )
    return (
        mixed,
        grad_tokens,
        grad_qkv,
        grad_attn,
        grad_glu,
        grad_down,
        grad_attn_gain.reshape(rows),
        grad_ffn_gain.reshape(rows),
    )


def solution(mesh):
    in_specs = (
        P(("shard", "replica"), None),
        P(("shard", "replica")),
        P("shard", None),
        P("shard", None),
        P("shard", None),
        P("shard", None),
        P("shard"),
        P("shard"),
        P(("shard", "replica"), None),
    )
    out_specs = (
        P(("shard", "replica"), None),
        P(("shard", "replica"), None),
        P("shard", None),
        P("shard", None),
        P("shard", None),
        P("shard", None),
        P("shard"),
        P("shard"),
    )
    return jax.shard_map(
        on_device, mesh=mesh, in_specs=in_specs, out_specs=out_specs, check_vma=False
    )
```

```python
import math

import jax
import jax.numpy as jnp
from jax import lax
from jax.experimental import pallas as pl
from jax.experimental.pallas import tpu as pltpu
from jax.sharding import PartitionSpec as P

HEAD = 64
RADIUS = 64
BLOCK = 128
EPSILON = 1e-05
THETA_BASE = 10000.0
NEGATIVE = -1e30
VMEM_BYTES = 24 * 1024 * 1024
VMEM_ALL = 60 * 1024 * 1024
BF = jnp.bfloat16
F32 = jnp.float32


def xor_send(array, axis, bit):
    count = lax.axis_size(axis)
    return lax.ppermute(array, axis, [(i, i ^ bit) for i in range(count)])


def bits_of(count):
    return [1 << i for i in range(count.bit_length() - 1)]


def core_send(array, bits):
    count = lax.axis_size("shard")
    return lax.ppermute(array, "shard", [(i, i ^ bits[i & 1]) for i in range(count)])


def gather_pieces(own, split, chip_bits, before=None):
    if len(chip_bits) == 2:
        x, y = chip_bits
        from_x, from_y = xor_send(own, "shard", x), xor_send(own, "shard", y)
        if before is not None:
            (from_x, from_y), _ = lax.optimization_barrier(((from_x, from_y), before))
        pieces = [(0, 2, own), (x, 2, from_x), (y, 2, from_y)]
        forward = [from_x[:, :split], from_y[:, split:]]
        pieces.append((x | y, 0, xor_send(forward[0], "shard", y)))
        pieces.append((x | y, 1, xor_send(forward[1], "shard", x)))
    else:
        streams = ([(0, 0, own[:, :split])], [(0, 1, own[:, split:])])
        for stage in range(len(chip_bits)):
            grown = []
            for which, bit in ((0, chip_bits[stage]), (1, chip_bits[-1 - stage])):
                grown.append(
                    [(j ^ bit, s, xor_send(a, "shard", bit)) for j, s, a in streams[which]]
                )
            for held, more in zip(streams, grown):
                held.extend(more)
        pieces = streams[0] + streams[1]
        forward = []
    return pieces, forward


def with_core(pieces, joined):
    rows = pieces[0][2].shape[0]
    arrays = [a for _, _, a in pieces]
    names = [(j, s, i, 0) for i, (j, s, _) in enumerate(pieces)]
    whole = [p for p in pieces if p[1] == 2]
    others = pieces[len(whole) :]
    if joined and whole:
        whole.append((others[0][0], 2, jnp.concatenate([a for _, _, a in others], axis=1)))
        others = []
    groups = ([whole] if whole else []) + [[p] for p in others]
    for group in groups:
        sent = [a for _, _, a in group]
        sent = jnp.concatenate(sent, axis=0) if len(sent) > 1 else sent[0]
        arrays.append(xor_send(sent, "shard", 1))
        names += [(p[0] ^ 1, p[1], len(arrays) - 1, i * rows) for i, p in enumerate(group)]
    return names, arrays


def add_low(left, right):
    return (left.astype(F32) + right.astype(F32)).astype(BF)


def halve(keep, other):
    middle = keep.shape[0] // 2
    return add_low(keep[middle:], other[middle:]), add_low(keep[:middle], other[:middle])


def scatter_sums(sums, chip_bits, before_add=None, before_last=None):
    send, keep = sums
    orders = list(zip(chip_bits, chip_bits[::-1]))
    for bits in orders[:-1]:
        other = core_send(send, bits)
        if before_add is not None:
            other, _ = lax.optimization_barrier((other, before_add))
        send, keep = halve(keep, other)
    if before_last is not None:
        send, _ = lax.optimization_barrier((send, before_last))
    return keep, core_send(send, orders[-1]), send


def last_sums(keep, other, _):
    middle = keep.shape[1] // 2
    return [
        add_low(keep[0, :middle], other[0, :middle]),
        add_low(keep[0, middle:], other[0, middle:]),
    ]


def side_sum(total, after=None):
    for bit in bits_of(lax.axis_size("replica"))[1:]:
        other = xor_send(total, "replica", bit)
        if after is not None:
            other, _ = lax.optimization_barrier((other, after))
        total = add_low(total, other)
    return total


def dot(left, right):
    return jnp.dot(left, right, preferred_element_type=F32)


def dot_cols(left, right):
    return lax.dot_general(left, right, (((1,), (1,)), ((), ())), preferred_element_type=F32)


def dot_rows(left, right):
    return lax.dot_general(left, right, (((0,), (0,)), ((), ())), preferred_element_type=F32)


def standardize(vector):
    average = jnp.mean(vector, axis=-1, keepdims=True)
    centred = vector - average
    spread = jnp.mean(centred * centred, axis=-1, keepdims=True)
    inverse = lax.rsqrt(spread + EPSILON)
    return centred * inverse, inverse


def norm_back(grad, gain, hat, inverse):
    dhat = grad * gain
    mean = jnp.mean(dhat, axis=-1, keepdims=True)
    along = jnp.mean(dhat * hat, axis=-1, keepdims=True)
    return (dhat - mean - hat * along) * inverse


def turned(vector):
    width = vector.shape[-1]
    lane = lax.broadcasted_iota(jnp.int32, vector.shape, 1)
    return jnp.where(
        (lane & 63) < 32, pltpu.roll(vector, width - 32, 1), pltpu.roll(vector, 32, 1)
    )


def place(me, pieces, refs, layout, sems):
    copies = []
    for j, stream, which, base in pieces:
        owner = me ^ j
        ref = refs[which]
        for row, rows, col, cols, dst, dst_col in layout[stream]:
            start = owner * rows
            if rows % 16 == 0:
                start = pl.multiple_of(start, 16)
            copy = pltpu.make_async_copy(
                ref.at[pl.ds(base + row, rows), pl.ds(col, cols)],
                dst.at[pl.ds(start, rows), pl.ds(dst_col, cols)],
                sems.at[len(copies)],
            )
            copy.start()
            copies.append(copy)
    return copies


def call(kernel, out_shape, inputs, in_any, scratch, flops, traffic, vmem_bytes=VMEM_BYTES):
    any_spec = pl.BlockSpec(memory_space=pl.ANY)
    vmem = pl.BlockSpec(memory_space=pltpu.VMEM)
    specs = [vmem] * len(inputs) + [any_spec] * len(in_any)
    return pl.pallas_call(
        kernel,
        out_shape=out_shape,
        in_specs=specs,
        out_specs=jax.tree.map(lambda _: vmem, out_shape),
        scratch_shapes=scratch,
        compiler_params=pltpu.CompilerParams(vmem_limit_bytes=vmem_bytes),
        cost_estimate=pl.CostEstimate(flops=flops, bytes_accessed=traffic, transcendentals=0),
    )(*inputs, *in_any)


def shard_at():
    return lax.axis_index("shard").astype(jnp.int32)


def side_at():
    return lax.axis_index("replica").astype(jnp.int32) & 1


def shaped(shape, dtype):
    return jax.ShapeDtypeStruct(shape, dtype)


def pack_qkv_kernel(half):
    def body(weight, attn_gain, ffn_gain, out, attn_held, ffn_held, sems):
        rows = weight.shape[0]
        first = side_at() * half
        copies = [
            pltpu.make_async_copy(attn_gain, attn_held, sems.at[0]),
            pltpu.make_async_copy(ffn_gain, ffn_held, sems.at[1]),
        ]
        for i in range(3):
            start = pl.multiple_of(i * 2 * half + first, 128)
            copies.append(
                pltpu.make_async_copy(
                    weight.at[:, pl.ds(start, half)],
                    out.at[:, pl.ds(i * half, half)],
                    sems.at[2 + i],
                )
            )
        for copy in copies:
            copy.start()
        copies[0].wait()
        copies[1].wait()
        gains = [ref[...].astype(F32) for ref in (attn_held, ffn_held)]
        gains = jnp.concatenate(gains + [jnp.zeros((6, rows), F32)], axis=0)
        gains = jnp.concatenate([gains, jnp.zeros((8, 128 - rows), F32)], axis=1)
        square = jnp.concatenate([gains, jnp.zeros((120, 128), F32)], axis=0)
        out[:, 3 * half :] = square.T[0:rows, :].astype(BF)
        for copy in copies[2:]:
            copy.wait()

    return body


def pack_mlp_kernel(count, down_rows, take):
    def body(attn, glu, down, out):
        rows, width = attn.shape
        units = count * take
        hidden = count * down_rows
        out[:, 0:width] = attn[...]
        last = width + 2 * units

        def pick(first):
            for part in range(2):
                for s in range(count):
                    at = part * hidden + s * down_rows + first
                    to = width + part * units + s * take
                    out[:, to : to + take] = glu[:, at : at + take]
            out[0:take, last:] = down[first : first + take, :]

        @pl.when(side_at() == 0)
        def _():
            pick(0)

        @pl.when(side_at() != 0)
        def _():
            pick(down_rows - take)

        if rows > take:
            out[take:, last:] = jnp.zeros((rows - take, width), BF)

    return body


def around_kernel(own, places, partner, near, far, out, cosine, sine, bias):
    def arrange(*blocks):
        for i, ref in enumerate(blocks):
            out[i * BLOCK : (i + 1) * BLOCK, :] = ref[0:BLOCK, :]

    @pl.when(side_at() == 0)
    def _():
        arrange(near, own, partner, far)

    @pl.when(side_at() != 0)
    def _():
        arrange(far, partner, own, near)

    def places_of(ref):
        first = ref.shape[0] - 16
        return ref[first : first + 1, 0:BLOCK].astype(F32) * 256.0 + ref[
            first + 1 : first + 2, 0:BLOCK
        ].astype(F32)

    mine, theirs = places[...].astype(F32), places_of(partner)
    inner, outer = places_of(near), places_of(far)
    even = side_at() == 0
    lines = [
        jnp.where(even, inner, outer),
        jnp.where(even, mine, theirs),
        jnp.where(even, theirs, mine),
        jnp.where(even, outer, inner),
    ]
    stacked = jnp.concatenate([jnp.broadcast_to(line, (BLOCK, BLOCK)).T for line in lines], axis=0)
    lane = lax.broadcasted_iota(jnp.int32, (1, 128), 1)
    power = lax.rem(lane, HEAD // 2).astype(F32) * (2.0 / HEAD)
    phases = stacked * jnp.exp(power * -math.log(THETA_BASE))
    cosine[...] = jnp.cos(phases)
    sine[...] = jnp.where((lane & 63) < 32, -1.0, 1.0) * jnp.sin(phases)
    offset = (
        lax.broadcasted_iota(jnp.int32, (BLOCK, 2 * BLOCK), 1)
        - RADIUS
        - lax.broadcasted_iota(jnp.int32, (BLOCK, 2 * BLOCK), 0)
    )
    distance = offset.astype(F32)
    for b in range(3):
        start = RADIUS + b * BLOCK
        key = jnp.concatenate([lines[b], lines[b + 1]], axis=1)
        query = jnp.concatenate([stacked[start : start + BLOCK, :]] * 2, axis=1)
        later = jnp.where(offset >= 0, key - distance, query + distance)
        allowed = (jnp.abs(offset) <= RADIUS) & (later >= 0.0)
        bias[b * BLOCK : (b + 1) * BLOCK, :] = jnp.where(allowed, 0.0, NEGATIVE)


def around_back_kernel(own, partner, near, far, out):
    def arrange(before, first, second, after):
        out[0:RADIUS, :] = before[...]
        out[RADIUS : RADIUS + BLOCK, :] = first
        out[RADIUS + BLOCK : RADIUS + 2 * BLOCK, :] = second
        out[RADIUS + 2 * BLOCK :, :] = after[...]

    theirs = partner[...]

    @pl.when(side_at() == 0)
    def _():
        arrange(near, own[...], theirs, far)

    @pl.when(side_at() != 0)
    def _():
        arrange(far, theirs, own[...], near)


def qkv_layout(rows, half, weight, gains=None):
    wide = 3 * half
    split = (wide + 128) // 2
    streams = [[(0, rows, 0, split, weight, 0)], [(0, rows, 0, wide - split, weight, split)]]
    streams.append([(0, rows, 0, wide, weight, 0)])
    if gains is not None:
        streams[1].append((0, rows, wide - split, 128, gains, 0))
        streams[2].append((0, rows, wide, 128, gains, 0))
    return streams


def project_kernel(pieces, n_refs, rows, width, skip):
    half = width // 2
    span = 4 * BLOCK

    def body(tok, cosine, sine, bias, *rest):
        refs, rest = rest[skip : n_refs + skip], rest[n_refs + skip :]
        q_out, k_out, v_out, p_out, ctx_out, normed_out, gains_out = rest[:7]
        weight, gain_cols, normed, sems = rest[7:]
        layout = qkv_layout(rows, half, weight, gain_cols)
        copies = place(shard_at(), pieces, refs, layout, sems)
        hats = [
            standardize(tok[i * BLOCK : (i + 1) * BLOCK, :].astype(F32))[0] for i in range(4)
        ]
        for copy in copies:
            copy.wait()
        pick = jnp.where(
            lax.broadcasted_iota(jnp.int32, (8, 128), 0)
            == lax.broadcasted_iota(jnp.int32, (8, 128), 1),
            1.0,
            0.0,
        ).astype(BF)
        gains = dot_cols(pick, gain_cols[...])
        gains_out[...] = gains
        for i, hat in enumerate(hats):
            normed[i * BLOCK : (i + 1) * BLOCK, :] = (hat * gains[0:1]).astype(BF)
        normed_out[...] = normed[BLOCK : 3 * BLOCK, :]
        cos3 = jnp.concatenate([cosine[...]] * 3, axis=1)
        sin3 = jnp.concatenate([sine[...]] * 3, axis=1)
        mid = slice(RADIUS, span - RADIUS)
        joined = dot(normed[mid, :], weight[:, 0:half])
        q_out[...] = (joined * cos3[mid] + turned(joined) * sin3[mid]).astype(BF)
        joined = dot(normed[...], weight[:, half : 2 * half])
        k_out[...] = (joined * cos3 + turned(joined) * sin3).astype(BF)
        v_out[...] = dot(normed[...], weight[:, 2 * half : 3 * half]).astype(BF)
        lane = lax.broadcasted_iota(jnp.int32, (BLOCK, 128), 1)
        scale = 1.0 / math.sqrt(HEAD)
        for pair in range(half // 128):
            cols = slice(pair * 128, pair * 128 + 128)
            for b in range(3):
                rows_q = slice(b * BLOCK, (b + 1) * BLOCK)
                rows_k = slice(b * BLOCK, (b + 2) * BLOCK)
                queries, keys, values = q_out[rows_q, cols], k_out[rows_k, cols], v_out[rows_k, cols]
                parts = []
                for h in range(2):
                    mine = (lane < HEAD) if h == 0 else (lane >= HEAD)
                    masked = jnp.where(mine, queries.astype(F32) * scale, 0.0).astype(BF)
                    scores = dot_cols(masked, keys) + bias[rows_q, :]
                    exponent = jnp.exp(scores - jnp.max(scores, axis=1, keepdims=True))
                    total = jnp.sum(exponent, axis=1, keepdims=True)
                    shares = (exponent * (1.0 / total)).astype(BF)
                    p_out[(pair * 2 + h) * 3 + b] = shares
                    parts.append(dot(shares, values))
                ctx_out[rows_q, cols] = jnp.where(lane < HEAD, parts[0], parts[1]).astype(BF)

    return body


def attn_layout(rows, width, attn):
    parts = [(0, rows, 0, width, attn, 0)]
    return (parts, (), parts)


def mlp_layout(rows, take, width, units, attn, glu, down):
    one = (0, rows, 0, width, attn, 0)
    gate = (0, rows, width, units, glu, 0)
    up = (0, rows, 0, units, glu, units)
    low = (0, take, units, width, down, 0)
    whole = (one, (0, rows, width, 2 * units, glu, 0), (0, take, width + 2 * units, width, down, 0))
    return ((one, gate), (up, low), whole)


def mlp_kernel(pieces, n_refs, rows, down_rows, take, width, units):
    half = width // 2
    pair = slice(RADIUS, RADIUS + 2 * BLOCK)

    def body(tok, ctx_own, ctx_other, dy, gains, *rest):
        refs, rest = rest[1 : n_refs + 1], rest[n_refs + 1 :]
        mix_keep, mix_send, shared, ctx_pair, hidden, gn_out = rest[:6]
        attn, glu, down, ggu, mix, sems = rest[6:]
        layout = mlp_layout(rows, take, width, units, attn, glu, down)
        copies = place(shard_at(), pieces, refs, layout, sems)
        at = side_at()
        inputs = tok[RADIUS : RADIUS + 3 * BLOCK, :].astype(F32)
        own_rows = pl.ds(pl.multiple_of(at * half, 128), half)
        other_rows = pl.ds(pl.multiple_of((1 - at) * half, 128), half)

        @pl.when(at == 0)
        def _():
            ctx_pair[:, 0:half] = ctx_own[pair, :]
            ctx_pair[:, half:] = ctx_other[pair, :]

        @pl.when(at != 0)
        def _():
            ctx_pair[:, 0:half] = ctx_other[pair, :]
            ctx_pair[:, half:] = ctx_own[pair, :]

        for copy in copies:
            copy.wait()
        lifted = dot(ctx_own[...], attn[own_rows, :]) + dot(ctx_other[...], attn[other_rows, :])
        hidden[...] = inputs + lifted
        hat, _ = standardize(hidden[...])
        normed = (hat * gains[1:2, :]).astype(BF)
        shared[:, 0:width] = normed[pair]
        partial = jnp.zeros((2 * BLOCK, width), F32)
        unit = lax.rem(lax.broadcasted_iota(jnp.int32, (1, units), 1), take)
        mask = jnp.where(unit >= at * (2 * take - down_rows), 1.0, 0.0)
        for c in range(0, units, 256):
            wide = min(256, units - c)
            cols = slice(c, c + wide)
            gate = dot(normed, glu[:, cols])
            up = dot(normed, glu[:, units + c : units + c + wide])
            grad_act = dot_cols(dy[...], down[cols, :]) * mask[:, cols]
            share = 0.5 * (1.0 + lax.erf(gate * (1.0 / math.sqrt(2.0))))
            density = jnp.exp(-0.5 * gate * gate) * (1.0 / math.sqrt(2.0 * math.pi))
            gelu = gate * share
            act = (gelu[pair] * up[pair] * mask[:, cols]).astype(BF)
            shared[:, width + c : width + c + wide] = act
            partial = partial + dot(act, down[cols, :])
            ggu[:, cols] = (grad_act * up * (share + gate * density)).astype(BF)
            ggu[:, units + c : units + c + wide] = (grad_act * gelu).astype(BF)
        mix[...] = partial
        mine = pl.ds(pl.multiple_of(at * BLOCK, BLOCK), BLOCK)
        theirs = pl.ds(pl.multiple_of((1 - at) * BLOCK, BLOCK), BLOCK)
        mix_keep[...] = mix[mine, :] + hidden[pl.ds(pl.multiple_of(RADIUS + at * BLOCK, 8), BLOCK), :]
        mix_send[...] = mix[theirs, :].astype(BF)
        shared[:, width + units :] = ggu[pair, :]
        grad = dot_cols(ggu[...], glu[...])
        gn_out[...] = grad.astype(BF)

    return body


def pair_back(pair, gctx, q, k, v, p, cos, sin):
    lane = lax.broadcasted_iota(jnp.int32, (BLOCK, 128), 1)
    lane2 = lax.broadcasted_iota(jnp.int32, (2 * BLOCK, 128), 1)
    scale = 1.0 / math.sqrt(HEAD)
    cols = slice(pair * 128, pair * 128 + 128)
    first, second = slice(0, BLOCK), slice(BLOCK, 2 * BLOCK)
    low, high = slice(0, RADIUS), slice(RADIUS, BLOCK)
    grad_q = jnp.zeros((2 * BLOCK, 128), F32)
    grad_k, grad_v = [0.0, 0.0], [0.0, 0.0]
    for h in range(2):
        mine = (lane < HEAD) if h == 0 else (lane >= HEAD)
        mine2 = (lane2 < HEAD) if h == 0 else (lane2 >= HEAD)
        scores, shares, queries, grads, parts = [], [], [], [], []
        for b in range(3):
            rows_q = slice(b * BLOCK, (b + 1) * BLOCK)
            rows_k = slice(b * BLOCK, (b + 2) * BLOCK)
            keys, values = k[rows_k, cols], v[rows_k, cols]
            lowered = jnp.where(mine, gctx[rows_q, cols].astype(F32), 0.0).astype(BF)
            query = jnp.where(mine, q[rows_q, cols].astype(F32) * scale, 0.0).astype(BF)
            share = p[(pair * 2 + h) * 3 + b]
            wide = share.astype(F32)
            grad_share = dot_cols(lowered, values)
            row = jnp.sum(wide * grad_share, axis=1, keepdims=True)
            grad_score = (wide * (grad_share - row)).astype(BF)
            scores.append(grad_score)
            shares.append(share)
            queries.append(query)
            grads.append(lowered)
            part = (high, first, low)[b]
            parts.append(dot(grad_score[part], keys))
        grad_q = grad_q + jnp.where(mine2, jnp.concatenate(parts, axis=0) * scale, 0.0)
        for i in range(2):
            two = slice(i, i + 2)
            for total, left, right in ((grad_k, scores, queries), (grad_v, shares, grads)):
                upper, lower = left[i][:, second], left[i + 1][:, first]
                total[i] = total[i] + dot_rows(
                    jnp.concatenate([upper, lower], axis=0), jnp.concatenate(right[two], axis=0)
                )
    grad_k, grad_v = jnp.concatenate(grad_k, axis=0), jnp.concatenate(grad_v, axis=0)
    return (
        (grad_q * cos - turned(grad_q) * sin).astype(BF),
        (grad_k * cos - turned(grad_k) * sin).astype(BF),
        grad_v.astype(BF),
    )


def hidden_back_kernel(mlp_pieces, n_mlp, rows, width):
    half = width // 2
    pair = slice(RADIUS, RADIUS + 2 * BLOCK)

    def body(gn_own, gn_other, hidden, dy, gains, q, k, v, p, cosine, sine, *rest):
        mlp_refs, rest = rest[1 : n_mlp + 1], rest[n_mlp + 1 :]
        ghid_out, halves_out, gctx, first_out, attn, held, attn_sems = rest
        copies = place(shard_at(), mlp_pieces, mlp_refs, attn_layout(rows, width, attn), attn_sems)
        at = side_at()
        hat, inverse = standardize(hidden[...])
        grad = gn_own[...].astype(F32) + gn_other[...].astype(F32)
        grad_hidden = dy[...].astype(F32) + norm_back(grad, gains[1:2, :], hat, inverse)
        held[...] = grad_hidden[pair]
        ghid_out[...] = held[pl.ds(pl.multiple_of(at * BLOCK, BLOCK), BLOCK), :]
        halves = jnp.where(at == 0, grad_hidden[pair, 0:half], grad_hidden[pair, half:])
        halves_out[...] = halves.astype(BF)
        grad_low = grad_hidden.astype(BF)
        for copy in copies:
            copy.wait()
        own_rows = pl.ds(pl.multiple_of(at * half, 128), half)
        gctx[...] = dot_cols(grad_low, attn[own_rows, :]).astype(BF)
        cos, sin = cosine[BLOCK : 3 * BLOCK, :], sine[BLOCK : 3 * BLOCK, :]
        for part, grad in enumerate(pair_back(0, gctx, q, k, v, p, cos, sin)):
            first_out[:, part * 128 : (part + 1) * 128] = grad

    return body


def back_kernel(width):
    half = width // 2

    def body(first, halves, gctx, q, k, v, p, cosine, sine, sent, mixed, gj_out):
        gj_out[:, 3 * half :] = halves[...]
        cos, sin = cosine[BLOCK : 3 * BLOCK, :], sine[BLOCK : 3 * BLOCK, :]
        for part in range(3):
            gj_out[:, part * half : part * half + 128] = first[:, part * 128 : (part + 1) * 128]
        for i in range(1, half // 128):
            for part, grad in enumerate(pair_back(i, gctx, q, k, v, p, cos, sin)):
                col = part * half + i * 128
                gj_out[:, col : col + 128] = grad

    return body


def norm_back_kernel(pieces, n_refs, rows, width):
    half = width // 2

    def body(gj, *rest):
        refs, rest = rest[:n_refs], rest[n_refs:]
        keep_out, send_out, weight, held, sems = rest
        copies = place(shard_at(), pieces, refs, qkv_layout(rows, half, weight), sems)
        at = side_at()
        for copy in copies:
            copy.wait()
        held[...] = dot_cols(gj[:, 0 : 3 * half], weight[...])
        keep_out[...] = held[pl.ds(pl.multiple_of(at * BLOCK, BLOCK), BLOCK), :]
        theirs = pl.ds(pl.multiple_of((1 - at) * BLOCK, BLOCK), BLOCK)
        send_out[...] = held[theirs, :].astype(BF)

    return body


def final_kernel(tok, keep, other, ghid, gains, out):
    hat, inverse = standardize(tok[...].astype(F32))
    grad = keep[...] + other[...].astype(F32)
    out[...] = (ghid[...] + norm_back(grad, gains[0:1, :], hat, inverse)).astype(BF)


def slots_of(chip_bits):
    tables = []
    for order in (chip_bits, chip_bits[::-1]):
        kept = [0]
        for bit in order[1:][::-1]:
            kept = kept + [j | bit for j in kept]
        tables.append([(1, i, j) for i, j in enumerate(kept)])
        tables[-1] += [(0, i, j | order[0]) for i, j in enumerate(kept)]
    return [(kept, i, j, k) for (kept, i, j), (_, _, k) in zip(*tables)]


def owner_rows(me, slots, lhs_t, rows):
    parts = []
    for _, _, even, odd in slots:
        owner = me ^ jnp.where((me & 1) == 0, even, odd)
        parts.append(lhs_t[pl.ds(pl.multiple_of(owner * rows, 16), rows), :])
    return jnp.concatenate(parts, axis=0)


def emit(outs, slots, rows, grad, start):
    grad = grad.astype(BF)
    for i, (kept, at, _, _) in enumerate(slots):
        for c in range(grad.shape[1] // 128):
            row = start + c * rows
            outs[kept][at, row : row + rows, :] = grad[
                i * rows : (i + 1) * rows, c * 128 : (c + 1) * 128
            ]


def mlp_grad_kernel(slots, rows, take, width, units):
    half = width // 2

    def body(own, other, dy_own, dy_other, *rest):
        outs, (normed_t, act_t, ggu, dy) = rest[1:3], rest[3:]
        me = shard_at()
        pair = slice(RADIUS, RADIUS + 2 * BLOCK)
        for i, (ref, dref) in enumerate(((own, dy_own), (other, dy_other))):
            tok = slice(i * 2 * BLOCK, (i + 1) * 2 * BLOCK)
            normed_t[:, tok] = ref[:, 0:width].T
            act_t[:, tok] = ref[:, width : width + units].T
            ggu[tok, :] = ref[:, width + units :]
            dy[tok, :] = dref[pair, :]
        left = owner_rows(me, slots, normed_t, rows)
        act = owner_rows(me, slots, act_t, take)
        height = outs[0].shape[1] // 2
        for s in range(2):
            grad = dot(left, ggu[:, s * units : (s + 1) * units])
            emit(outs, slots, rows, grad, s * height)
            grad = dot(act, dy[:, s * half : (s + 1) * half])
            emit(outs, slots, take, grad, s * height + rows * (units // 128))

    return body


def qkv_grad_kernel(slots, rows, width):
    half = width // 2

    def body(normed_own, normed_other, ctx_own, ctx_other, own, other, *rest):
        outs, (normed_t, ctx_t, gj) = rest[1:3], rest[3:]
        me = shard_at()
        count = 2 * BLOCK
        each = ((normed_own, ctx_own, own), (normed_other, ctx_other, other))
        for i, (nref, cref, ref) in enumerate(each):
            tok = slice(i * count, (i + 1) * count)
            normed_t[:, tok] = nref[...].T
            ctx_t[:, tok] = cref[...].T
            gj[tok, :] = ref[...]
        left = owner_rows(me, slots, normed_t, rows)
        ctx = owner_rows(me, slots, ctx_t, rows)
        emit(outs, slots, rows, dot(left, gj[:, 0 : 3 * half]), 0)
        emit(outs, slots, rows, dot(ctx, gj[:, 3 * half :]), 9 * rows)

    return body


def gain_grad(weight, grad, gain):
    total = jnp.sum(weight[...].astype(F32) * grad[...], axis=1, keepdims=True)
    rows = total.shape[0]
    total = jnp.concatenate([total, jnp.zeros((128 - rows, 1), F32)], axis=0)
    return jnp.broadcast_to(total, (128, 128)).T[0:1, 0:rows] / gain[...].astype(F32)


def mlp_unpack_kernel(rows, down_rows, take, width, units, count):
    hidden = count * down_rows
    spare = 2 * take - down_rows

    def body(mine_0, mine_1, other_0, other_1, weight, gain, sent, glu, down, gain_out, held, wide):
        at = side_at()
        tiles = units // 128
        for s, (mine, other) in enumerate(((mine_0, other_0), (mine_1, other_1))):
            held[at, s] = mine[...].astype(F32)
            held[1 - at, s] = other[...].astype(F32)
        for s in range(2):
            for t in range(2):
                for c in range(tiles):
                    row = c * rows
                    wide[:, c * 128 : (c + 1) * 128] = held[t, s, row : row + rows, :]
                skip = 0 if t == 0 else spare
                for i in range(count):
                    col = s * hidden + i * down_rows + t * take
                    glu[:, col : col + take - skip] = wide[:, i * take + skip : (i + 1) * take]
                for c in range(width // 256):
                    row = tiles * rows + c * take
                    col = s * (width // 2) + c * 128
                    down[t * take : (t + 1) * take - skip, col : col + 128] = held[
                        t, s, row + skip : row + take, :
                    ]
        gain_out[...] = gain_grad(weight, glu, gain)

    return body


def qkv_unpack_kernel(rows, width):
    half = width // 2
    tiles = half // 128

    def body(mine_0, mine_1, other_0, other_1, weight, gain, qkv, attn, gain_out, held):
        at = side_at()
        for s, (mine, other) in enumerate(((mine_0, other_0), (mine_1, other_1))):
            held[at, s] = mine[...].astype(F32)
            held[1 - at, s] = other[...].astype(F32)
        for t in range(2):
            for i in range(3):
                for c in range(tiles):
                    row = (i % 2 * tiles + c) * rows
                    col = i * width + t * half + c * 128
                    qkv[:, col : col + 128] = held[t, i // 2, row : row + rows, :]
            for c in range(tiles):
                row = (tiles + c) * rows
                attn[:, t * half + c * 128 : t * half + (c + 1) * 128] = held[t, 1, row : row + rows, :]
        gain_out[...] = gain_grad(weight, qkv, gain)

    return body


def on_device(
    tokens,
    positions,
    qkv_weight,
    attn_weight,
    glu_weight,
    down_weight,
    attn_gain,
    ffn_gain,
    cotangent,
):
    block, width = tokens.shape
    half = width // 2
    rows, down_rows = qkv_weight.shape[0], down_weight.shape[0]
    count, replicas = lax.axis_size("shard"), lax.axis_size("replica")
    everyone = count * replicas
    take = -(-down_rows // 32) * 16
    units = count * take
    me = lax.axis_index("shard").astype(jnp.int32)
    side = lax.axis_index("replica").astype(jnp.int32) & 1
    chip_bits = bits_of(count)[1:]

    own = call(
        pack_qkv_kernel(half),
        shaped((rows, 3 * half + 128), BF),
        (),
        [qkv_weight, attn_gain[None], ffn_gain[None]],
        [
            pltpu.VMEM((1, rows), BF),
            pltpu.VMEM((1, rows), BF),
            pltpu.SemaphoreType.DMA((5,)),
        ],
        1_000_000,
        1_000_000,
        VMEM_ALL,
    )

    places = jnp.stack([positions >> 8, positions & 255]).astype(BF)
    places = jnp.pad(places, ((0, 14), (0, width - block)))
    rim = jnp.concatenate([tokens, places], axis=0)
    rim, _ = lax.optimization_barrier((rim, own))
    step = [1 if i & 1 else -1 for i in range(everyone)]
    both = ("shard", "replica")

    def outward(array):
        moves = [(i, i + step[i]) for i in range(everyone)]
        return lax.ppermute(array, both, [(a, b) for a, b in moves if 0 <= b < everyone])

    own_mlp = call(
        pack_mlp_kernel(count, down_rows, take),
        shaped((rows, 2 * width + 2 * units), BF),
        (attn_weight, glu_weight, down_weight),
        [],
        [],
        1_000_000,
        2_000_000,
    )
    qkv_parts, _ = gather_pieces(
        own, (3 * half + 128) // 2, chip_bits, rim
    )
    near, partner = outward(rim), xor_send(rim, "replica", 1)
    arrived = [a for _, _, a in qkv_parts]
    own, near, partner, arrived = lax.optimization_barrier((own_mlp, near, partner, arrived))
    qkv_parts = [(j, s, a) for (j, s, _), a in zip(qkv_parts, arrived)]
    far = xor_send(near, "replica", 1)
    mlp_parts, forward = gather_pieces(own, width + units, chip_bits)

    tok, cosine, sine, bias = call(
        around_kernel,
        (
            shaped((4 * BLOCK, width), BF),
            shaped((4 * BLOCK, 128), F32),
            shaped((4 * BLOCK, 128), F32),
            shaped((3 * BLOCK, 2 * BLOCK), F32),
        ),
        (tokens, positions[None], partner, near, far),
        [],
        [],
        1_000_000,
        2_000_000,
    )
    rim = jnp.where(side == 0, cotangent[:RADIUS], cotangent[block - RADIUS :])
    rim, _ = lax.optimization_barrier((rim, near))
    near_dy = outward(rim)
    sent, near_dy = lax.optimization_barrier((cotangent, near_dy))
    partner_dy = xor_send(sent, "replica", 1)
    far_dy = xor_send(near_dy, "replica", 1)
    qkv_names, qkv_arrays = with_core(qkv_parts, True)
    weight_bytes = width * 3 * width * 2

    q, k, v, p, ctx, normed, gains = call(
        project_kernel(qkv_names, len(qkv_arrays), rows, width, 2 + len(forward)),
        (
            shaped((3 * BLOCK, half), BF),
            shaped((4 * BLOCK, half), BF),
            shaped((4 * BLOCK, half), BF),
            shaped((3 * half // HEAD, BLOCK, 2 * BLOCK), BF),
            shaped((3 * BLOCK, half), BF),
            shaped((2 * BLOCK, width), BF),
            shaped((8, width), F32),
        ),
        (tok, cosine, sine, bias),
        [far_dy, partner_dy] + forward + qkv_arrays,
        [
            pltpu.VMEM((width, 3 * half), BF),
            pltpu.VMEM((width, 128), BF),
            pltpu.VMEM((4 * BLOCK, width), BF),
            pltpu.SemaphoreType.DMA((2 * len(qkv_names),)),
        ],
        7_000_000_000,
        weight_bytes,
    )
    ctx_other = xor_send(ctx, "replica", 1)
    normed_other = xor_send(normed, "shard", 1)
    near_dy, far_dy, partner_dy, _ = lax.optimization_barrier(
        (near_dy, far_dy, partner_dy, ctx)
    )
    dy = call(
        around_back_kernel,
        shaped((3 * BLOCK, width), BF),
        (cotangent, partner_dy, near_dy, far_dy),
        [],
        [],
        1_000_000,
        2_000_000,
    )
    dy_other = xor_send(dy, "shard", 1)
    held, _ = lax.optimization_barrier(([a for _, _, a in mlp_parts], ctx))
    mlp_parts = [(j, s, a) for (j, s, _), a in zip(mlp_parts, held)]
    names, arrays = with_core(mlp_parts, False)

    mix_keep, mix_send, shared, ctx_pair, hidden, gn = call(
        mlp_kernel(names, len(arrays), rows, down_rows, take, width, units),
        (
            shaped((BLOCK, width), F32),
            shaped((BLOCK, width), BF),
            shaped((2 * BLOCK, width + 3 * units), BF),
            shaped((2 * BLOCK, width), BF),
            shaped((3 * BLOCK, width), F32),
            shaped((3 * BLOCK, width), BF),
        ),
        (tok, ctx, ctx_other, dy, gains),
        [normed_other] + arrays,
        [
            pltpu.VMEM((width, width), BF),
            pltpu.VMEM((width, 2 * units), BF),
            pltpu.VMEM((units, width), BF),
            pltpu.VMEM((3 * BLOCK, 2 * units), BF),
            pltpu.VMEM((2 * BLOCK, width), F32),
            pltpu.SemaphoreType.DMA((3 * len(names),)),
        ],
        8_000_000_000,
        2 * weight_bytes,
    )
    gn_other = xor_send(gn, "replica", 1)
    shared_other = xor_send(shared, "shard", 1)
    ctx_pair_other = xor_send(ctx_pair, "shard", 1)

    slots = slots_of(chip_bits)
    portion = count // 4

    def stack(height):
        return (shaped((portion, 2 * height, 128), BF),) * 2

    height = rows * (units // 128) + take * (half // 128)
    sums = call(
        mlp_grad_kernel(slots, rows, take, width, units),
        stack(height),
        (shared, shared_other, dy, dy_other),
        [ctx_pair_other],
        [
            pltpu.VMEM((width, 4 * BLOCK), BF),
            pltpu.VMEM((units, 4 * BLOCK), BF),
            pltpu.VMEM((4 * BLOCK, 2 * units), BF),
            pltpu.VMEM((4 * BLOCK, width), BF),
        ],
        4_000_000_000,
        weight_bytes,
    )

    ghid, halves, gctx, gj_first = call(
        hidden_back_kernel(names, len(arrays), rows, width),
        (
            shaped((BLOCK, width), F32),
            shaped((2 * BLOCK, half), BF),
            shaped((3 * BLOCK, half), BF),
            shaped((2 * BLOCK, 3 * 128), BF),
        ),
        (gn, gn_other, hidden, dy, gains, q, k, v, p, cosine, sine),
        [sums[1]] + arrays,
        [
            pltpu.VMEM((width, width), BF),
            pltpu.VMEM((2 * BLOCK, width), F32),
            pltpu.SemaphoreType.DMA((len(names),)),
        ],
        5_000_000_000,
        weight_bytes,
    )
    mlp_sums = scatter_sums(sums, chip_bits, gctx)
    mix_other = xor_send(mix_send, "replica", 1)
    gj = call(
        back_kernel(width),
        shaped((2 * BLOCK, 4 * half), BF),
        (gj_first, halves, gctx, q, k, v, p, cosine, sine),
        [mlp_sums[2], mix_other],
        [],
        6_000_000_000,
        weight_bytes,
    )
    gj_other = xor_send(gj, "shard", 1)
    norm_keep, norm_send = call(
        norm_back_kernel(qkv_names, len(qkv_arrays), rows, width),
        (shaped((BLOCK, width), F32), shaped((BLOCK, width), BF)),
        (gj,),
        qkv_arrays,
        [
            pltpu.VMEM((width, 3 * half), BF),
            pltpu.VMEM((2 * BLOCK, width), F32),
            pltpu.SemaphoreType.DMA((len(qkv_names),)),
        ],
        3_000_000_000,
        weight_bytes,
    )
    sums = call(
        qkv_grad_kernel(slots, rows, width),
        stack(6 * rows),
        (normed, normed_other, ctx_pair, ctx_pair_other, gj, gj_other),
        [norm_keep],
        [
            pltpu.VMEM((width, 4 * BLOCK), BF),
            pltpu.VMEM((width, 4 * BLOCK), BF),
            pltpu.VMEM((4 * BLOCK, 4 * half), BF),
        ],
        3_000_000_000,
        weight_bytes,
    )
    mlp_sums, _ = lax.optimization_barrier((mlp_sums, sums[1]))
    mlp_sums = last_sums(*mlp_sums)
    qkv_sums = scatter_sums(sums, chip_bits)
    mlp_mine = [side_sum(part, qkv_sums[2]) for part in mlp_sums]
    mlp_other = [xor_send(part, "replica", 1) for part in mlp_mine]
    sent = qkv_sums[1]
    norm_send, _ = lax.optimization_barrier((norm_send, sums[1]))
    norm_other = xor_send(norm_send, "replica", 1)
    norm_other, mix_other, _ = lax.optimization_barrier((norm_other, mix_other, sent))
    mixed = (mix_keep + mix_other.astype(F32)).astype(BF)
    grad_tokens = call(
        final_kernel,
        shaped((block, width), BF),
        (tokens, norm_keep, norm_other, ghid, gains),
        [],
        [],
        1_000_000,
        1_000_000,
    )
    grad_glu, grad_down, grad_ffn_gain = call(
        mlp_unpack_kernel(rows, down_rows, take, width, units, count),
        (
            shaped((rows, 2 * count * down_rows), F32),
            shaped((down_rows, width), F32),
            shaped((1, rows), F32),
        ),
        (*mlp_mine, *mlp_other, glu_weight, ffn_gain[None]),
        [sent],
        [pltpu.VMEM((2, 2, height, 128), F32), pltpu.VMEM((rows, units), F32)],
        1_000_000,
        4_000_000,
    )
    done = (mixed, grad_tokens, grad_glu)
    qkv_mine = [side_sum(part, done) for part in last_sums(*qkv_sums)]
    qkv_other = [xor_send(part, "replica", 1) for part in qkv_mine]
    grad_qkv, grad_attn, grad_attn_gain = call(
        qkv_unpack_kernel(rows, width),
        (
            shaped((rows, 3 * width), F32),
            shaped((rows, width), F32),
            shaped((1, rows), F32),
        ),
        (*qkv_mine, *qkv_other, qkv_weight, attn_gain[None]),
        [],
        [pltpu.VMEM((2, 2, 6 * rows, 128), F32)],
        1_000_000,
        4_000_000,
    )
    return (
        mixed,
        grad_tokens,
        grad_qkv,
        grad_attn,
        grad_glu,
        grad_down,
        grad_attn_gain.reshape(rows),
        grad_ffn_gain.reshape(rows),
    )


def solution(mesh):
    in_specs = (
        P(("shard", "replica"), None),
        P(("shard", "replica")),
        P("shard", None),
        P("shard", None),
        P("shard", None),
        P("shard", None),
        P("shard"),
        P("shard"),
        P(("shard", "replica"), None),
    )
    out_specs = (
        P(("shard", "replica"), None),
        P(("shard", "replica"), None),
        P("shard", None),
        P("shard", None),
        P("shard", None),
        P("shard", None),
        P("shard"),
        P("shard"),
    )
    return jax.shard_map(
        on_device, mesh=mesh, in_specs=in_specs, out_specs=out_specs, check_vma=False
    )
```

```python
import math

import jax
import jax.numpy as jnp
from jax import lax
from jax.experimental import pallas as pl
from jax.experimental.pallas import tpu as pltpu
from jax.sharding import PartitionSpec as P

HEAD = 64
RADIUS = 64
BLOCK = 128
EPSILON = 1e-05
THETA_BASE = 10000.0
NEGATIVE = -1e30
VMEM_BYTES = 24 * 1024 * 1024
VMEM_ALL = 60 * 1024 * 1024
BF = jnp.bfloat16
F32 = jnp.float32


def xor_send(array, axis, bit):
    count = lax.axis_size(axis)
    return lax.ppermute(array, axis, [(i, i ^ bit) for i in range(count)])


def bits_of(count):
    return [1 << i for i in range(count.bit_length() - 1)]


def core_send(array, bits):
    count = lax.axis_size("shard")
    return lax.ppermute(array, "shard", [(i, i ^ bits[i & 1]) for i in range(count)])


def gather_pieces(own, split, chip_bits, before=None):
    if len(chip_bits) == 2:
        x, y = chip_bits
        from_x, from_y = xor_send(own, "shard", x), xor_send(own, "shard", y)
        if before is not None:
            (from_x, from_y), _ = lax.optimization_barrier(((from_x, from_y), before))
        pieces = [(0, 2, own), (x, 2, from_x), (y, 2, from_y)]
        forward = [from_x[:, :split], from_y[:, split:]]
        pieces.append((x | y, 0, xor_send(forward[0], "shard", y)))
        pieces.append((x | y, 1, xor_send(forward[1], "shard", x)))
    else:
        streams = ([(0, 0, own[:, :split])], [(0, 1, own[:, split:])])
        for stage in range(len(chip_bits)):
            grown = []
            for which, bit in ((0, chip_bits[stage]), (1, chip_bits[-1 - stage])):
                grown.append(
                    [(j ^ bit, s, xor_send(a, "shard", bit)) for j, s, a in streams[which]]
                )
            for held, more in zip(streams, grown):
                held.extend(more)
        pieces = streams[0] + streams[1]
        forward = []
    return pieces, forward


def with_core(pieces, joined):
    rows = pieces[0][2].shape[0]
    arrays = [a for _, _, a in pieces]
    names = [(j, s, i, 0) for i, (j, s, _) in enumerate(pieces)]
    whole = [p for p in pieces if p[1] == 2]
    others = pieces[len(whole) :]
    if joined and whole:
        whole.append((others[0][0], 2, jnp.concatenate([a for _, _, a in others], axis=1)))
        others = []
    groups = ([whole] if whole else []) + [[p] for p in others]
    for group in groups:
        sent = [a for _, _, a in group]
        sent = jnp.concatenate(sent, axis=0) if len(sent) > 1 else sent[0]
        arrays.append(xor_send(sent, "shard", 1))
        names += [(p[0] ^ 1, p[1], len(arrays) - 1, i * rows) for i, p in enumerate(group)]
    return names, arrays


def add_low(left, right):
    return (left.astype(F32) + right.astype(F32)).astype(BF)


def halve(keep, other):
    middle = keep.shape[0] // 2
    return add_low(keep[middle:], other[middle:]), add_low(keep[:middle], other[:middle])


def scatter_sums(sums, chip_bits, before_add=None, before_last=None):
    send, keep = sums
    orders = list(zip(chip_bits, chip_bits[::-1]))
    for bits in orders[:-1]:
        other = core_send(send, bits)
        if before_add is not None:
            other, _ = lax.optimization_barrier((other, before_add))
        send, keep = halve(keep, other)
    if before_last is not None:
        send, _ = lax.optimization_barrier((send, before_last))
    return keep, core_send(send, orders[-1]), send


def last_sums(keep, other, _):
    middle = keep.shape[1] // 2
    return [
        add_low(keep[0, :middle], other[0, :middle]),
        add_low(keep[0, middle:], other[0, middle:]),
    ]


def side_sum(total, after=None):
    for bit in bits_of(lax.axis_size("replica"))[1:]:
        other = xor_send(total, "replica", bit)
        if after is not None:
            other, _ = lax.optimization_barrier((other, after))
        total = add_low(total, other)
    return total


def dot(left, right):
    return jnp.dot(left, right, preferred_element_type=F32)


def dot_cols(left, right):
    return lax.dot_general(left, right, (((1,), (1,)), ((), ())), preferred_element_type=F32)


def dot_rows(left, right):
    return lax.dot_general(left, right, (((0,), (0,)), ((), ())), preferred_element_type=F32)


def standardize(vector):
    average = jnp.mean(vector, axis=-1, keepdims=True)
    centred = vector - average
    spread = jnp.mean(centred * centred, axis=-1, keepdims=True)
    inverse = lax.rsqrt(spread + EPSILON)
    return centred * inverse, inverse


def norm_back(grad, gain, hat, inverse):
    dhat = grad * gain
    mean = jnp.mean(dhat, axis=-1, keepdims=True)
    along = jnp.mean(dhat * hat, axis=-1, keepdims=True)
    return (dhat - mean - hat * along) * inverse


def turned(vector):
    width = vector.shape[-1]
    lane = lax.broadcasted_iota(jnp.int32, vector.shape, 1)
    return jnp.where(
        (lane & 63) < 32, pltpu.roll(vector, width - 32, 1), pltpu.roll(vector, 32, 1)
    )


def place(me, pieces, refs, layout, sems):
    copies = []
    for j, stream, which, base in pieces:
        owner = me ^ j
        ref = refs[which]
        for row, rows, col, cols, dst, dst_col in layout[stream]:
            start = owner * rows
            if rows % 16 == 0:
                start = pl.multiple_of(start, 16)
            copy = pltpu.make_async_copy(
                ref.at[pl.ds(base + row, rows), pl.ds(col, cols)],
                dst.at[pl.ds(start, rows), pl.ds(dst_col, cols)],
                sems.at[len(copies)],
            )
            copy.start()
            copies.append(copy)
    return copies


def call(kernel, out_shape, inputs, in_any, scratch, flops, traffic, vmem_bytes=VMEM_BYTES):
    any_spec = pl.BlockSpec(memory_space=pl.ANY)
    vmem = pl.BlockSpec(memory_space=pltpu.VMEM)
    specs = [vmem] * len(inputs) + [any_spec] * len(in_any)
    return pl.pallas_call(
        kernel,
        out_shape=out_shape,
        in_specs=specs,
        out_specs=jax.tree.map(lambda _: vmem, out_shape),
        scratch_shapes=scratch,
        compiler_params=pltpu.CompilerParams(vmem_limit_bytes=vmem_bytes),
        cost_estimate=pl.CostEstimate(flops=flops, bytes_accessed=traffic, transcendentals=0),
    )(*inputs, *in_any)


def shard_at():
    return lax.axis_index("shard").astype(jnp.int32)


def side_at():
    return lax.axis_index("replica").astype(jnp.int32) & 1


def shaped(shape, dtype):
    return jax.ShapeDtypeStruct(shape, dtype)


def pack_qkv_kernel(half):
    def body(weight, attn_gain, ffn_gain, out, attn_held, ffn_held, sems):
        rows = weight.shape[0]
        first = side_at() * half
        copies = [
            pltpu.make_async_copy(attn_gain, attn_held, sems.at[0]),
            pltpu.make_async_copy(ffn_gain, ffn_held, sems.at[1]),
        ]
        for i in range(3):
            start = pl.multiple_of(i * 2 * half + first, 128)
            copies.append(
                pltpu.make_async_copy(
                    weight.at[:, pl.ds(start, half)],
                    out.at[:, pl.ds(i * half, half)],
                    sems.at[2 + i],
                )
            )
        for copy in copies:
            copy.start()
        copies[0].wait()
        copies[1].wait()
        gains = [ref[...].astype(F32) for ref in (attn_held, ffn_held)]
        gains = jnp.concatenate(gains + [jnp.zeros((6, rows), F32)], axis=0)
        gains = jnp.concatenate([gains, jnp.zeros((8, 128 - rows), F32)], axis=1)
        square = jnp.concatenate([gains, jnp.zeros((120, 128), F32)], axis=0)
        out[:, 3 * half :] = square.T[0:rows, :].astype(BF)
        for copy in copies[2:]:
            copy.wait()

    return body


def pack_mlp_kernel(count, down_rows, take):
    def body(attn, glu, down, out):
        rows, width = attn.shape
        units = count * take
        hidden = count * down_rows
        out[:, 0:width] = attn[...]
        last = width + 2 * units

        def pick(first):
            for part in range(2):
                for s in range(count):
                    at = part * hidden + s * down_rows + first
                    to = width + part * units + s * take
                    out[:, to : to + take] = glu[:, at : at + take]
            out[0:take, last:] = down[first : first + take, :]

        @pl.when(side_at() == 0)
        def _():
            pick(0)

        @pl.when(side_at() != 0)
        def _():
            pick(down_rows - take)

        if rows > take:
            out[take:, last:] = jnp.zeros((rows - take, width), BF)

    return body


def around_kernel(own, places, partner, near, far, out, cosine, sine, bias):
    def arrange(*blocks):
        for i, ref in enumerate(blocks):
            out[i * BLOCK : (i + 1) * BLOCK, :] = ref[0:BLOCK, :]

    @pl.when(side_at() == 0)
    def _():
        arrange(near, own, partner, far)

    @pl.when(side_at() != 0)
    def _():
        arrange(far, partner, own, near)

    def places_of(ref):
        first = ref.shape[0] - 16
        return ref[first : first + 1, 0:BLOCK].astype(F32) * 256.0 + ref[
            first + 1 : first + 2, 0:BLOCK
        ].astype(F32)

    mine, theirs = places[...].astype(F32), places_of(partner)
    inner, outer = places_of(near), places_of(far)
    even = side_at() == 0
    lines = [
        jnp.where(even, inner, outer),
        jnp.where(even, mine, theirs),
        jnp.where(even, theirs, mine),
        jnp.where(even, outer, inner),
    ]
    stacked = jnp.concatenate([jnp.broadcast_to(line, (BLOCK, BLOCK)).T for line in lines], axis=0)
    lane = lax.broadcasted_iota(jnp.int32, (1, 128), 1)
    power = lax.rem(lane, HEAD // 2).astype(F32) * (2.0 / HEAD)
    phases = stacked * jnp.exp(power * -math.log(THETA_BASE))
    cosine[...] = jnp.cos(phases)
    sine[...] = jnp.where((lane & 63) < 32, -1.0, 1.0) * jnp.sin(phases)
    offset = (
        lax.broadcasted_iota(jnp.int32, (BLOCK, 2 * BLOCK), 1)
        - RADIUS
        - lax.broadcasted_iota(jnp.int32, (BLOCK, 2 * BLOCK), 0)
    )
    distance = offset.astype(F32)
    for b in range(3):
        start = RADIUS + b * BLOCK
        key = jnp.concatenate([lines[b], lines[b + 1]], axis=1)
        query = jnp.concatenate([stacked[start : start + BLOCK, :]] * 2, axis=1)
        later = jnp.where(offset >= 0, key - distance, query + distance)
        allowed = (jnp.abs(offset) <= RADIUS) & (later >= 0.0)
        bias[b * BLOCK : (b + 1) * BLOCK, :] = jnp.where(allowed, 0.0, NEGATIVE)


def around_back_kernel(own, partner, near, far, out):
    def arrange(before, first, second, after):
        out[0:RADIUS, :] = before[...]
        out[RADIUS : RADIUS + BLOCK, :] = first
        out[RADIUS + BLOCK : RADIUS + 2 * BLOCK, :] = second
        out[RADIUS + 2 * BLOCK :, :] = after[...]

    theirs = partner[...]

    @pl.when(side_at() == 0)
    def _():
        arrange(near, own[...], theirs, far)

    @pl.when(side_at() != 0)
    def _():
        arrange(far, theirs, own[...], near)


def qkv_layout(rows, half, weight, gains=None):
    wide = 3 * half
    split = (wide + 128) // 2
    streams = [[(0, rows, 0, split, weight, 0)], [(0, rows, 0, wide - split, weight, split)]]
    streams.append([(0, rows, 0, wide, weight, 0)])
    if gains is not None:
        streams[1].append((0, rows, wide - split, 128, gains, 0))
        streams[2].append((0, rows, wide, 128, gains, 0))
    return streams


def project_kernel(pieces, n_refs, rows, width, skip):
    half = width // 2
    span = 4 * BLOCK

    def body(tok, cosine, sine, bias, *rest):
        refs, rest = rest[skip : n_refs + skip], rest[n_refs + skip :]
        q_out, k_out, v_out, p_out, ctx_out, normed_out, gains_out = rest[:7]
        weight, gain_cols, normed, sems = rest[7:]
        layout = qkv_layout(rows, half, weight, gain_cols)
        copies = place(shard_at(), pieces, refs, layout, sems)
        hats = [
            standardize(tok[i * BLOCK : (i + 1) * BLOCK, :].astype(F32))[0] for i in range(4)
        ]
        for copy in copies:
            copy.wait()
        pick = jnp.where(
            lax.broadcasted_iota(jnp.int32, (8, 128), 0)
            == lax.broadcasted_iota(jnp.int32, (8, 128), 1),
            1.0,
            0.0,
        ).astype(BF)
        gains = dot_cols(pick, gain_cols[...])
        gains_out[...] = gains
        for i, hat in enumerate(hats):
            normed[i * BLOCK : (i + 1) * BLOCK, :] = (hat * gains[0:1]).astype(BF)
        normed_out[...] = normed[BLOCK : 3 * BLOCK, :]
        cos3 = jnp.concatenate([cosine[...]] * 3, axis=1)
        sin3 = jnp.concatenate([sine[...]] * 3, axis=1)
        mid = slice(RADIUS, span - RADIUS)
        joined = dot(normed[mid, :], weight[:, 0:half])
        q_out[...] = (joined * cos3[mid] + turned(joined) * sin3[mid]).astype(BF)
        joined = dot(normed[...], weight[:, half : 2 * half])
        k_out[...] = (joined * cos3 + turned(joined) * sin3).astype(BF)
        v_out[...] = dot(normed[...], weight[:, 2 * half : 3 * half]).astype(BF)
        lane = lax.broadcasted_iota(jnp.int32, (BLOCK, 128), 1)
        scale = 1.0 / math.sqrt(HEAD)
        for pair in range(half // 128):
            cols = slice(pair * 128, pair * 128 + 128)
            for b in range(3):
                rows_q = slice(b * BLOCK, (b + 1) * BLOCK)
                rows_k = slice(b * BLOCK, (b + 2) * BLOCK)
                queries, keys, values = q_out[rows_q, cols], k_out[rows_k, cols], v_out[rows_k, cols]
                parts = []
                for h in range(2):
                    mine = (lane < HEAD) if h == 0 else (lane >= HEAD)
                    masked = jnp.where(mine, queries.astype(F32) * scale, 0.0).astype(BF)
                    scores = dot_cols(masked, keys) + bias[rows_q, :]
                    exponent = jnp.exp(scores - jnp.max(scores, axis=1, keepdims=True))
                    total = jnp.sum(exponent, axis=1, keepdims=True)
                    shares = (exponent * (1.0 / total)).astype(BF)
                    p_out[(pair * 2 + h) * 3 + b] = shares
                    parts.append(dot(shares, values))
                ctx_out[rows_q, cols] = jnp.where(lane < HEAD, parts[0], parts[1]).astype(BF)

    return body


def attn_layout(rows, width, attn):
    parts = [(0, rows, 0, width, attn, 0)]
    return (parts, (), parts)


def mlp_layout(rows, take, width, units, glu, down):
    gate = (0, rows, width, units, glu, 0)
    up = (0, rows, 0, units, glu, units)
    low = (0, take, units, width, down, 0)
    whole = ((0, rows, width, 2 * units, glu, 0), (0, take, width + 2 * units, width, down, 0))
    return ((gate,), (up, low), whole)


def mlp_kernel(pieces, n_refs, rows, down_rows, take, width, units):
    half = width // 2
    pair = slice(RADIUS, RADIUS + 2 * BLOCK)

    def body(tok, ctx_own, ctx_other, dy, gains, *rest):
        refs, rest = rest[1 : n_refs + 1], rest[n_refs + 1 :]
        mix_keep, mix_send, shared, ctx_pair, hidden, gn_out = rest[:6]
        attn, glu, down, ggu, mix, attn_sems, sems = rest[6:]
        first = place(shard_at(), pieces, refs, attn_layout(rows, width, attn), attn_sems)
        layout = mlp_layout(rows, take, width, units, glu, down)
        copies = place(shard_at(), pieces, refs, layout, sems)
        at = side_at()
        inputs = tok[RADIUS : RADIUS + 3 * BLOCK, :].astype(F32)
        own_rows = pl.ds(pl.multiple_of(at * half, 128), half)
        other_rows = pl.ds(pl.multiple_of((1 - at) * half, 128), half)

        @pl.when(at == 0)
        def _():
            ctx_pair[:, 0:half] = ctx_own[pair, :]
            ctx_pair[:, half:] = ctx_other[pair, :]

        @pl.when(at != 0)
        def _():
            ctx_pair[:, 0:half] = ctx_other[pair, :]
            ctx_pair[:, half:] = ctx_own[pair, :]

        for copy in first:
            copy.wait()
        lifted = dot(ctx_own[...], attn[own_rows, :]) + dot(ctx_other[...], attn[other_rows, :])
        hidden[...] = inputs + lifted
        hat, _ = standardize(hidden[...])
        normed = (hat * gains[1:2, :]).astype(BF)
        shared[:, 0:width] = normed[pair]
        for copy in copies:
            copy.wait()
        partial = jnp.zeros((2 * BLOCK, width), F32)
        unit = lax.rem(lax.broadcasted_iota(jnp.int32, (1, units), 1), take)
        mask = jnp.where(unit >= at * (2 * take - down_rows), 1.0, 0.0)
        for c in range(0, units, 256):
            wide = min(256, units - c)
            cols = slice(c, c + wide)
            gate = dot(normed, glu[:, cols])
            up = dot(normed, glu[:, units + c : units + c + wide])
            grad_act = dot_cols(dy[...], down[cols, :]) * mask[:, cols]
            share = 0.5 * (1.0 + lax.erf(gate * (1.0 / math.sqrt(2.0))))
            density = jnp.exp(-0.5 * gate * gate) * (1.0 / math.sqrt(2.0 * math.pi))
            gelu = gate * share
            act = (gelu[pair] * up[pair] * mask[:, cols]).astype(BF)
            shared[:, width + c : width + c + wide] = act
            partial = partial + dot(act, down[cols, :])
            ggu[:, cols] = (grad_act * up * (share + gate * density)).astype(BF)
            ggu[:, units + c : units + c + wide] = (grad_act * gelu).astype(BF)
        mix[...] = partial
        mine = pl.ds(pl.multiple_of(at * BLOCK, BLOCK), BLOCK)
        theirs = pl.ds(pl.multiple_of((1 - at) * BLOCK, BLOCK), BLOCK)
        mix_keep[...] = mix[mine, :] + hidden[pl.ds(pl.multiple_of(RADIUS + at * BLOCK, 8), BLOCK), :]
        mix_send[...] = mix[theirs, :].astype(BF)
        shared[:, width + units :] = ggu[pair, :]
        grad = dot_cols(ggu[...], glu[...])
        gn_out[...] = grad.astype(BF)

    return body


def pair_back(pair, gctx, q, k, v, p, cos, sin):
    lane = lax.broadcasted_iota(jnp.int32, (BLOCK, 128), 1)
    lane2 = lax.broadcasted_iota(jnp.int32, (2 * BLOCK, 128), 1)
    scale = 1.0 / math.sqrt(HEAD)
    cols = slice(pair * 128, pair * 128 + 128)
    first, second = slice(0, BLOCK), slice(BLOCK, 2 * BLOCK)
    low, high = slice(0, RADIUS), slice(RADIUS, BLOCK)
    grad_q = jnp.zeros((2 * BLOCK, 128), F32)
    grad_k, grad_v = [0.0, 0.0], [0.0, 0.0]
    for h in range(2):
        mine = (lane < HEAD) if h == 0 else (lane >= HEAD)
        mine2 = (lane2 < HEAD) if h == 0 else (lane2 >= HEAD)
        scores, shares, queries, grads, parts = [], [], [], [], []
        for b in range(3):
            rows_q = slice(b * BLOCK, (b + 1) * BLOCK)
            rows_k = slice(b * BLOCK, (b + 2) * BLOCK)
            keys, values = k[rows_k, cols], v[rows_k, cols]
            lowered = jnp.where(mine, gctx[rows_q, cols].astype(F32), 0.0).astype(BF)
            query = jnp.where(mine, q[rows_q, cols].astype(F32) * scale, 0.0).astype(BF)
            share = p[(pair * 2 + h) * 3 + b]
            wide = share.astype(F32)
            grad_share = dot_cols(lowered, values)
            row = jnp.sum(wide * grad_share, axis=1, keepdims=True)
            grad_score = (wide * (grad_share - row)).astype(BF)
            scores.append(grad_score)
            shares.append(share)
            queries.append(query)
            grads.append(lowered)
            part = (high, first, low)[b]
            parts.append(dot(grad_score[part], keys))
        grad_q = grad_q + jnp.where(mine2, jnp.concatenate(parts, axis=0) * scale, 0.0)
        for i in range(2):
            two = slice(i, i + 2)
            for total, left, right in ((grad_k, scores, queries), (grad_v, shares, grads)):
                upper, lower = left[i][:, second], left[i + 1][:, first]
                total[i] = total[i] + dot_rows(
                    jnp.concatenate([upper, lower], axis=0), jnp.concatenate(right[two], axis=0)
                )
    grad_k, grad_v = jnp.concatenate(grad_k, axis=0), jnp.concatenate(grad_v, axis=0)
    return (
        (grad_q * cos - turned(grad_q) * sin).astype(BF),
        (grad_k * cos - turned(grad_k) * sin).astype(BF),
        grad_v.astype(BF),
    )


def hidden_back_kernel(mlp_pieces, n_mlp, rows, width):
    half = width // 2
    pair = slice(RADIUS, RADIUS + 2 * BLOCK)

    def body(gn_own, gn_other, hidden, dy, gains, q, k, v, p, cosine, sine, *rest):
        mlp_refs, rest = rest[1 : n_mlp + 1], rest[n_mlp + 1 :]
        ghid_out, halves_out, gctx, first_out, attn, held, attn_sems = rest
        copies = place(shard_at(), mlp_pieces, mlp_refs, attn_layout(rows, width, attn), attn_sems)
        at = side_at()
        hat, inverse = standardize(hidden[...])
        grad = gn_own[...].astype(F32) + gn_other[...].astype(F32)
        grad_hidden = dy[...].astype(F32) + norm_back(grad, gains[1:2, :], hat, inverse)
        held[...] = grad_hidden[pair]
        ghid_out[...] = held[pl.ds(pl.multiple_of(at * BLOCK, BLOCK), BLOCK), :]
        halves = jnp.where(at == 0, grad_hidden[pair, 0:half], grad_hidden[pair, half:])
        halves_out[...] = halves.astype(BF)
        grad_low = grad_hidden.astype(BF)
        for copy in copies:
            copy.wait()
        own_rows = pl.ds(pl.multiple_of(at * half, 128), half)
        gctx[...] = dot_cols(grad_low, attn[own_rows, :]).astype(BF)
        cos, sin = cosine[BLOCK : 3 * BLOCK, :], sine[BLOCK : 3 * BLOCK, :]
        for part, grad in enumerate(pair_back(0, gctx, q, k, v, p, cos, sin)):
            first_out[:, part * 128 : (part + 1) * 128] = grad

    return body


def back_kernel(width):
    half = width // 2

    def body(first, halves, gctx, q, k, v, p, cosine, sine, sent, mixed, gj_out):
        gj_out[:, 3 * half :] = halves[...]
        cos, sin = cosine[BLOCK : 3 * BLOCK, :], sine[BLOCK : 3 * BLOCK, :]
        for part in range(3):
            gj_out[:, part * half : part * half + 128] = first[:, part * 128 : (part + 1) * 128]
        for i in range(1, half // 128):
            for part, grad in enumerate(pair_back(i, gctx, q, k, v, p, cos, sin)):
                col = part * half + i * 128
                gj_out[:, col : col + 128] = grad

    return body


def norm_back_kernel(pieces, n_refs, rows, width):
    half = width // 2

    def body(gj, *rest):
        refs, rest = rest[:n_refs], rest[n_refs:]
        keep_out, send_out, weight, held, sems = rest
        copies = place(shard_at(), pieces, refs, qkv_layout(rows, half, weight), sems)
        at = side_at()
        for copy in copies:
            copy.wait()
        held[...] = dot_cols(gj[:, 0 : 3 * half], weight[...])
        keep_out[...] = held[pl.ds(pl.multiple_of(at * BLOCK, BLOCK), BLOCK), :]
        theirs = pl.ds(pl.multiple_of((1 - at) * BLOCK, BLOCK), BLOCK)
        send_out[...] = held[theirs, :].astype(BF)

    return body


def final_kernel(tok, keep, other, ghid, gains, out):
    hat, inverse = standardize(tok[...].astype(F32))
    grad = keep[...] + other[...].astype(F32)
    out[...] = (ghid[...] + norm_back(grad, gains[0:1, :], hat, inverse)).astype(BF)


def slots_of(chip_bits):
    tables = []
    for order in (chip_bits, chip_bits[::-1]):
        kept = [0]
        for bit in order[1:][::-1]:
            kept = kept + [j | bit for j in kept]
        tables.append([(1, i, j) for i, j in enumerate(kept)])
        tables[-1] += [(0, i, j | order[0]) for i, j in enumerate(kept)]
    return [(kept, i, j, k) for (kept, i, j), (_, _, k) in zip(*tables)]


def owner_rows(me, slots, lhs_t, rows):
    parts = []
    for _, _, even, odd in slots:
        owner = me ^ jnp.where((me & 1) == 0, even, odd)
        parts.append(lhs_t[pl.ds(pl.multiple_of(owner * rows, 16), rows), :])
    return jnp.concatenate(parts, axis=0)


def emit(outs, slots, rows, grad, start):
    grad = grad.astype(BF)
    for i, (kept, at, _, _) in enumerate(slots):
        for c in range(grad.shape[1] // 128):
            row = start + c * rows
            outs[kept][at, row : row + rows, :] = grad[
                i * rows : (i + 1) * rows, c * 128 : (c + 1) * 128
            ]


def mlp_grad_kernel(slots, rows, take, width, units):
    half = width // 2

    def body(own, other, dy_own, dy_other, *rest):
        outs, (normed_t, act_t, ggu, dy) = rest[1:3], rest[3:]
        me = shard_at()
        pair = slice(RADIUS, RADIUS + 2 * BLOCK)
        for i, (ref, dref) in enumerate(((own, dy_own), (other, dy_other))):
            tok = slice(i * 2 * BLOCK, (i + 1) * 2 * BLOCK)
            normed_t[:, tok] = ref[:, 0:width].T
            act_t[:, tok] = ref[:, width : width + units].T
            ggu[tok, :] = ref[:, width + units :]
            dy[tok, :] = dref[pair, :]
        left = owner_rows(me, slots, normed_t, rows)
        act = owner_rows(me, slots, act_t, take)
        height = outs[0].shape[1] // 2
        for s in range(2):
            grad = dot(left, ggu[:, s * units : (s + 1) * units])
            emit(outs, slots, rows, grad, s * height)
            grad = dot(act, dy[:, s * half : (s + 1) * half])
            emit(outs, slots, take, grad, s * height + rows * (units // 128))

    return body


def qkv_grad_kernel(slots, rows, width):
    half = width // 2

    def body(normed_own, normed_other, ctx_own, ctx_other, own, other, *rest):
        outs, (normed_t, ctx_t, gj) = rest[1:3], rest[3:]
        me = shard_at()
        count = 2 * BLOCK
        each = ((normed_own, ctx_own, own), (normed_other, ctx_other, other))
        for i, (nref, cref, ref) in enumerate(each):
            tok = slice(i * count, (i + 1) * count)
            normed_t[:, tok] = nref[...].T
            ctx_t[:, tok] = cref[...].T
            gj[tok, :] = ref[...]
        left = owner_rows(me, slots, normed_t, rows)
        ctx = owner_rows(me, slots, ctx_t, rows)
        emit(outs, slots, rows, dot(left, gj[:, 0 : 3 * half]), 0)
        emit(outs, slots, rows, dot(ctx, gj[:, 3 * half :]), 9 * rows)

    return body


def gain_grad(weight, grad, gain):
    total = jnp.sum(weight[...].astype(F32) * grad[...], axis=1, keepdims=True)
    rows = total.shape[0]
    total = jnp.concatenate([total, jnp.zeros((128 - rows, 1), F32)], axis=0)
    return jnp.broadcast_to(total, (128, 128)).T[0:1, 0:rows] / gain[...].astype(F32)


def mlp_unpack_kernel(rows, down_rows, take, width, units, count):
    hidden = count * down_rows
    spare = 2 * take - down_rows

    def body(mine_0, mine_1, other_0, other_1, weight, gain, sent, glu, down, gain_out, held, wide):
        at = side_at()
        tiles = units // 128
        for s, (mine, other) in enumerate(((mine_0, other_0), (mine_1, other_1))):
            held[at, s] = mine[...].astype(F32)
            held[1 - at, s] = other[...].astype(F32)
        for s in range(2):
            for t in range(2):
                for c in range(tiles):
                    row = c * rows
                    wide[:, c * 128 : (c + 1) * 128] = held[t, s, row : row + rows, :]
                skip = 0 if t == 0 else spare
                for i in range(count):
                    col = s * hidden + i * down_rows + t * take
                    glu[:, col : col + take - skip] = wide[:, i * take + skip : (i + 1) * take]
                for c in range(width // 256):
                    row = tiles * rows + c * take
                    col = s * (width // 2) + c * 128
                    down[t * take : (t + 1) * take - skip, col : col + 128] = held[
                        t, s, row + skip : row + take, :
                    ]
        gain_out[...] = gain_grad(weight, glu, gain)

    return body


def qkv_unpack_kernel(rows, width):
    half = width // 2
    tiles = half // 128

    def body(mine_0, mine_1, other_0, other_1, weight, gain, qkv, attn, gain_out, held):
        at = side_at()
        for s, (mine, other) in enumerate(((mine_0, other_0), (mine_1, other_1))):
            held[at, s] = mine[...].astype(F32)
            held[1 - at, s] = other[...].astype(F32)
        for t in range(2):
            for i in range(3):
                for c in range(tiles):
                    row = (i % 2 * tiles + c) * rows
                    col = i * width + t * half + c * 128
                    qkv[:, col : col + 128] = held[t, i // 2, row : row + rows, :]
            for c in range(tiles):
                row = (tiles + c) * rows
                attn[:, t * half + c * 128 : t * half + (c + 1) * 128] = held[t, 1, row : row + rows, :]
        gain_out[...] = gain_grad(weight, qkv, gain)

    return body


def on_device(
    tokens,
    positions,
    qkv_weight,
    attn_weight,
    glu_weight,
    down_weight,
    attn_gain,
    ffn_gain,
    cotangent,
):
    block, width = tokens.shape
    half = width // 2
    rows, down_rows = qkv_weight.shape[0], down_weight.shape[0]
    count, replicas = lax.axis_size("shard"), lax.axis_size("replica")
    everyone = count * replicas
    take = -(-down_rows // 32) * 16
    units = count * take
    me = lax.axis_index("shard").astype(jnp.int32)
    side = lax.axis_index("replica").astype(jnp.int32) & 1
    chip_bits = bits_of(count)[1:]

    own = call(
        pack_qkv_kernel(half),
        shaped((rows, 3 * half + 128), BF),
        (),
        [qkv_weight, attn_gain[None], ffn_gain[None]],
        [
            pltpu.VMEM((1, rows), BF),
            pltpu.VMEM((1, rows), BF),
            pltpu.SemaphoreType.DMA((5,)),
        ],
        1_000_000,
        1_000_000,
        VMEM_ALL,
    )

    places = jnp.stack([positions >> 8, positions & 255]).astype(BF)
    places = jnp.pad(places, ((0, 14), (0, width - block)))
    rim = jnp.concatenate([tokens, places], axis=0)
    rim, _ = lax.optimization_barrier((rim, own))
    step = [1 if i & 1 else -1 for i in range(everyone)]
    both = ("shard", "replica")

    def outward(array):
        moves = [(i, i + step[i]) for i in range(everyone)]
        return lax.ppermute(array, both, [(a, b) for a, b in moves if 0 <= b < everyone])

    own_mlp = call(
        pack_mlp_kernel(count, down_rows, take),
        shaped((rows, 2 * width + 2 * units), BF),
        (attn_weight, glu_weight, down_weight),
        [],
        [],
        1_000_000,
        2_000_000,
    )
    qkv_parts, _ = gather_pieces(
        own, (3 * half + 128) // 2, chip_bits, rim
    )
    near, partner = outward(rim), xor_send(rim, "replica", 1)
    arrived = [a for _, _, a in qkv_parts]
    own, near, partner, arrived = lax.optimization_barrier((own_mlp, near, partner, arrived))
    qkv_parts = [(j, s, a) for (j, s, _), a in zip(qkv_parts, arrived)]
    far = xor_send(near, "replica", 1)
    mlp_parts, forward = gather_pieces(own, width + units, chip_bits)

    tok, cosine, sine, bias = call(
        around_kernel,
        (
            shaped((4 * BLOCK, width), BF),
            shaped((4 * BLOCK, 128), F32),
            shaped((4 * BLOCK, 128), F32),
            shaped((3 * BLOCK, 2 * BLOCK), F32),
        ),
        (tokens, positions[None], partner, near, far),
        [],
        [],
        1_000_000,
        2_000_000,
    )
    rim = jnp.where(side == 0, cotangent[:RADIUS], cotangent[block - RADIUS :])
    rim, _ = lax.optimization_barrier((rim, near))
    near_dy = outward(rim)
    sent, near_dy = lax.optimization_barrier((cotangent, near_dy))
    partner_dy = xor_send(sent, "replica", 1)
    far_dy = xor_send(near_dy, "replica", 1)
    qkv_names, qkv_arrays = with_core(qkv_parts, True)
    weight_bytes = width * 3 * width * 2

    q, k, v, p, ctx, normed, gains = call(
        project_kernel(qkv_names, len(qkv_arrays), rows, width, 2 + len(forward)),
        (
            shaped((3 * BLOCK, half), BF),
            shaped((4 * BLOCK, half), BF),
            shaped((4 * BLOCK, half), BF),
            shaped((3 * half // HEAD, BLOCK, 2 * BLOCK), BF),
            shaped((3 * BLOCK, half), BF),
            shaped((2 * BLOCK, width), BF),
            shaped((8, width), F32),
        ),
        (tok, cosine, sine, bias),
        [far_dy, partner_dy] + forward + qkv_arrays,
        [
            pltpu.VMEM((width, 3 * half), BF),
            pltpu.VMEM((width, 128), BF),
            pltpu.VMEM((4 * BLOCK, width), BF),
            pltpu.SemaphoreType.DMA((2 * len(qkv_names),)),
        ],
        7_000_000_000,
        weight_bytes,
    )
    ctx_other = xor_send(ctx, "replica", 1)
    normed_other = xor_send(normed, "shard", 1)
    near_dy, far_dy, partner_dy, _ = lax.optimization_barrier(
        (near_dy, far_dy, partner_dy, ctx)
    )
    dy = call(
        around_back_kernel,
        shaped((3 * BLOCK, width), BF),
        (cotangent, partner_dy, near_dy, far_dy),
        [],
        [],
        1_000_000,
        2_000_000,
    )
    dy_other = xor_send(dy, "shard", 1)
    held, _ = lax.optimization_barrier(([a for _, _, a in mlp_parts], ctx))
    mlp_parts = [(j, s, a) for (j, s, _), a in zip(mlp_parts, held)]
    names, arrays = with_core(mlp_parts, False)

    mix_keep, mix_send, shared, ctx_pair, hidden, gn = call(
        mlp_kernel(names, len(arrays), rows, down_rows, take, width, units),
        (
            shaped((BLOCK, width), F32),
            shaped((BLOCK, width), BF),
            shaped((2 * BLOCK, width + 3 * units), BF),
            shaped((2 * BLOCK, width), BF),
            shaped((3 * BLOCK, width), F32),
            shaped((3 * BLOCK, width), BF),
        ),
        (tok, ctx, ctx_other, dy, gains),
        [normed_other] + arrays,
        [
            pltpu.VMEM((width, width), BF),
            pltpu.VMEM((width, 2 * units), BF),
            pltpu.VMEM((units, width), BF),
            pltpu.VMEM((3 * BLOCK, 2 * units), BF),
            pltpu.VMEM((2 * BLOCK, width), F32),
            pltpu.SemaphoreType.DMA((len(names),)),
            pltpu.SemaphoreType.DMA((2 * len(names),)),
        ],
        8_000_000_000,
        2 * weight_bytes,
    )
    gn_other = xor_send(gn, "replica", 1)
    shared_other = xor_send(shared, "shard", 1)
    ctx_pair_other = xor_send(ctx_pair, "shard", 1)

    slots = slots_of(chip_bits)
    portion = count // 4

    def stack(height):
        return (shaped((portion, 2 * height, 128), BF),) * 2

    height = rows * (units // 128) + take * (half // 128)
    sums = call(
        mlp_grad_kernel(slots, rows, take, width, units),
        stack(height),
        (shared, shared_other, dy, dy_other),
        [ctx_pair_other],
        [
            pltpu.VMEM((width, 4 * BLOCK), BF),
            pltpu.VMEM((units, 4 * BLOCK), BF),
            pltpu.VMEM((4 * BLOCK, 2 * units), BF),
            pltpu.VMEM((4 * BLOCK, width), BF),
        ],
        4_000_000_000,
        weight_bytes,
    )

    ghid, halves, gctx, gj_first = call(
        hidden_back_kernel(names, len(arrays), rows, width),
        (
            shaped((BLOCK, width), F32),
            shaped((2 * BLOCK, half), BF),
            shaped((3 * BLOCK, half), BF),
            shaped((2 * BLOCK, 3 * 128), BF),
        ),
        (gn, gn_other, hidden, dy, gains, q, k, v, p, cosine, sine),
        [sums[1]] + arrays,
        [
            pltpu.VMEM((width, width), BF),
            pltpu.VMEM((2 * BLOCK, width), F32),
            pltpu.SemaphoreType.DMA((len(names),)),
        ],
        5_000_000_000,
        weight_bytes,
    )
    mlp_sums = scatter_sums(sums, chip_bits, gctx)
    mix_other = xor_send(mix_send, "replica", 1)
    gj = call(
        back_kernel(width),
        shaped((2 * BLOCK, 4 * half), BF),
        (gj_first, halves, gctx, q, k, v, p, cosine, sine),
        [mlp_sums[2], mix_other],
        [],
        6_000_000_000,
        weight_bytes,
    )
    gj_other = xor_send(gj, "shard", 1)
    norm_keep, norm_send = call(
        norm_back_kernel(qkv_names, len(qkv_arrays), rows, width),
        (shaped((BLOCK, width), F32), shaped((BLOCK, width), BF)),
        (gj,),
        qkv_arrays,
        [
            pltpu.VMEM((width, 3 * half), BF),
            pltpu.VMEM((2 * BLOCK, width), F32),
            pltpu.SemaphoreType.DMA((len(qkv_names),)),
        ],
        3_000_000_000,
        weight_bytes,
    )
    sums = call(
        qkv_grad_kernel(slots, rows, width),
        stack(6 * rows),
        (normed, normed_other, ctx_pair, ctx_pair_other, gj, gj_other),
        [norm_keep],
        [
            pltpu.VMEM((width, 4 * BLOCK), BF),
            pltpu.VMEM((width, 4 * BLOCK), BF),
            pltpu.VMEM((4 * BLOCK, 4 * half), BF),
        ],
        3_000_000_000,
        weight_bytes,
    )
    mlp_sums, _ = lax.optimization_barrier((mlp_sums, sums[1]))
    mlp_sums = last_sums(*mlp_sums)
    norm_send, _ = lax.optimization_barrier((norm_send, sums[1]))
    norm_other = xor_send(norm_send, "replica", 1)
    mixed = (mix_keep + mix_other.astype(F32)).astype(BF)
    grad_tokens = call(
        final_kernel,
        shaped((block, width), BF),
        (tokens, norm_keep, norm_other, ghid, gains),
        [],
        [],
        1_000_000,
        1_000_000,
    )
    qkv_sums = scatter_sums(sums, chip_bits, (mixed, grad_tokens))
    mlp_mine = [side_sum(part, qkv_sums[2]) for part in mlp_sums]
    mlp_other = [xor_send(part, "replica", 1) for part in mlp_mine]
    sent = qkv_sums[1]
    grad_glu, grad_down, grad_ffn_gain = call(
        mlp_unpack_kernel(rows, down_rows, take, width, units, count),
        (
            shaped((rows, 2 * count * down_rows), F32),
            shaped((down_rows, width), F32),
            shaped((1, rows), F32),
        ),
        (*mlp_mine, *mlp_other, glu_weight, ffn_gain[None]),
        [sent],
        [pltpu.VMEM((2, 2, height, 128), F32), pltpu.VMEM((rows, units), F32)],
        1_000_000,
        4_000_000,
    )
    done = grad_glu
    qkv_mine = [side_sum(part, done) for part in last_sums(*qkv_sums)]
    qkv_other = [xor_send(part, "replica", 1) for part in qkv_mine]
    grad_qkv, grad_attn, grad_attn_gain = call(
        qkv_unpack_kernel(rows, width),
        (
            shaped((rows, 3 * width), F32),
            shaped((rows, width), F32),
            shaped((1, rows), F32),
        ),
        (*qkv_mine, *qkv_other, qkv_weight, attn_gain[None]),
        [],
        [pltpu.VMEM((2, 2, 6 * rows, 128), F32)],
        1_000_000,
        4_000_000,
    )
    return (
        mixed,
        grad_tokens,
        grad_qkv,
        grad_attn,
        grad_glu,
        grad_down,
        grad_attn_gain.reshape(rows),
        grad_ffn_gain.reshape(rows),
    )


def solution(mesh):
    in_specs = (
        P(("shard", "replica"), None),
        P(("shard", "replica")),
        P("shard", None),
        P("shard", None),
        P("shard", None),
        P("shard", None),
        P("shard"),
        P("shard"),
        P(("shard", "replica"), None),
    )
    out_specs = (
        P(("shard", "replica"), None),
        P(("shard", "replica"), None),
        P("shard", None),
        P("shard", None),
        P("shard", None),
        P("shard", None),
        P("shard"),
        P("shard"),
    )
    return jax.shard_map(
        on_device, mesh=mesh, in_specs=in_specs, out_specs=out_specs, check_vma=False
    )
```

```python
import math

import jax
import jax.numpy as jnp
from jax import lax
from jax.experimental import pallas as pl
from jax.experimental.pallas import tpu as pltpu
from jax.sharding import PartitionSpec as P

HEAD = 64
RADIUS = 64
BLOCK = 128
EPSILON = 1e-05
THETA_BASE = 10000.0
NEGATIVE = -1e30
VMEM_BYTES = 24 * 1024 * 1024
VMEM_ALL = 60 * 1024 * 1024
BF = jnp.bfloat16
F32 = jnp.float32


def xor_send(array, axis, bit):
    count = lax.axis_size(axis)
    return lax.ppermute(array, axis, [(i, i ^ bit) for i in range(count)])


def bits_of(count):
    return [1 << i for i in range(count.bit_length() - 1)]


def core_send(array, bits):
    count = lax.axis_size("shard")
    return lax.ppermute(array, "shard", [(i, i ^ bits[i & 1]) for i in range(count)])


def gather_pieces(own, split, chip_bits, before=None):
    if len(chip_bits) == 2:
        x, y = chip_bits
        from_x, from_y = xor_send(own, "shard", x), xor_send(own, "shard", y)
        if before is not None:
            (from_x, from_y), _ = lax.optimization_barrier(((from_x, from_y), before))
        pieces = [(0, 2, own), (x, 2, from_x), (y, 2, from_y)]
        forward = [from_x[:, :split], from_y[:, split:]]
        pieces.append((x | y, 0, xor_send(forward[0], "shard", y)))
        pieces.append((x | y, 1, xor_send(forward[1], "shard", x)))
    else:
        streams = ([(0, 0, own[:, :split])], [(0, 1, own[:, split:])])
        for stage in range(len(chip_bits)):
            grown = []
            for which, bit in ((0, chip_bits[stage]), (1, chip_bits[-1 - stage])):
                grown.append(
                    [(j ^ bit, s, xor_send(a, "shard", bit)) for j, s, a in streams[which]]
                )
            for held, more in zip(streams, grown):
                held.extend(more)
        pieces = streams[0] + streams[1]
        forward = []
    return pieces, forward


def with_core(pieces, joined):
    rows = pieces[0][2].shape[0]
    arrays = [a for _, _, a in pieces]
    names = [(j, s, i, 0) for i, (j, s, _) in enumerate(pieces)]
    whole = [p for p in pieces if p[1] == 2]
    others = pieces[len(whole) :]
    if joined and whole:
        whole.append((others[0][0], 2, jnp.concatenate([a for _, _, a in others], axis=1)))
        others = []
    groups = ([whole] if whole else []) + [[p] for p in others]
    for group in groups:
        sent = [a for _, _, a in group]
        sent = jnp.concatenate(sent, axis=0) if len(sent) > 1 else sent[0]
        arrays.append(xor_send(sent, "shard", 1))
        names += [(p[0] ^ 1, p[1], len(arrays) - 1, i * rows) for i, p in enumerate(group)]
    return names, arrays


def add_low(left, right):
    return (left.astype(F32) + right.astype(F32)).astype(BF)


def halve(keep, other):
    middle = keep.shape[0] // 2
    return add_low(keep[middle:], other[middle:]), add_low(keep[:middle], other[:middle])


def scatter_sums(sums, chip_bits, before_add=None, before_last=None):
    send, keep = sums
    orders = list(zip(chip_bits, chip_bits[::-1]))
    for bits in orders[:-1]:
        other = core_send(send, bits)
        if before_add is not None:
            other, _ = lax.optimization_barrier((other, before_add))
        send, keep = halve(keep, other)
    if before_last is not None:
        send, _ = lax.optimization_barrier((send, before_last))
    return keep, core_send(send, orders[-1]), send


def last_sums(keep, other, _):
    middle = keep.shape[1] // 2
    return [
        add_low(keep[0, :middle], other[0, :middle]),
        add_low(keep[0, middle:], other[0, middle:]),
    ]


def side_sum(total, after=None):
    for bit in bits_of(lax.axis_size("replica"))[1:]:
        other = xor_send(total, "replica", bit)
        if after is not None:
            other, _ = lax.optimization_barrier((other, after))
        total = add_low(total, other)
    return total


def dot(left, right):
    return jnp.dot(left, right, preferred_element_type=F32)


def dot_cols(left, right):
    return lax.dot_general(left, right, (((1,), (1,)), ((), ())), preferred_element_type=F32)


def dot_rows(left, right):
    return lax.dot_general(left, right, (((0,), (0,)), ((), ())), preferred_element_type=F32)


def standardize(vector):
    average = jnp.mean(vector, axis=-1, keepdims=True)
    centred = vector - average
    spread = jnp.mean(centred * centred, axis=-1, keepdims=True)
    inverse = lax.rsqrt(spread + EPSILON)
    return centred * inverse, inverse


def norm_back(grad, gain, hat, inverse):
    dhat = grad * gain
    mean = jnp.mean(dhat, axis=-1, keepdims=True)
    along = jnp.mean(dhat * hat, axis=-1, keepdims=True)
    return (dhat - mean - hat * along) * inverse


def turned(vector):
    width = vector.shape[-1]
    lane = lax.broadcasted_iota(jnp.int32, vector.shape, 1)
    return jnp.where(
        (lane & 63) < 32, pltpu.roll(vector, width - 32, 1), pltpu.roll(vector, 32, 1)
    )


def place(me, pieces, refs, layout, sems):
    copies = []
    for j, stream, which, base in pieces:
        owner = me ^ j
        ref = refs[which]
        for row, rows, col, cols, dst, dst_col in layout[stream]:
            start = owner * rows
            if rows % 16 == 0:
                start = pl.multiple_of(start, 16)
            copy = pltpu.make_async_copy(
                ref.at[pl.ds(base + row, rows), pl.ds(col, cols)],
                dst.at[pl.ds(start, rows), pl.ds(dst_col, cols)],
                sems.at[len(copies)],
            )
            copy.start()
            copies.append(copy)
    return copies


def call(kernel, out_shape, inputs, in_any, scratch, flops, traffic, vmem_bytes=VMEM_BYTES):
    any_spec = pl.BlockSpec(memory_space=pl.ANY)
    vmem = pl.BlockSpec(memory_space=pltpu.VMEM)
    specs = [vmem] * len(inputs) + [any_spec] * len(in_any)
    return pl.pallas_call(
        kernel,
        out_shape=out_shape,
        in_specs=specs,
        out_specs=jax.tree.map(lambda _: vmem, out_shape),
        scratch_shapes=scratch,
        compiler_params=pltpu.CompilerParams(vmem_limit_bytes=vmem_bytes),
        cost_estimate=pl.CostEstimate(flops=flops, bytes_accessed=traffic, transcendentals=0),
    )(*inputs, *in_any)


def shard_at():
    return lax.axis_index("shard").astype(jnp.int32)


def side_at():
    return lax.axis_index("replica").astype(jnp.int32) & 1


def shaped(shape, dtype):
    return jax.ShapeDtypeStruct(shape, dtype)


def pack_qkv_kernel(half):
    def body(weight, attn_gain, ffn_gain, out, attn_held, ffn_held, sems):
        rows = weight.shape[0]
        first = side_at() * half
        copies = [
            pltpu.make_async_copy(attn_gain, attn_held, sems.at[0]),
            pltpu.make_async_copy(ffn_gain, ffn_held, sems.at[1]),
        ]
        for i in range(3):
            start = pl.multiple_of(i * 2 * half + first, 128)
            copies.append(
                pltpu.make_async_copy(
                    weight.at[:, pl.ds(start, half)],
                    out.at[:, pl.ds(i * half, half)],
                    sems.at[2 + i],
                )
            )
        for copy in copies:
            copy.start()
        copies[0].wait()
        copies[1].wait()
        gains = [ref[...].astype(F32) for ref in (attn_held, ffn_held)]
        gains = jnp.concatenate(gains + [jnp.zeros((6, rows), F32)], axis=0)
        gains = jnp.concatenate([gains, jnp.zeros((8, 128 - rows), F32)], axis=1)
        square = jnp.concatenate([gains, jnp.zeros((120, 128), F32)], axis=0)
        out[:, 3 * half :] = square.T[0:rows, :].astype(BF)
        for copy in copies[2:]:
            copy.wait()

    return body


def pack_mlp_kernel(count, down_rows, take):
    def body(attn, glu, down, out):
        rows, width = attn.shape
        units = count * take
        hidden = count * down_rows
        out[:, 0:width] = attn[...]
        last = width + 2 * units

        def pick(first):
            for part in range(2):
                for s in range(count):
                    at = part * hidden + s * down_rows + first
                    to = width + part * units + s * take
                    out[:, to : to + take] = glu[:, at : at + take]
            out[0:take, last:] = down[first : first + take, :]

        @pl.when(side_at() == 0)
        def _():
            pick(0)

        @pl.when(side_at() != 0)
        def _():
            pick(down_rows - take)

        if rows > take:
            out[take:, last:] = jnp.zeros((rows - take, width), BF)

    return body


def around_kernel(own, places, partner, near, far, out, cosine, sine, bias):
    def arrange(*blocks):
        for i, ref in enumerate(blocks):
            out[i * BLOCK : (i + 1) * BLOCK, :] = ref[0:BLOCK, :]

    @pl.when(side_at() == 0)
    def _():
        arrange(near, own, partner, far)

    @pl.when(side_at() != 0)
    def _():
        arrange(far, partner, own, near)

    def places_of(ref):
        first = ref.shape[0] - 16
        return ref[first : first + 1, 0:BLOCK].astype(F32) * 256.0 + ref[
            first + 1 : first + 2, 0:BLOCK
        ].astype(F32)

    mine, theirs = places[...].astype(F32), places_of(partner)
    inner, outer = places_of(near), places_of(far)
    even = side_at() == 0
    lines = [
        jnp.where(even, inner, outer),
        jnp.where(even, mine, theirs),
        jnp.where(even, theirs, mine),
        jnp.where(even, outer, inner),
    ]
    stacked = jnp.concatenate([jnp.broadcast_to(line, (BLOCK, BLOCK)).T for line in lines], axis=0)
    lane = lax.broadcasted_iota(jnp.int32, (1, 128), 1)
    power = lax.rem(lane, HEAD // 2).astype(F32) * (2.0 / HEAD)
    phases = stacked * jnp.exp(power * -math.log(THETA_BASE))
    cosine[...] = jnp.cos(phases)
    sine[...] = jnp.where((lane & 63) < 32, -1.0, 1.0) * jnp.sin(phases)
    offset = (
        lax.broadcasted_iota(jnp.int32, (BLOCK, 2 * BLOCK), 1)
        - RADIUS
        - lax.broadcasted_iota(jnp.int32, (BLOCK, 2 * BLOCK), 0)
    )
    distance = offset.astype(F32)
    for b in range(3):
        start = RADIUS + b * BLOCK
        key = jnp.concatenate([lines[b], lines[b + 1]], axis=1)
        query = jnp.concatenate([stacked[start : start + BLOCK, :]] * 2, axis=1)
        later = jnp.where(offset >= 0, key - distance, query + distance)
        allowed = (jnp.abs(offset) <= RADIUS) & (later >= 0.0)
        bias[b * BLOCK : (b + 1) * BLOCK, :] = jnp.where(allowed, 0.0, NEGATIVE)


def around_back_kernel(own, partner, near, far, out):
    def arrange(before, first, second, after):
        out[0:RADIUS, :] = before[...]
        out[RADIUS : RADIUS + BLOCK, :] = first
        out[RADIUS + BLOCK : RADIUS + 2 * BLOCK, :] = second
        out[RADIUS + 2 * BLOCK :, :] = after[...]

    theirs = partner[...]

    @pl.when(side_at() == 0)
    def _():
        arrange(near, own[...], theirs, far)

    @pl.when(side_at() != 0)
    def _():
        arrange(far, theirs, own[...], near)


def qkv_layout(rows, half, weight, gains=None):
    wide = 3 * half
    split = (wide + 128) // 2
    streams = [[(0, rows, 0, split, weight, 0)], [(0, rows, 0, wide - split, weight, split)]]
    streams.append([(0, rows, 0, wide, weight, 0)])
    if gains is not None:
        streams[1].append((0, rows, wide - split, 128, gains, 0))
        streams[2].append((0, rows, wide, 128, gains, 0))
    return streams


def project_kernel(pieces, n_refs, rows, width, skip):
    half = width // 2
    span = 4 * BLOCK

    def body(tok, cosine, sine, bias, *rest):
        refs, rest = rest[skip : n_refs + skip], rest[n_refs + skip :]
        q_out, k_out, v_out, p_out, ctx_out, normed_out, gains_out = rest[:7]
        weight, gain_cols, normed, sems = rest[7:]
        layout = qkv_layout(rows, half, weight, gain_cols)
        copies = place(shard_at(), pieces, refs, layout, sems)
        hats = [
            standardize(tok[i * BLOCK : (i + 1) * BLOCK, :].astype(F32))[0] for i in range(4)
        ]
        for copy in copies:
            copy.wait()
        pick = jnp.where(
            lax.broadcasted_iota(jnp.int32, (8, 128), 0)
            == lax.broadcasted_iota(jnp.int32, (8, 128), 1),
            1.0,
            0.0,
        ).astype(BF)
        gains = dot_cols(pick, gain_cols[...])
        gains_out[...] = gains
        for i, hat in enumerate(hats):
            normed[i * BLOCK : (i + 1) * BLOCK, :] = (hat * gains[0:1]).astype(BF)
        normed_out[...] = normed[BLOCK : 3 * BLOCK, :]
        cos3 = jnp.concatenate([cosine[...]] * 3, axis=1)
        sin3 = jnp.concatenate([sine[...]] * 3, axis=1)
        mid = slice(RADIUS, span - RADIUS)
        joined = dot(normed[mid, :], weight[:, 0:half])
        q_out[...] = (joined * cos3[mid] + turned(joined) * sin3[mid]).astype(BF)
        joined = dot(normed[...], weight[:, half : 2 * half])
        k_out[...] = (joined * cos3 + turned(joined) * sin3).astype(BF)
        v_out[...] = dot(normed[...], weight[:, 2 * half : 3 * half]).astype(BF)
        lane = lax.broadcasted_iota(jnp.int32, (BLOCK, 128), 1)
        scale = 1.0 / math.sqrt(HEAD)
        for pair in range(half // 128):
            cols = slice(pair * 128, pair * 128 + 128)
            for b in range(3):
                rows_q = slice(b * BLOCK, (b + 1) * BLOCK)
                rows_k = slice(b * BLOCK, (b + 2) * BLOCK)
                queries, keys, values = q_out[rows_q, cols], k_out[rows_k, cols], v_out[rows_k, cols]
                parts = []
                for h in range(2):
                    mine = (lane < HEAD) if h == 0 else (lane >= HEAD)
                    masked = jnp.where(mine, queries.astype(F32) * scale, 0.0).astype(BF)
                    scores = dot_cols(masked, keys) + bias[rows_q, :]
                    exponent = jnp.exp(scores - jnp.max(scores, axis=1, keepdims=True))
                    total = jnp.sum(exponent, axis=1, keepdims=True)
                    shares = (exponent * (1.0 / total)).astype(BF)
                    p_out[(pair * 2 + h) * 3 + b] = shares
                    parts.append(dot(shares, values))
                ctx_out[rows_q, cols] = jnp.where(lane < HEAD, parts[0], parts[1]).astype(BF)

    return body


def attn_layout(rows, width, attn):
    parts = [(0, rows, 0, width, attn, 0)]
    return (parts, (), parts)


def mlp_layout(rows, take, width, units, glu, down):
    gate = (0, rows, width, units, glu, 0)
    up = (0, rows, 0, units, glu, units)
    low = (0, take, units, width, down, 0)
    whole = ((0, rows, width, 2 * units, glu, 0), (0, take, width + 2 * units, width, down, 0))
    return ((gate,), (up, low), whole)


def mlp_kernel(pieces, n_refs, rows, down_rows, take, width, units):
    half = width // 2
    pair = slice(RADIUS, RADIUS + 2 * BLOCK)

    def body(tok, ctx_own, ctx_other, dy, gains, *rest):
        refs, rest = rest[1 : n_refs + 1], rest[n_refs + 1 :]
        mix_keep, mix_send, shared, ctx_pair, hidden, gn_out = rest[:6]
        attn, glu, down, ggu, mix, attn_sems, sems = rest[6:]
        first = place(shard_at(), pieces, refs, attn_layout(rows, width, attn), attn_sems)
        layout = mlp_layout(rows, take, width, units, glu, down)
        copies = place(shard_at(), pieces, refs, layout, sems)
        at = side_at()
        inputs = tok[RADIUS : RADIUS + 3 * BLOCK, :].astype(F32)
        own_rows = pl.ds(pl.multiple_of(at * half, 128), half)
        other_rows = pl.ds(pl.multiple_of((1 - at) * half, 128), half)

        @pl.when(at == 0)
        def _():
            ctx_pair[:, 0:half] = ctx_own[pair, :]
            ctx_pair[:, half:] = ctx_other[pair, :]

        @pl.when(at != 0)
        def _():
            ctx_pair[:, 0:half] = ctx_other[pair, :]
            ctx_pair[:, half:] = ctx_own[pair, :]

        for copy in first:
            copy.wait()
        lifted = dot(ctx_own[...], attn[own_rows, :]) + dot(ctx_other[...], attn[other_rows, :])
        hidden[...] = inputs + lifted
        hat, _ = standardize(hidden[...])
        normed = (hat * gains[1:2, :]).astype(BF)
        shared[:, 0:width] = normed[pair]
        for copy in copies:
            copy.wait()
        partial = jnp.zeros((2 * BLOCK, width), F32)
        unit = lax.rem(lax.broadcasted_iota(jnp.int32, (1, units), 1), take)
        mask = jnp.where(unit >= at * (2 * take - down_rows), 1.0, 0.0)
        for c in range(0, units, 640):
            wide = min(640, units - c)
            cols = slice(c, c + wide)
            gate = dot(normed, glu[:, cols])
            up = dot(normed, glu[:, units + c : units + c + wide])
            grad_act = dot_cols(dy[...], down[cols, :]) * mask[:, cols]
            share = 0.5 * (1.0 + lax.erf(gate * (1.0 / math.sqrt(2.0))))
            density = jnp.exp(-0.5 * gate * gate) * (1.0 / math.sqrt(2.0 * math.pi))
            gelu = gate * share
            act = (gelu[pair] * up[pair] * mask[:, cols]).astype(BF)
            shared[:, width + c : width + c + wide] = act
            partial = partial + dot(act, down[cols, :])
            ggu[:, cols] = (grad_act * up * (share + gate * density)).astype(BF)
            ggu[:, units + c : units + c + wide] = (grad_act * gelu).astype(BF)
        mix[...] = partial
        mine = pl.ds(pl.multiple_of(at * BLOCK, BLOCK), BLOCK)
        theirs = pl.ds(pl.multiple_of((1 - at) * BLOCK, BLOCK), BLOCK)
        mix_keep[...] = mix[mine, :] + hidden[pl.ds(pl.multiple_of(RADIUS + at * BLOCK, 8), BLOCK), :]
        mix_send[...] = mix[theirs, :].astype(BF)
        shared[:, width + units :] = ggu[pair, :]
        grad = dot_cols(ggu[...], glu[...])
        gn_out[...] = grad.astype(BF)

    return body


def pair_back(pair, gctx, q, k, v, p, cos, sin):
    lane = lax.broadcasted_iota(jnp.int32, (BLOCK, 128), 1)
    lane2 = lax.broadcasted_iota(jnp.int32, (2 * BLOCK, 128), 1)
    scale = 1.0 / math.sqrt(HEAD)
    cols = slice(pair * 128, pair * 128 + 128)
    first, second = slice(0, BLOCK), slice(BLOCK, 2 * BLOCK)
    low, high = slice(0, RADIUS), slice(RADIUS, BLOCK)
    grad_q = jnp.zeros((2 * BLOCK, 128), F32)
    grad_k, grad_v = [0.0, 0.0], [0.0, 0.0]
    for h in range(2):
        mine = (lane < HEAD) if h == 0 else (lane >= HEAD)
        mine2 = (lane2 < HEAD) if h == 0 else (lane2 >= HEAD)
        scores, shares, queries, grads, parts = [], [], [], [], []
        for b in range(3):
            rows_q = slice(b * BLOCK, (b + 1) * BLOCK)
            rows_k = slice(b * BLOCK, (b + 2) * BLOCK)
            keys, values = k[rows_k, cols], v[rows_k, cols]
            lowered = jnp.where(mine, gctx[rows_q, cols].astype(F32), 0.0).astype(BF)
            query = jnp.where(mine, q[rows_q, cols].astype(F32) * scale, 0.0).astype(BF)
            share = p[(pair * 2 + h) * 3 + b]
            wide = share.astype(F32)
            grad_share = dot_cols(lowered, values)
            row = jnp.sum(wide * grad_share, axis=1, keepdims=True)
            grad_score = (wide * (grad_share - row)).astype(BF)
            scores.append(grad_score)
            shares.append(share)
            queries.append(query)
            grads.append(lowered)
            part = (high, first, low)[b]
            parts.append(dot(grad_score[part], keys))
        grad_q = grad_q + jnp.where(mine2, jnp.concatenate(parts, axis=0) * scale, 0.0)
        for i in range(2):
            two = slice(i, i + 2)
            for total, left, right in ((grad_k, scores, queries), (grad_v, shares, grads)):
                upper, lower = left[i][:, second], left[i + 1][:, first]
                total[i] = total[i] + dot_rows(
                    jnp.concatenate([upper, lower], axis=0), jnp.concatenate(right[two], axis=0)
                )
    grad_k, grad_v = jnp.concatenate(grad_k, axis=0), jnp.concatenate(grad_v, axis=0)
    return (
        (grad_q * cos - turned(grad_q) * sin).astype(BF),
        (grad_k * cos - turned(grad_k) * sin).astype(BF),
        grad_v.astype(BF),
    )


def hidden_back_kernel(mlp_pieces, n_mlp, rows, width):
    half = width // 2
    pair = slice(RADIUS, RADIUS + 2 * BLOCK)

    def body(gn_own, gn_other, hidden, dy, gains, q, k, v, p, cosine, sine, *rest):
        mlp_refs, rest = rest[1 : n_mlp + 1], rest[n_mlp + 1 :]
        ghid_out, halves_out, gctx, first_out, attn, held, attn_sems = rest
        copies = place(shard_at(), mlp_pieces, mlp_refs, attn_layout(rows, width, attn), attn_sems)
        at = side_at()
        hat, inverse = standardize(hidden[...])
        grad = gn_own[...].astype(F32) + gn_other[...].astype(F32)
        grad_hidden = dy[...].astype(F32) + norm_back(grad, gains[1:2, :], hat, inverse)
        held[...] = grad_hidden[pair]
        ghid_out[...] = held[pl.ds(pl.multiple_of(at * BLOCK, BLOCK), BLOCK), :]
        halves = jnp.where(at == 0, grad_hidden[pair, 0:half], grad_hidden[pair, half:])
        halves_out[...] = halves.astype(BF)
        grad_low = grad_hidden.astype(BF)
        for copy in copies:
            copy.wait()
        own_rows = pl.ds(pl.multiple_of(at * half, 128), half)
        gctx[...] = dot_cols(grad_low, attn[own_rows, :]).astype(BF)
        cos, sin = cosine[BLOCK : 3 * BLOCK, :], sine[BLOCK : 3 * BLOCK, :]
        for part, grad in enumerate(pair_back(0, gctx, q, k, v, p, cos, sin)):
            first_out[:, part * 128 : (part + 1) * 128] = grad

    return body


def back_kernel(width):
    half = width // 2

    def body(first, halves, gctx, q, k, v, p, cosine, sine, sent, gj_out):
        gj_out[:, 3 * half :] = halves[...]
        cos, sin = cosine[BLOCK : 3 * BLOCK, :], sine[BLOCK : 3 * BLOCK, :]
        for part in range(3):
            gj_out[:, part * half : part * half + 128] = first[:, part * 128 : (part + 1) * 128]
        for i in range(1, half // 128):
            for part, grad in enumerate(pair_back(i, gctx, q, k, v, p, cos, sin)):
                col = part * half + i * 128
                gj_out[:, col : col + 128] = grad

    return body


def norm_back_kernel(pieces, n_refs, rows, width):
    half = width // 2

    def body(gj, *rest):
        refs, rest = rest[:n_refs], rest[n_refs:]
        keep_out, send_out, weight, held, sems = rest
        copies = place(shard_at(), pieces, refs, qkv_layout(rows, half, weight), sems)
        at = side_at()
        for copy in copies:
            copy.wait()
        held[...] = dot_cols(gj[:, 0 : 3 * half], weight[...])
        keep_out[...] = held[pl.ds(pl.multiple_of(at * BLOCK, BLOCK), BLOCK), :]
        theirs = pl.ds(pl.multiple_of((1 - at) * BLOCK, BLOCK), BLOCK)
        send_out[...] = held[theirs, :].astype(BF)

    return body


def final_kernel(tok, keep, other, ghid, gains, out):
    hat, inverse = standardize(tok[...].astype(F32))
    grad = keep[...] + other[...].astype(F32)
    out[...] = (ghid[...] + norm_back(grad, gains[0:1, :], hat, inverse)).astype(BF)


def slots_of(chip_bits):
    tables = []
    for order in (chip_bits, chip_bits[::-1]):
        kept = [0]
        for bit in order[1:][::-1]:
            kept = kept + [j | bit for j in kept]
        tables.append([(1, i, j) for i, j in enumerate(kept)])
        tables[-1] += [(0, i, j | order[0]) for i, j in enumerate(kept)]
    return [(kept, i, j, k) for (kept, i, j), (_, _, k) in zip(*tables)]


def owner_rows(me, slots, lhs_t, rows):
    parts = []
    for _, _, even, odd in slots:
        owner = me ^ jnp.where((me & 1) == 0, even, odd)
        parts.append(lhs_t[pl.ds(pl.multiple_of(owner * rows, 16), rows), :])
    return jnp.concatenate(parts, axis=0)


def emit(outs, slots, rows, grad, start):
    grad = grad.astype(BF)
    for i, (kept, at, _, _) in enumerate(slots):
        for c in range(grad.shape[1] // 128):
            row = start + c * rows
            outs[kept][at, row : row + rows, :] = grad[
                i * rows : (i + 1) * rows, c * 128 : (c + 1) * 128
            ]


def mlp_grad_kernel(slots, rows, take, width, units):
    half = width // 2

    def body(own, other, dy_own, dy_other, *rest):
        outs, (normed_t, act_t, ggu, dy) = rest[1:3], rest[3:]
        me = shard_at()
        pair = slice(RADIUS, RADIUS + 2 * BLOCK)
        for i, (ref, dref) in enumerate(((own, dy_own), (other, dy_other))):
            tok = slice(i * 2 * BLOCK, (i + 1) * 2 * BLOCK)
            normed_t[:, tok] = ref[:, 0:width].T
            act_t[:, tok] = ref[:, width : width + units].T
            ggu[tok, :] = ref[:, width + units :]
            dy[tok, :] = dref[pair, :]
        left = owner_rows(me, slots, normed_t, rows)
        act = owner_rows(me, slots, act_t, take)
        height = outs[0].shape[1] // 2
        for s in range(2):
            grad = dot(left, ggu[:, s * units : (s + 1) * units])
            emit(outs, slots, rows, grad, s * height)
            grad = dot(act, dy[:, s * half : (s + 1) * half])
            emit(outs, slots, take, grad, s * height + rows * (units // 128))

    return body


def qkv_grad_kernel(slots, rows, width):
    half = width // 2

    def body(normed_own, normed_other, ctx_own, ctx_other, own, other, *rest):
        outs, (normed_t, ctx_t, gj) = rest[1:3], rest[3:]
        me = shard_at()
        count = 2 * BLOCK
        each = ((normed_own, ctx_own, own), (normed_other, ctx_other, other))
        for i, (nref, cref, ref) in enumerate(each):
            tok = slice(i * count, (i + 1) * count)
            normed_t[:, tok] = nref[...].T
            ctx_t[:, tok] = cref[...].T
            gj[tok, :] = ref[...]
        left = owner_rows(me, slots, normed_t, rows)
        ctx = owner_rows(me, slots, ctx_t, rows)
        emit(outs, slots, rows, dot(left, gj[:, 0 : 3 * half]), 0)
        emit(outs, slots, rows, dot(ctx, gj[:, 3 * half :]), 9 * rows)

    return body


def gain_grad(weight, grad, gain):
    total = jnp.sum(weight[...].astype(F32) * grad[...], axis=1, keepdims=True)
    rows = total.shape[0]
    total = jnp.concatenate([total, jnp.zeros((128 - rows, 1), F32)], axis=0)
    return jnp.broadcast_to(total, (128, 128)).T[0:1, 0:rows] / gain[...].astype(F32)


def mlp_unpack_kernel(rows, down_rows, take, width, units, count):
    hidden = count * down_rows
    spare = 2 * take - down_rows

    def body(mine_0, mine_1, other_0, other_1, weight, gain, sent, glu, down, gain_out, held, wide):
        at = side_at()
        tiles = units // 128
        for s, (mine, other) in enumerate(((mine_0, other_0), (mine_1, other_1))):
            held[at, s] = mine[...].astype(F32)
            held[1 - at, s] = other[...].astype(F32)
        for s in range(2):
            for t in range(2):
                for c in range(tiles):
                    row = c * rows
                    wide[:, c * 128 : (c + 1) * 128] = held[t, s, row : row + rows, :]
                skip = 0 if t == 0 else spare
                for i in range(count):
                    col = s * hidden + i * down_rows + t * take
                    glu[:, col : col + take - skip] = wide[:, i * take + skip : (i + 1) * take]
                for c in range(width // 256):
                    row = tiles * rows + c * take
                    col = s * (width // 2) + c * 128
                    down[t * take : (t + 1) * take - skip, col : col + 128] = held[
                        t, s, row + skip : row + take, :
                    ]
        gain_out[...] = gain_grad(weight, glu, gain)

    return body


def qkv_unpack_kernel(rows, width):
    half = width // 2
    tiles = half // 128

    def body(mine_0, mine_1, other_0, other_1, weight, gain, qkv, attn, gain_out, held):
        at = side_at()
        for s, (mine, other) in enumerate(((mine_0, other_0), (mine_1, other_1))):
            held[at, s] = mine[...].astype(F32)
            held[1 - at, s] = other[...].astype(F32)
        for t in range(2):
            for i in range(3):
                for c in range(tiles):
                    row = (i % 2 * tiles + c) * rows
                    col = i * width + t * half + c * 128
                    qkv[:, col : col + 128] = held[t, i // 2, row : row + rows, :]
            for c in range(tiles):
                row = (tiles + c) * rows
                attn[:, t * half + c * 128 : t * half + (c + 1) * 128] = held[t, 1, row : row + rows, :]
        gain_out[...] = gain_grad(weight, qkv, gain)

    return body


def on_device(
    tokens,
    positions,
    qkv_weight,
    attn_weight,
    glu_weight,
    down_weight,
    attn_gain,
    ffn_gain,
    cotangent,
):
    block, width = tokens.shape
    half = width // 2
    rows, down_rows = qkv_weight.shape[0], down_weight.shape[0]
    count, replicas = lax.axis_size("shard"), lax.axis_size("replica")
    everyone = count * replicas
    take = -(-down_rows // 32) * 16
    units = count * take
    me = lax.axis_index("shard").astype(jnp.int32)
    side = lax.axis_index("replica").astype(jnp.int32) & 1
    chip_bits = bits_of(count)[1:]

    own = call(
        pack_qkv_kernel(half),
        shaped((rows, 3 * half + 128), BF),
        (),
        [qkv_weight, attn_gain[None], ffn_gain[None]],
        [
            pltpu.VMEM((1, rows), BF),
            pltpu.VMEM((1, rows), BF),
            pltpu.SemaphoreType.DMA((5,)),
        ],
        1_000_000,
        1_000_000,
        VMEM_ALL,
    )

    places = jnp.stack([positions >> 8, positions & 255]).astype(BF)
    places = jnp.pad(places, ((0, 14), (0, width - block)))
    rim = jnp.concatenate([tokens, places], axis=0)
    rim, _ = lax.optimization_barrier((rim, own))
    step = [1 if i & 1 else -1 for i in range(everyone)]
    both = ("shard", "replica")

    def outward(array):
        moves = [(i, i + step[i]) for i in range(everyone)]
        return lax.ppermute(array, both, [(a, b) for a, b in moves if 0 <= b < everyone])

    own_mlp = call(
        pack_mlp_kernel(count, down_rows, take),
        shaped((rows, 2 * width + 2 * units), BF),
        (attn_weight, glu_weight, down_weight),
        [],
        [],
        1_000_000,
        2_000_000,
    )
    qkv_parts, _ = gather_pieces(
        own, (3 * half + 128) // 2, chip_bits, rim
    )
    near, partner = outward(rim), xor_send(rim, "replica", 1)
    arrived = [a for _, _, a in qkv_parts]
    own, near, partner, arrived = lax.optimization_barrier((own_mlp, near, partner, arrived))
    qkv_parts = [(j, s, a) for (j, s, _), a in zip(qkv_parts, arrived)]
    far = xor_send(near, "replica", 1)
    mlp_parts, forward = gather_pieces(own, width + units, chip_bits)

    tok, cosine, sine, bias = call(
        around_kernel,
        (
            shaped((4 * BLOCK, width), BF),
            shaped((4 * BLOCK, 128), F32),
            shaped((4 * BLOCK, 128), F32),
            shaped((3 * BLOCK, 2 * BLOCK), F32),
        ),
        (tokens, positions[None], partner, near, far),
        [],
        [],
        1_000_000,
        2_000_000,
    )
    rim = jnp.where(side == 0, cotangent[:RADIUS], cotangent[block - RADIUS :])
    rim, _ = lax.optimization_barrier((rim, near))
    near_dy = outward(rim)
    sent, near_dy = lax.optimization_barrier((cotangent, near_dy))
    partner_dy = xor_send(sent, "replica", 1)
    far_dy = xor_send(near_dy, "replica", 1)
    qkv_names, qkv_arrays = with_core(qkv_parts, True)
    weight_bytes = width * 3 * width * 2

    q, k, v, p, ctx, normed, gains = call(
        project_kernel(qkv_names, len(qkv_arrays), rows, width, 2 + len(forward)),
        (
            shaped((3 * BLOCK, half), BF),
            shaped((4 * BLOCK, half), BF),
            shaped((4 * BLOCK, half), BF),
            shaped((3 * half // HEAD, BLOCK, 2 * BLOCK), BF),
            shaped((3 * BLOCK, half), BF),
            shaped((2 * BLOCK, width), BF),
            shaped((8, width), F32),
        ),
        (tok, cosine, sine, bias),
        [far_dy, partner_dy] + forward + qkv_arrays,
        [
            pltpu.VMEM((width, 3 * half), BF),
            pltpu.VMEM((width, 128), BF),
            pltpu.VMEM((4 * BLOCK, width), BF),
            pltpu.SemaphoreType.DMA((2 * len(qkv_names),)),
        ],
        7_000_000_000,
        weight_bytes,
    )
    ctx_other = xor_send(ctx, "replica", 1)
    normed_other = xor_send(normed, "shard", 1)
    near_dy, far_dy, partner_dy, _ = lax.optimization_barrier(
        (near_dy, far_dy, partner_dy, ctx)
    )
    dy = call(
        around_back_kernel,
        shaped((3 * BLOCK, width), BF),
        (cotangent, partner_dy, near_dy, far_dy),
        [],
        [],
        1_000_000,
        2_000_000,
    )
    dy_other = xor_send(dy, "shard", 1)
    held, _ = lax.optimization_barrier(([a for _, _, a in mlp_parts], ctx))
    mlp_parts = [(j, s, a) for (j, s, _), a in zip(mlp_parts, held)]
    names, arrays = with_core(mlp_parts, False)

    mix_keep, mix_send, shared, ctx_pair, hidden, gn = call(
        mlp_kernel(names, len(arrays), rows, down_rows, take, width, units),
        (
            shaped((BLOCK, width), F32),
            shaped((BLOCK, width), BF),
            shaped((2 * BLOCK, width + 3 * units), BF),
            shaped((2 * BLOCK, width), BF),
            shaped((3 * BLOCK, width), F32),
            shaped((3 * BLOCK, width), BF),
        ),
        (tok, ctx, ctx_other, dy, gains),
        [normed_other] + arrays,
        [
            pltpu.VMEM((width, width), BF),
            pltpu.VMEM((width, 2 * units), BF),
            pltpu.VMEM((units, width), BF),
            pltpu.VMEM((3 * BLOCK, 2 * units), BF),
            pltpu.VMEM((2 * BLOCK, width), F32),
            pltpu.SemaphoreType.DMA((len(names),)),
            pltpu.SemaphoreType.DMA((2 * len(names),)),
        ],
        8_000_000_000,
        2 * weight_bytes,
    )
    gn_other = xor_send(gn, "replica", 1)
    shared_other = xor_send(shared, "shard", 1)
    ctx_pair_other = xor_send(ctx_pair, "shard", 1)

    slots = slots_of(chip_bits)
    portion = count // 4

    def stack(height):
        return (shaped((portion, 2 * height, 128), BF),) * 2

    height = rows * (units // 128) + take * (half // 128)
    sums = call(
        mlp_grad_kernel(slots, rows, take, width, units),
        stack(height),
        (shared, shared_other, dy, dy_other),
        [ctx_pair_other],
        [
            pltpu.VMEM((width, 4 * BLOCK), BF),
            pltpu.VMEM((units, 4 * BLOCK), BF),
            pltpu.VMEM((4 * BLOCK, 2 * units), BF),
            pltpu.VMEM((4 * BLOCK, width), BF),
        ],
        4_000_000_000,
        weight_bytes,
    )

    ghid, halves, gctx, gj_first = call(
        hidden_back_kernel(names, len(arrays), rows, width),
        (
            shaped((BLOCK, width), F32),
            shaped((2 * BLOCK, half), BF),
            shaped((3 * BLOCK, half), BF),
            shaped((2 * BLOCK, 3 * 128), BF),
        ),
        (gn, gn_other, hidden, dy, gains, q, k, v, p, cosine, sine),
        [sums[1]] + arrays,
        [
            pltpu.VMEM((width, width), BF),
            pltpu.VMEM((2 * BLOCK, width), F32),
            pltpu.SemaphoreType.DMA((len(names),)),
        ],
        5_000_000_000,
        weight_bytes,
    )
    mlp_sums = scatter_sums(sums, chip_bits, gctx)
    mix_other = xor_send(mix_send, "replica", 1)
    gj = call(
        back_kernel(width),
        shaped((2 * BLOCK, 4 * half), BF),
        (gj_first, halves, gctx, q, k, v, p, cosine, sine),
        [mlp_sums[2]],
        [],
        6_000_000_000,
        weight_bytes,
    )
    gj_other = xor_send(gj, "shard", 1)
    norm_keep, norm_send = call(
        norm_back_kernel(qkv_names, len(qkv_arrays), rows, width),
        (shaped((BLOCK, width), F32), shaped((BLOCK, width), BF)),
        (gj,),
        qkv_arrays,
        [
            pltpu.VMEM((width, 3 * half), BF),
            pltpu.VMEM((2 * BLOCK, width), F32),
            pltpu.SemaphoreType.DMA((len(qkv_names),)),
        ],
        3_000_000_000,
        weight_bytes,
    )
    sums = call(
        qkv_grad_kernel(slots, rows, width),
        stack(6 * rows),
        (normed, normed_other, ctx_pair, ctx_pair_other, gj, gj_other),
        [norm_keep],
        [
            pltpu.VMEM((width, 4 * BLOCK), BF),
            pltpu.VMEM((width, 4 * BLOCK), BF),
            pltpu.VMEM((4 * BLOCK, 4 * half), BF),
        ],
        3_000_000_000,
        weight_bytes,
    )
    mlp_sums, mix_other, _ = lax.optimization_barrier((mlp_sums, mix_other, sums[1]))
    mlp_sums = last_sums(*mlp_sums)
    norm_send, _ = lax.optimization_barrier((norm_send, sums[1]))
    norm_other = xor_send(norm_send, "replica", 1)
    mixed = (mix_keep + mix_other.astype(F32)).astype(BF)
    grad_tokens = call(
        final_kernel,
        shaped((block, width), BF),
        (tokens, norm_keep, norm_other, ghid, gains),
        [],
        [],
        1_000_000,
        1_000_000,
    )
    qkv_sums = scatter_sums(sums, chip_bits, (mixed, grad_tokens))
    mlp_mine = [side_sum(part, qkv_sums[2]) for part in mlp_sums]
    mlp_other = [xor_send(part, "replica", 1) for part in mlp_mine]
    sent = qkv_sums[1]
    grad_glu, grad_down, grad_ffn_gain = call(
        mlp_unpack_kernel(rows, down_rows, take, width, units, count),
        (
            shaped((rows, 2 * count * down_rows), F32),
            shaped((down_rows, width), F32),
            shaped((1, rows), F32),
        ),
        (*mlp_mine, *mlp_other, glu_weight, ffn_gain[None]),
        [sent],
        [pltpu.VMEM((2, 2, height, 128), F32), pltpu.VMEM((rows, units), F32)],
        1_000_000,
        4_000_000,
    )
    done = grad_glu
    qkv_mine = [side_sum(part, done) for part in last_sums(*qkv_sums)]
    qkv_other = [xor_send(part, "replica", 1) for part in qkv_mine]
    grad_qkv, grad_attn, grad_attn_gain = call(
        qkv_unpack_kernel(rows, width),
        (
            shaped((rows, 3 * width), F32),
            shaped((rows, width), F32),
            shaped((1, rows), F32),
        ),
        (*qkv_mine, *qkv_other, qkv_weight, attn_gain[None]),
        [],
        [pltpu.VMEM((2, 2, 6 * rows, 128), F32)],
        1_000_000,
        4_000_000,
    )
    return (
        mixed,
        grad_tokens,
        grad_qkv,
        grad_attn,
        grad_glu,
        grad_down,
        grad_attn_gain.reshape(rows),
        grad_ffn_gain.reshape(rows),
    )


def solution(mesh):
    in_specs = (
        P(("shard", "replica"), None),
        P(("shard", "replica")),
        P("shard", None),
        P("shard", None),
        P("shard", None),
        P("shard", None),
        P("shard"),
        P("shard"),
        P(("shard", "replica"), None),
    )
    out_specs = (
        P(("shard", "replica"), None),
        P(("shard", "replica"), None),
        P("shard", None),
        P("shard", None),
        P("shard", None),
        P("shard", None),
        P("shard"),
        P("shard"),
    )
    return jax.shard_map(
        on_device, mesh=mesh, in_specs=in_specs, out_specs=out_specs, check_vma=False
    )
```

```python
import math

import jax
import jax.numpy as jnp
from jax import lax
from jax.experimental import pallas as pl
from jax.experimental.pallas import tpu as pltpu
from jax.sharding import PartitionSpec as P

HEAD = 64
RADIUS = 64
BLOCK = 128
EPSILON = 1e-05
THETA_BASE = 10000.0
NEGATIVE = -1e30
VMEM_BYTES = 24 * 1024 * 1024
VMEM_ALL = 60 * 1024 * 1024
BF = jnp.bfloat16
F32 = jnp.float32


def xor_send(array, axis, bit):
    count = lax.axis_size(axis)
    return lax.ppermute(array, axis, [(i, i ^ bit) for i in range(count)])


def bits_of(count):
    return [1 << i for i in range(count.bit_length() - 1)]


def core_send(array, bits):
    count = lax.axis_size("shard")
    return lax.ppermute(array, "shard", [(i, i ^ bits[i & 1]) for i in range(count)])


def gather_pieces(own, split, chip_bits, before=None):
    if len(chip_bits) == 2:
        x, y = chip_bits
        from_x, from_y = xor_send(own, "shard", x), xor_send(own, "shard", y)
        if before is not None:
            (from_x, from_y), _ = lax.optimization_barrier(((from_x, from_y), before))
        pieces = [(0, 2, own), (x, 2, from_x), (y, 2, from_y)]
        forward = [from_x[:, :split], from_y[:, split:]]
        pieces.append((x | y, 0, xor_send(forward[0], "shard", y)))
        pieces.append((x | y, 1, xor_send(forward[1], "shard", x)))
    else:
        streams = ([(0, 0, own[:, :split])], [(0, 1, own[:, split:])])
        for stage in range(len(chip_bits)):
            grown = []
            for which, bit in ((0, chip_bits[stage]), (1, chip_bits[-1 - stage])):
                grown.append(
                    [(j ^ bit, s, xor_send(a, "shard", bit)) for j, s, a in streams[which]]
                )
            for held, more in zip(streams, grown):
                held.extend(more)
        pieces = streams[0] + streams[1]
        forward = []
    return pieces, forward


def with_core(pieces, joined):
    rows = pieces[0][2].shape[0]
    arrays = [a for _, _, a in pieces]
    names = [(j, s, i, 0) for i, (j, s, _) in enumerate(pieces)]
    whole = [p for p in pieces if p[1] == 2]
    others = pieces[len(whole) :]
    if joined and whole:
        whole.append((others[0][0], 2, jnp.concatenate([a for _, _, a in others], axis=1)))
        others = []
    groups = ([whole] if whole else []) + [[p] for p in others]
    for group in groups:
        sent = [a for _, _, a in group]
        sent = jnp.concatenate(sent, axis=0) if len(sent) > 1 else sent[0]
        arrays.append(xor_send(sent, "shard", 1))
        names += [(p[0] ^ 1, p[1], len(arrays) - 1, i * rows) for i, p in enumerate(group)]
    return names, arrays


def add_low(left, right):
    return (left.astype(F32) + right.astype(F32)).astype(BF)


def halve(keep, other):
    middle = keep.shape[0] // 2
    return add_low(keep[middle:], other[middle:]), add_low(keep[:middle], other[:middle])


def scatter_sums(sums, chip_bits, before_add=None, before_last=None):
    send, keep = sums
    orders = list(zip(chip_bits, chip_bits[::-1]))
    for bits in orders[:-1]:
        other = core_send(send, bits)
        if before_add is not None:
            other, _ = lax.optimization_barrier((other, before_add))
        send, keep = halve(keep, other)
    if before_last is not None:
        send, _ = lax.optimization_barrier((send, before_last))
    return keep, core_send(send, orders[-1]), send


def last_sums(keep, other, _):
    middle = keep.shape[1] // 2
    return [
        add_low(keep[0, :middle], other[0, :middle]),
        add_low(keep[0, middle:], other[0, middle:]),
    ]


def side_sum(total, after=None):
    for bit in bits_of(lax.axis_size("replica"))[1:]:
        other = xor_send(total, "replica", bit)
        if after is not None:
            other, _ = lax.optimization_barrier((other, after))
        total = add_low(total, other)
    return total


def dot(left, right):
    return jnp.dot(left, right, preferred_element_type=F32)


def dot_cols(left, right):
    return lax.dot_general(left, right, (((1,), (1,)), ((), ())), preferred_element_type=F32)


def dot_rows(left, right):
    return lax.dot_general(left, right, (((0,), (0,)), ((), ())), preferred_element_type=F32)


def standardize(vector):
    average = jnp.mean(vector, axis=-1, keepdims=True)
    centred = vector - average
    spread = jnp.mean(centred * centred, axis=-1, keepdims=True)
    inverse = lax.rsqrt(spread + EPSILON)
    return centred * inverse, inverse


def norm_back(grad, gain, hat, inverse):
    dhat = grad * gain
    mean = jnp.mean(dhat, axis=-1, keepdims=True)
    along = jnp.mean(dhat * hat, axis=-1, keepdims=True)
    return (dhat - mean - hat * along) * inverse


def turned(vector):
    width = vector.shape[-1]
    lane = lax.broadcasted_iota(jnp.int32, vector.shape, 1)
    return jnp.where(
        (lane & 63) < 32, pltpu.roll(vector, width - 32, 1), pltpu.roll(vector, 32, 1)
    )


def place(me, pieces, refs, layout, sems):
    copies = []
    for j, stream, which, base in pieces:
        owner = me ^ j
        ref = refs[which]
        for row, rows, col, cols, dst, dst_col in layout[stream]:
            start = owner * rows
            if rows % 16 == 0:
                start = pl.multiple_of(start, 16)
            copy = pltpu.make_async_copy(
                ref.at[pl.ds(base + row, rows), pl.ds(col, cols)],
                dst.at[pl.ds(start, rows), pl.ds(dst_col, cols)],
                sems.at[len(copies)],
            )
            copy.start()
            copies.append(copy)
    return copies


def call(kernel, out_shape, inputs, in_any, scratch, flops, traffic, vmem_bytes=VMEM_BYTES):
    any_spec = pl.BlockSpec(memory_space=pl.ANY)
    vmem = pl.BlockSpec(memory_space=pltpu.VMEM)
    specs = [vmem] * len(inputs) + [any_spec] * len(in_any)
    return pl.pallas_call(
        kernel,
        out_shape=out_shape,
        in_specs=specs,
        out_specs=jax.tree.map(lambda _: vmem, out_shape),
        scratch_shapes=scratch,
        compiler_params=pltpu.CompilerParams(vmem_limit_bytes=vmem_bytes),
        cost_estimate=pl.CostEstimate(flops=flops, bytes_accessed=traffic, transcendentals=0),
    )(*inputs, *in_any)


def shard_at():
    return lax.axis_index("shard").astype(jnp.int32)


def side_at():
    return lax.axis_index("replica").astype(jnp.int32) & 1


def shaped(shape, dtype):
    return jax.ShapeDtypeStruct(shape, dtype)


def pack_qkv_kernel(half):
    def body(weight, attn_gain, ffn_gain, out, attn_held, ffn_held, sems):
        rows = weight.shape[0]
        first = side_at() * half
        copies = [
            pltpu.make_async_copy(attn_gain, attn_held, sems.at[0]),
            pltpu.make_async_copy(ffn_gain, ffn_held, sems.at[1]),
        ]
        for i in range(3):
            start = pl.multiple_of(i * 2 * half + first, 128)
            copies.append(
                pltpu.make_async_copy(
                    weight.at[:, pl.ds(start, half)],
                    out.at[:, pl.ds(i * half, half)],
                    sems.at[2 + i],
                )
            )
        for copy in copies:
            copy.start()
        copies[0].wait()
        copies[1].wait()
        gains = [ref[...].astype(F32) for ref in (attn_held, ffn_held)]
        gains = jnp.concatenate(gains + [jnp.zeros((6, rows), F32)], axis=0)
        gains = jnp.concatenate([gains, jnp.zeros((8, 128 - rows), F32)], axis=1)
        square = jnp.concatenate([gains, jnp.zeros((120, 128), F32)], axis=0)
        out[:, 3 * half :] = square.T[0:rows, :].astype(BF)
        for copy in copies[2:]:
            copy.wait()

    return body


def pack_mlp_kernel(count, down_rows, take):
    def body(attn, glu, down, out):
        rows, width = attn.shape
        units = count * take
        hidden = count * down_rows
        out[:, 0:width] = attn[...]
        last = width + 2 * units

        def pick(first):
            for part in range(2):
                for s in range(count):
                    at = part * hidden + s * down_rows + first
                    to = width + part * units + s * take
                    out[:, to : to + take] = glu[:, at : at + take]
            out[0:take, last:] = down[first : first + take, :]

        @pl.when(side_at() == 0)
        def _():
            pick(0)

        @pl.when(side_at() != 0)
        def _():
            pick(down_rows - take)

        if rows > take:
            out[take:, last:] = jnp.zeros((rows - take, width), BF)

    return body


def around_kernel(own, places, partner, near, far, out, cosine, sine, bias):
    def arrange(*blocks):
        for i, ref in enumerate(blocks):
            out[i * BLOCK : (i + 1) * BLOCK, :] = ref[0:BLOCK, :]

    @pl.when(side_at() == 0)
    def _():
        arrange(near, own, partner, far)

    @pl.when(side_at() != 0)
    def _():
        arrange(far, partner, own, near)

    def places_of(ref):
        first = ref.shape[0] - 16
        return ref[first : first + 1, 0:BLOCK].astype(F32) * 256.0 + ref[
            first + 1 : first + 2, 0:BLOCK
        ].astype(F32)

    mine, theirs = places[...].astype(F32), places_of(partner)
    inner, outer = places_of(near), places_of(far)
    even = side_at() == 0
    lines = [
        jnp.where(even, inner, outer),
        jnp.where(even, mine, theirs),
        jnp.where(even, theirs, mine),
        jnp.where(even, outer, inner),
    ]
    stacked = jnp.concatenate([jnp.broadcast_to(line, (BLOCK, BLOCK)).T for line in lines], axis=0)
    lane = lax.broadcasted_iota(jnp.int32, (1, 128), 1)
    power = lax.rem(lane, HEAD // 2).astype(F32) * (2.0 / HEAD)
    phases = stacked * jnp.exp(power * -math.log(THETA_BASE))
    cosine[...] = jnp.cos(phases)
    sine[...] = jnp.where((lane & 63) < 32, -1.0, 1.0) * jnp.sin(phases)
    offset = (
        lax.broadcasted_iota(jnp.int32, (BLOCK, 2 * BLOCK), 1)
        - RADIUS
        - lax.broadcasted_iota(jnp.int32, (BLOCK, 2 * BLOCK), 0)
    )
    distance = offset.astype(F32)
    for b in range(3):
        start = RADIUS + b * BLOCK
        key = jnp.concatenate([lines[b], lines[b + 1]], axis=1)
        query = jnp.concatenate([stacked[start : start + BLOCK, :]] * 2, axis=1)
        later = jnp.where(offset >= 0, key - distance, query + distance)
        allowed = (jnp.abs(offset) <= RADIUS) & (later >= 0.0)
        bias[b * BLOCK : (b + 1) * BLOCK, :] = jnp.where(allowed, 0.0, NEGATIVE)


def around_back_kernel(own, partner, near, far, out):
    def arrange(before, first, second, after):
        out[0:RADIUS, :] = before[...]
        out[RADIUS : RADIUS + BLOCK, :] = first
        out[RADIUS + BLOCK : RADIUS + 2 * BLOCK, :] = second
        out[RADIUS + 2 * BLOCK :, :] = after[...]

    theirs = partner[...]

    @pl.when(side_at() == 0)
    def _():
        arrange(near, own[...], theirs, far)

    @pl.when(side_at() != 0)
    def _():
        arrange(far, theirs, own[...], near)


def qkv_layout(rows, half, weight, gains=None):
    wide = 3 * half
    split = (wide + 128) // 2
    streams = [[(0, rows, 0, split, weight, 0)], [(0, rows, 0, wide - split, weight, split)]]
    streams.append([(0, rows, 0, wide, weight, 0)])
    if gains is not None:
        streams[1].append((0, rows, wide - split, 128, gains, 0))
        streams[2].append((0, rows, wide, 128, gains, 0))
    return streams


def project_kernel(pieces, n_refs, rows, width, skip):
    half = width // 2
    span = 4 * BLOCK

    def body(tok, cosine, sine, bias, *rest):
        refs, rest = rest[skip : n_refs + skip], rest[n_refs + skip :]
        q_out, k_out, v_out, p_out, ctx_out, normed_out, gains_out = rest[:7]
        weight, gain_cols, normed, sems = rest[7:]
        layout = qkv_layout(rows, half, weight, gain_cols)
        copies = place(shard_at(), pieces, refs, layout, sems)
        hats = [
            standardize(tok[i * BLOCK : (i + 1) * BLOCK, :].astype(F32))[0] for i in range(4)
        ]
        for copy in copies:
            copy.wait()
        pick = jnp.where(
            lax.broadcasted_iota(jnp.int32, (8, 128), 0)
            == lax.broadcasted_iota(jnp.int32, (8, 128), 1),
            1.0,
            0.0,
        ).astype(BF)
        gains = dot_cols(pick, gain_cols[...])
        gains_out[...] = gains
        for i, hat in enumerate(hats):
            normed[i * BLOCK : (i + 1) * BLOCK, :] = (hat * gains[0:1]).astype(BF)
        normed_out[...] = normed[BLOCK : 3 * BLOCK, :]
        cos3 = jnp.concatenate([cosine[...]] * 3, axis=1)
        sin3 = jnp.concatenate([sine[...]] * 3, axis=1)
        mid = slice(RADIUS, span - RADIUS)
        joined = dot(normed[mid, :], weight[:, 0:half])
        q_out[...] = (joined * cos3[mid] + turned(joined) * sin3[mid]).astype(BF)
        joined = dot(normed[...], weight[:, half : 2 * half])
        k_out[...] = (joined * cos3 + turned(joined) * sin3).astype(BF)
        v_out[...] = dot(normed[...], weight[:, 2 * half : 3 * half]).astype(BF)
        lane = lax.broadcasted_iota(jnp.int32, (BLOCK, 128), 1)
        scale = 1.0 / math.sqrt(HEAD)
        for pair in range(half // 128):
            cols = slice(pair * 128, pair * 128 + 128)
            for b in range(3):
                rows_q = slice(b * BLOCK, (b + 1) * BLOCK)
                rows_k = slice(b * BLOCK, (b + 2) * BLOCK)
                queries, keys, values = q_out[rows_q, cols], k_out[rows_k, cols], v_out[rows_k, cols]
                parts = []
                for h in range(2):
                    mine = (lane < HEAD) if h == 0 else (lane >= HEAD)
                    masked = jnp.where(mine, queries.astype(F32) * scale, 0.0).astype(BF)
                    scores = dot_cols(masked, keys) + bias[rows_q, :]
                    exponent = jnp.exp(scores - jnp.max(scores, axis=1, keepdims=True))
                    total = jnp.sum(exponent, axis=1, keepdims=True)
                    shares = (exponent * (1.0 / total)).astype(BF)
                    p_out[(pair * 2 + h) * 3 + b] = shares
                    parts.append(dot(shares, values))
                ctx_out[rows_q, cols] = jnp.where(lane < HEAD, parts[0], parts[1]).astype(BF)

    return body


def attn_layout(rows, width, attn):
    parts = [(0, rows, 0, width, attn, 0)]
    return (parts, (), parts)


def mlp_layout(rows, take, width, units, glu, down):
    gate = (0, rows, width, units, glu, 0)
    up = (0, rows, 0, units, glu, units)
    low = (0, take, units, width, down, 0)
    whole = ((0, rows, width, 2 * units, glu, 0), (0, take, width + 2 * units, width, down, 0))
    return ((gate,), (up, low), whole)


def mlp_kernel(pieces, n_refs, rows, down_rows, take, width, units):
    half = width // 2
    pair = slice(RADIUS, RADIUS + 2 * BLOCK)

    def body(tok, ctx_own, ctx_other, dy, gains, *rest):
        refs, rest = rest[1 : n_refs + 1], rest[n_refs + 1 :]
        mix_keep, mix_send, shared, ctx_pair, hidden, gn_out = rest[:6]
        attn, glu, down, ggu, mix, attn_sems, sems = rest[6:]
        first = place(shard_at(), pieces, refs, attn_layout(rows, width, attn), attn_sems)
        layout = mlp_layout(rows, take, width, units, glu, down)
        copies = place(shard_at(), pieces, refs, layout, sems)
        at = side_at()
        inputs = tok[RADIUS : RADIUS + 3 * BLOCK, :].astype(F32)
        own_rows = pl.ds(pl.multiple_of(at * half, 128), half)
        other_rows = pl.ds(pl.multiple_of((1 - at) * half, 128), half)

        @pl.when(at == 0)
        def _():
            ctx_pair[:, 0:half] = ctx_own[pair, :]
            ctx_pair[:, half:] = ctx_other[pair, :]

        @pl.when(at != 0)
        def _():
            ctx_pair[:, 0:half] = ctx_other[pair, :]
            ctx_pair[:, half:] = ctx_own[pair, :]

        for copy in first:
            copy.wait()
        lifted = dot(ctx_own[...], attn[own_rows, :]) + dot(ctx_other[...], attn[other_rows, :])
        hidden[...] = inputs + lifted
        hat, _ = standardize(hidden[...])
        normed = (hat * gains[1:2, :]).astype(BF)
        shared[:, 0:width] = normed[pair]
        for copy in copies:
            copy.wait()
        partial = jnp.zeros((2 * BLOCK, width), F32)
        unit = lax.rem(lax.broadcasted_iota(jnp.int32, (1, units), 1), take)
        mask = jnp.where(unit >= at * (2 * take - down_rows), 1.0, 0.0)
        for c in range(0, units, 640):
            wide = min(640, units - c)
            cols = slice(c, c + wide)
            gate = dot(normed, glu[:, cols])
            up = dot(normed, glu[:, units + c : units + c + wide])
            grad_act = dot_cols(dy[...], down[cols, :]) * mask[:, cols]
            share = 0.5 * (1.0 + lax.erf(gate * (1.0 / math.sqrt(2.0))))
            density = jnp.exp(-0.5 * gate * gate) * (1.0 / math.sqrt(2.0 * math.pi))
            gelu = gate * share
            act = (gelu[pair] * up[pair] * mask[:, cols]).astype(BF)
            shared[:, width + c : width + c + wide] = act
            partial = partial + dot(act, down[cols, :])
            ggu[:, cols] = (grad_act * up * (share + gate * density)).astype(BF)
            ggu[:, units + c : units + c + wide] = (grad_act * gelu).astype(BF)
        mix[...] = partial
        mine = pl.ds(pl.multiple_of(at * BLOCK, BLOCK), BLOCK)
        theirs = pl.ds(pl.multiple_of((1 - at) * BLOCK, BLOCK), BLOCK)
        mix_keep[...] = mix[mine, :] + hidden[pl.ds(pl.multiple_of(RADIUS + at * BLOCK, 8), BLOCK), :]
        mix_send[...] = mix[theirs, :].astype(BF)
        shared[:, width + units :] = ggu[pair, :]
        grad = dot_cols(ggu[...], glu[...])
        gn_out[...] = grad.astype(BF)

    return body


def pair_back(pair, gctx, q, k, v, p, cos, sin):
    lane = lax.broadcasted_iota(jnp.int32, (BLOCK, 128), 1)
    lane2 = lax.broadcasted_iota(jnp.int32, (2 * BLOCK, 128), 1)
    scale = 1.0 / math.sqrt(HEAD)
    cols = slice(pair * 128, pair * 128 + 128)
    first, second = slice(0, BLOCK), slice(BLOCK, 2 * BLOCK)
    low, high = slice(0, RADIUS), slice(RADIUS, BLOCK)
    grad_q = jnp.zeros((2 * BLOCK, 128), F32)
    grad_k, grad_v = [0.0, 0.0], [0.0, 0.0]
    for h in range(2):
        mine = (lane < HEAD) if h == 0 else (lane >= HEAD)
        mine2 = (lane2 < HEAD) if h == 0 else (lane2 >= HEAD)
        scores, shares, queries, grads, parts = [], [], [], [], []
        for b in range(3):
            rows_q = slice(b * BLOCK, (b + 1) * BLOCK)
            rows_k = slice(b * BLOCK, (b + 2) * BLOCK)
            keys, values = k[rows_k, cols], v[rows_k, cols]
            lowered = jnp.where(mine, gctx[rows_q, cols].astype(F32), 0.0).astype(BF)
            query = jnp.where(mine, q[rows_q, cols].astype(F32) * scale, 0.0).astype(BF)
            share = p[(pair * 2 + h) * 3 + b]
            wide = share.astype(F32)
            grad_share = dot_cols(lowered, values)
            row = jnp.sum(wide * grad_share, axis=1, keepdims=True)
            grad_score = (wide * (grad_share - row)).astype(BF)
            scores.append(grad_score)
            shares.append(share)
            queries.append(query)
            grads.append(lowered)
            part = (high, first, low)[b]
            parts.append(dot(grad_score[part], keys))
        grad_q = grad_q + jnp.where(mine2, jnp.concatenate(parts, axis=0) * scale, 0.0)
        for i in range(2):
            two = slice(i, i + 2)
            for total, left, right in ((grad_k, scores, queries), (grad_v, shares, grads)):
                upper, lower = left[i][:, second], left[i + 1][:, first]
                total[i] = total[i] + dot_rows(
                    jnp.concatenate([upper, lower], axis=0), jnp.concatenate(right[two], axis=0)
                )
    grad_k, grad_v = jnp.concatenate(grad_k, axis=0), jnp.concatenate(grad_v, axis=0)
    return (
        (grad_q * cos - turned(grad_q) * sin).astype(BF),
        (grad_k * cos - turned(grad_k) * sin).astype(BF),
        grad_v.astype(BF),
    )


def hidden_back_kernel(mlp_pieces, n_mlp, rows, width):
    half = width // 2
    pair = slice(RADIUS, RADIUS + 2 * BLOCK)

    def body(gn_own, gn_other, hidden, dy, gains, q, k, v, p, cosine, sine, *rest):
        mlp_refs, rest = rest[1 : n_mlp + 1], rest[n_mlp + 1 :]
        ghid_out, gj_out, attn, gctx, held, attn_sems = rest
        copies = place(shard_at(), mlp_pieces, mlp_refs, attn_layout(rows, width, attn), attn_sems)
        at = side_at()
        hat, inverse = standardize(hidden[...])
        grad = gn_own[...].astype(F32) + gn_other[...].astype(F32)
        grad_hidden = dy[...].astype(F32) + norm_back(grad, gains[1:2, :], hat, inverse)
        held[...] = grad_hidden[pair]
        ghid_out[...] = held[pl.ds(pl.multiple_of(at * BLOCK, BLOCK), BLOCK), :]
        halves = jnp.where(at == 0, grad_hidden[pair, 0:half], grad_hidden[pair, half:])
        gj_out[:, 3 * half :] = halves.astype(BF)
        grad_low = grad_hidden.astype(BF)
        for copy in copies:
            copy.wait()
        own_rows = pl.ds(pl.multiple_of(at * half, 128), half)
        gctx[...] = dot_cols(grad_low, attn[own_rows, :]).astype(BF)
        cos, sin = cosine[BLOCK : 3 * BLOCK, :], sine[BLOCK : 3 * BLOCK, :]
        for i in range(half // 128):
            for part, grad in enumerate(pair_back(i, gctx, q, k, v, p, cos, sin)):
                col = part * half + i * 128
                gj_out[:, col : col + 128] = grad

    return body


def norm_back_kernel(pieces, n_refs, rows, width):
    half = width // 2

    def body(gj, *rest):
        refs, rest = rest[:n_refs], rest[n_refs:]
        keep_out, send_out, weight, held, sems = rest
        copies = place(shard_at(), pieces, refs, qkv_layout(rows, half, weight), sems)
        at = side_at()
        for copy in copies:
            copy.wait()
        held[...] = dot_cols(gj[:, 0 : 3 * half], weight[...])
        keep_out[...] = held[pl.ds(pl.multiple_of(at * BLOCK, BLOCK), BLOCK), :]
        theirs = pl.ds(pl.multiple_of((1 - at) * BLOCK, BLOCK), BLOCK)
        send_out[...] = held[theirs, :].astype(BF)

    return body


def final_kernel(tok, keep, other, ghid, gains, out):
    hat, inverse = standardize(tok[...].astype(F32))
    grad = keep[...] + other[...].astype(F32)
    out[...] = (ghid[...] + norm_back(grad, gains[0:1, :], hat, inverse)).astype(BF)


def slots_of(chip_bits):
    tables = []
    for order in (chip_bits, chip_bits[::-1]):
        kept = [0]
        for bit in order[1:][::-1]:
            kept = kept + [j | bit for j in kept]
        tables.append([(1, i, j) for i, j in enumerate(kept)])
        tables[-1] += [(0, i, j | order[0]) for i, j in enumerate(kept)]
    return [(kept, i, j, k) for (kept, i, j), (_, _, k) in zip(*tables)]


def owner_rows(me, slots, lhs_t, rows):
    parts = []
    for _, _, even, odd in slots:
        owner = me ^ jnp.where((me & 1) == 0, even, odd)
        parts.append(lhs_t[pl.ds(pl.multiple_of(owner * rows, 16), rows), :])
    return jnp.concatenate(parts, axis=0)


def emit(outs, slots, rows, grad, start):
    grad = grad.astype(BF)
    for i, (kept, at, _, _) in enumerate(slots):
        for c in range(grad.shape[1] // 128):
            row = start + c * rows
            outs[kept][at, row : row + rows, :] = grad[
                i * rows : (i + 1) * rows, c * 128 : (c + 1) * 128
            ]


def mlp_grad_kernel(slots, rows, take, width, units):
    half = width // 2

    def body(own, other, dy_own, dy_other, *rest):
        outs, (normed_t, act_t, ggu, dy) = rest[1:3], rest[3:]
        me = shard_at()
        pair = slice(RADIUS, RADIUS + 2 * BLOCK)
        for i, (ref, dref) in enumerate(((own, dy_own), (other, dy_other))):
            tok = slice(i * 2 * BLOCK, (i + 1) * 2 * BLOCK)
            normed_t[:, tok] = ref[:, 0:width].T
            act_t[:, tok] = ref[:, width : width + units].T
            ggu[tok, :] = ref[:, width + units :]
            dy[tok, :] = dref[pair, :]
        left = owner_rows(me, slots, normed_t, rows)
        act = owner_rows(me, slots, act_t, take)
        height = outs[0].shape[1] // 2
        for s in range(2):
            grad = dot(left, ggu[:, s * units : (s + 1) * units])
            emit(outs, slots, rows, grad, s * height)
            grad = dot(act, dy[:, s * half : (s + 1) * half])
            emit(outs, slots, take, grad, s * height + rows * (units // 128))

    return body


def qkv_grad_kernel(slots, rows, width):
    half = width // 2

    def body(normed_own, normed_other, ctx_own, ctx_other, own, other, *rest):
        outs, (normed_t, ctx_t, gj) = rest[1:3], rest[3:]
        me = shard_at()
        count = 2 * BLOCK
        each = ((normed_own, ctx_own, own), (normed_other, ctx_other, other))
        for i, (nref, cref, ref) in enumerate(each):
            tok = slice(i * count, (i + 1) * count)
            normed_t[:, tok] = nref[...].T
            ctx_t[:, tok] = cref[...].T
            gj[tok, :] = ref[...]
        left = owner_rows(me, slots, normed_t, rows)
        ctx = owner_rows(me, slots, ctx_t, rows)
        emit(outs, slots, rows, dot(left, gj[:, 0 : 3 * half]), 0)
        emit(outs, slots, rows, dot(ctx, gj[:, 3 * half :]), 9 * rows)

    return body


def gain_grad(weight, grad, gain):
    total = jnp.sum(weight[...].astype(F32) * grad[...], axis=1, keepdims=True)
    rows = total.shape[0]
    total = jnp.concatenate([total, jnp.zeros((128 - rows, 1), F32)], axis=0)
    return jnp.broadcast_to(total, (128, 128)).T[0:1, 0:rows] / gain[...].astype(F32)


def mlp_unpack_kernel(rows, down_rows, take, width, units, count):
    hidden = count * down_rows
    spare = 2 * take - down_rows

    def body(mine_0, mine_1, other_0, other_1, weight, gain, sent, glu, down, gain_out, held, wide):
        at = side_at()
        tiles = units // 128
        for s, (mine, other) in enumerate(((mine_0, other_0), (mine_1, other_1))):
            held[at, s] = mine[...].astype(F32)
            held[1 - at, s] = other[...].astype(F32)
        for s in range(2):
            for t in range(2):
                for c in range(tiles):
                    row = c * rows
                    wide[:, c * 128 : (c + 1) * 128] = held[t, s, row : row + rows, :]
                skip = 0 if t == 0 else spare
                for i in range(count):
                    col = s * hidden + i * down_rows + t * take
                    glu[:, col : col + take - skip] = wide[:, i * take + skip : (i + 1) * take]
                for c in range(width // 256):
                    row = tiles * rows + c * take
                    col = s * (width // 2) + c * 128
                    down[t * take : (t + 1) * take - skip, col : col + 128] = held[
                        t, s, row + skip : row + take, :
                    ]
        gain_out[...] = gain_grad(weight, glu, gain)

    return body


def qkv_unpack_kernel(rows, width):
    half = width // 2
    tiles = half // 128

    def body(mine_0, mine_1, other_0, other_1, weight, gain, qkv, attn, gain_out, held):
        at = side_at()
        for s, (mine, other) in enumerate(((mine_0, other_0), (mine_1, other_1))):
            held[at, s] = mine[...].astype(F32)
            held[1 - at, s] = other[...].astype(F32)
        for t in range(2):
            for i in range(3):
                for c in range(tiles):
                    row = (i % 2 * tiles + c) * rows
                    col = i * width + t * half + c * 128
                    qkv[:, col : col + 128] = held[t, i // 2, row : row + rows, :]
            for c in range(tiles):
                row = (tiles + c) * rows
                attn[:, t * half + c * 128 : t * half + (c + 1) * 128] = held[t, 1, row : row + rows, :]
        gain_out[...] = gain_grad(weight, qkv, gain)

    return body


def on_device(
    tokens,
    positions,
    qkv_weight,
    attn_weight,
    glu_weight,
    down_weight,
    attn_gain,
    ffn_gain,
    cotangent,
):
    block, width = tokens.shape
    half = width // 2
    rows, down_rows = qkv_weight.shape[0], down_weight.shape[0]
    count, replicas = lax.axis_size("shard"), lax.axis_size("replica")
    everyone = count * replicas
    take = -(-down_rows // 32) * 16
    units = count * take
    me = lax.axis_index("shard").astype(jnp.int32)
    side = lax.axis_index("replica").astype(jnp.int32) & 1
    chip_bits = bits_of(count)[1:]

    own = call(
        pack_qkv_kernel(half),
        shaped((rows, 3 * half + 128), BF),
        (),
        [qkv_weight, attn_gain[None], ffn_gain[None]],
        [
            pltpu.VMEM((1, rows), BF),
            pltpu.VMEM((1, rows), BF),
            pltpu.SemaphoreType.DMA((5,)),
        ],
        1_000_000,
        1_000_000,
        VMEM_ALL,
    )

    places = jnp.stack([positions >> 8, positions & 255]).astype(BF)
    places = jnp.pad(places, ((0, 14), (0, width - block)))
    rim = jnp.concatenate([tokens, places], axis=0)
    rim, _ = lax.optimization_barrier((rim, own))
    step = [1 if i & 1 else -1 for i in range(everyone)]
    both = ("shard", "replica")

    def outward(array):
        moves = [(i, i + step[i]) for i in range(everyone)]
        return lax.ppermute(array, both, [(a, b) for a, b in moves if 0 <= b < everyone])

    own_mlp = call(
        pack_mlp_kernel(count, down_rows, take),
        shaped((rows, 2 * width + 2 * units), BF),
        (attn_weight, glu_weight, down_weight),
        [],
        [],
        1_000_000,
        2_000_000,
    )
    qkv_parts, _ = gather_pieces(
        own, (3 * half + 128) // 2, chip_bits, rim
    )
    near, partner = outward(rim), xor_send(rim, "replica", 1)
    arrived = [a for _, _, a in qkv_parts]
    own, near, partner, arrived = lax.optimization_barrier((own_mlp, near, partner, arrived))
    qkv_parts = [(j, s, a) for (j, s, _), a in zip(qkv_parts, arrived)]
    far = xor_send(near, "replica", 1)
    mlp_parts, forward = gather_pieces(own, width + units, chip_bits)

    tok, cosine, sine, bias = call(
        around_kernel,
        (
            shaped((4 * BLOCK, width), BF),
            shaped((4 * BLOCK, 128), F32),
            shaped((4 * BLOCK, 128), F32),
            shaped((3 * BLOCK, 2 * BLOCK), F32),
        ),
        (tokens, positions[None], partner, near, far),
        [],
        [],
        1_000_000,
        2_000_000,
    )
    rim = jnp.where(side == 0, cotangent[:RADIUS], cotangent[block - RADIUS :])
    rim, _ = lax.optimization_barrier((rim, near))
    near_dy = outward(rim)
    sent, near_dy = lax.optimization_barrier((cotangent, near_dy))
    partner_dy = xor_send(sent, "replica", 1)
    far_dy = xor_send(near_dy, "replica", 1)
    qkv_names, qkv_arrays = with_core(qkv_parts, True)
    weight_bytes = width * 3 * width * 2

    q, k, v, p, ctx, normed, gains = call(
        project_kernel(qkv_names, len(qkv_arrays), rows, width, 2 + len(forward)),
        (
            shaped((3 * BLOCK, half), BF),
            shaped((4 * BLOCK, half), BF),
            shaped((4 * BLOCK, half), BF),
            shaped((3 * half // HEAD, BLOCK, 2 * BLOCK), BF),
            shaped((3 * BLOCK, half), BF),
            shaped((2 * BLOCK, width), BF),
            shaped((8, width), F32),
        ),
        (tok, cosine, sine, bias),
        [far_dy, partner_dy] + forward + qkv_arrays,
        [
            pltpu.VMEM((width, 3 * half), BF),
            pltpu.VMEM((width, 128), BF),
            pltpu.VMEM((4 * BLOCK, width), BF),
            pltpu.SemaphoreType.DMA((2 * len(qkv_names),)),
        ],
        7_000_000_000,
        weight_bytes,
    )
    ctx_other = xor_send(ctx, "replica", 1)
    normed_other = xor_send(normed, "shard", 1)
    near_dy, far_dy, partner_dy, _ = lax.optimization_barrier(
        (near_dy, far_dy, partner_dy, ctx)
    )
    dy = call(
        around_back_kernel,
        shaped((3 * BLOCK, width), BF),
        (cotangent, partner_dy, near_dy, far_dy),
        [],
        [],
        1_000_000,
        2_000_000,
    )
    dy_other = xor_send(dy, "shard", 1)
    held, _ = lax.optimization_barrier(([a for _, _, a in mlp_parts], ctx))
    mlp_parts = [(j, s, a) for (j, s, _), a in zip(mlp_parts, held)]
    names, arrays = with_core(mlp_parts, False)

    mix_keep, mix_send, shared, ctx_pair, hidden, gn = call(
        mlp_kernel(names, len(arrays), rows, down_rows, take, width, units),
        (
            shaped((BLOCK, width), F32),
            shaped((BLOCK, width), BF),
            shaped((2 * BLOCK, width + 3 * units), BF),
            shaped((2 * BLOCK, width), BF),
            shaped((3 * BLOCK, width), F32),
            shaped((3 * BLOCK, width), BF),
        ),
        (tok, ctx, ctx_other, dy, gains),
        [normed_other] + arrays,
        [
            pltpu.VMEM((width, width), BF),
            pltpu.VMEM((width, 2 * units), BF),
            pltpu.VMEM((units, width), BF),
            pltpu.VMEM((3 * BLOCK, 2 * units), BF),
            pltpu.VMEM((2 * BLOCK, width), F32),
            pltpu.SemaphoreType.DMA((len(names),)),
            pltpu.SemaphoreType.DMA((2 * len(names),)),
        ],
        8_000_000_000,
        2 * weight_bytes,
    )
    gn_other = xor_send(gn, "replica", 1)
    shared_other = xor_send(shared, "shard", 1)
    ctx_pair_other = xor_send(ctx_pair, "shard", 1)

    slots = slots_of(chip_bits)
    portion = count // 4

    def stack(height):
        return (shaped((portion, 2 * height, 128), BF),) * 2

    height = rows * (units // 128) + take * (half // 128)
    sums = call(
        mlp_grad_kernel(slots, rows, take, width, units),
        stack(height),
        (shared, shared_other, dy, dy_other),
        [ctx_pair_other],
        [
            pltpu.VMEM((width, 4 * BLOCK), BF),
            pltpu.VMEM((units, 4 * BLOCK), BF),
            pltpu.VMEM((4 * BLOCK, 2 * units), BF),
            pltpu.VMEM((4 * BLOCK, width), BF),
        ],
        4_000_000_000,
        weight_bytes,
    )

    ghid, gj = call(
        hidden_back_kernel(names, len(arrays), rows, width),
        (
            shaped((BLOCK, width), F32),
            shaped((2 * BLOCK, 4 * half), BF),
        ),
        (gn, gn_other, hidden, dy, gains, q, k, v, p, cosine, sine),
        [sums[1]] + arrays,
        [
            pltpu.VMEM((width, width), BF),
            pltpu.VMEM((3 * BLOCK, half), BF),
            pltpu.VMEM((2 * BLOCK, width), F32),
            pltpu.SemaphoreType.DMA((len(names),)),
        ],
        5_000_000_000,
        weight_bytes,
    )
    mlp_sums = scatter_sums(sums, chip_bits, gj)
    mix_other = xor_send(mix_send, "replica", 1)
    gj_other = xor_send(gj, "shard", 1)
    norm_keep, norm_send = call(
        norm_back_kernel(qkv_names, len(qkv_arrays), rows, width),
        (shaped((BLOCK, width), F32), shaped((BLOCK, width), BF)),
        (gj,),
        qkv_arrays,
        [
            pltpu.VMEM((width, 3 * half), BF),
            pltpu.VMEM((2 * BLOCK, width), F32),
            pltpu.SemaphoreType.DMA((len(qkv_names),)),
        ],
        3_000_000_000,
        weight_bytes,
    )
    sums = call(
        qkv_grad_kernel(slots, rows, width),
        stack(6 * rows),
        (normed, normed_other, ctx_pair, ctx_pair_other, gj, gj_other),
        [norm_keep],
        [
            pltpu.VMEM((width, 4 * BLOCK), BF),
            pltpu.VMEM((width, 4 * BLOCK), BF),
            pltpu.VMEM((4 * BLOCK, 4 * half), BF),
        ],
        3_000_000_000,
        weight_bytes,
    )
    mlp_sums, mix_other, _ = lax.optimization_barrier((mlp_sums, mix_other, sums[1]))
    mlp_sums = last_sums(*mlp_sums)
    norm_send, _ = lax.optimization_barrier((norm_send, sums[1]))
    norm_other = xor_send(norm_send, "replica", 1)
    mixed = (mix_keep + mix_other.astype(F32)).astype(BF)
    grad_tokens = call(
        final_kernel,
        shaped((block, width), BF),
        (tokens, norm_keep, norm_other, ghid, gains),
        [],
        [],
        1_000_000,
        1_000_000,
    )
    qkv_sums = scatter_sums(sums, chip_bits, (mixed, grad_tokens))
    mlp_mine = [side_sum(part, qkv_sums[2]) for part in mlp_sums]
    mlp_other = [xor_send(part, "replica", 1) for part in mlp_mine]
    sent = qkv_sums[1]
    grad_glu, grad_down, grad_ffn_gain = call(
        mlp_unpack_kernel(rows, down_rows, take, width, units, count),
        (
            shaped((rows, 2 * count * down_rows), F32),
            shaped((down_rows, width), F32),
            shaped((1, rows), F32),
        ),
        (*mlp_mine, *mlp_other, glu_weight, ffn_gain[None]),
        [sent],
        [pltpu.VMEM((2, 2, height, 128), F32), pltpu.VMEM((rows, units), F32)],
        1_000_000,
        4_000_000,
    )
    done = grad_glu
    qkv_mine = [side_sum(part, done) for part in last_sums(*qkv_sums)]
    qkv_other = [xor_send(part, "replica", 1) for part in qkv_mine]
    grad_qkv, grad_attn, grad_attn_gain = call(
        qkv_unpack_kernel(rows, width),
        (
            shaped((rows, 3 * width), F32),
            shaped((rows, width), F32),
            shaped((1, rows), F32),
        ),
        (*qkv_mine, *qkv_other, qkv_weight, attn_gain[None]),
        [],
        [pltpu.VMEM((2, 2, 6 * rows, 128), F32)],
        1_000_000,
        4_000_000,
    )
    return (
        mixed,
        grad_tokens,
        grad_qkv,
        grad_attn,
        grad_glu,
        grad_down,
        grad_attn_gain.reshape(rows),
        grad_ffn_gain.reshape(rows),
    )


def solution(mesh):
    in_specs = (
        P(("shard", "replica"), None),
        P(("shard", "replica")),
        P("shard", None),
        P("shard", None),
        P("shard", None),
        P("shard", None),
        P("shard"),
        P("shard"),
        P(("shard", "replica"), None),
    )
    out_specs = (
        P(("shard", "replica"), None),
        P(("shard", "replica"), None),
        P("shard", None),
        P("shard", None),
        P("shard", None),
        P("shard", None),
        P("shard"),
        P("shard"),
    )
    return jax.shard_map(
        on_device, mesh=mesh, in_specs=in_specs, out_specs=out_specs, check_vma=False
    )
```
